32 devices in a mesh: dp: 16 (over z, y, x), tensor: 2 (over core).
Axes of the slice: x: 2, y: 2, z: 4, core: 2. Of those that a mesh axis runs over, the one named last changes fastest.
Arguments:
- decoder_input: bfloat16 [16, 1024, 512], P('dp'), may hold values from -6 to 6
- encoder_states: bfloat16 [16, 1024, 512], P('dp'), may hold values from -6 to 6
- decoder_segments: int32 [16, 1024], P('dp'), may hold values from 0 to 3, never falling along the last dimension, each value on 1 to 512 neighbouring positions
- encoder_segments: int32 [16, 1024], P('dp'), may hold values from 0 to 3, never falling along the last dimension, each value on 1 to 512 neighbouring positions
- output_cotangent: bfloat16 [16, 1024, 512], P('dp'), may hold values from -6 to 6
- block_slots: int32 [256], replicated, may hold values from 0 to 255, as said below
- master: float32 [2, 256, 128, 64], P('tensor', 'dp')
- first_moment: float32 [2, 256, 128, 64], P('tensor', 'dp')
- second_moment: float32 [2, 256, 128, 64], P('tensor', 'dp'), as said below
- row_statistics: float32 [2, 256, 128, 128], P('tensor', 'dp')
- column_statistics: float32 [2, 256, 64, 64], P('tensor', 'dp')
- row_basis: float32 [2, 256, 128, 128], P('tensor', 'dp')
- column_basis: float32 [2, 256, 64, 64], P('tensor', 'dp')
- vectors: float32 [6, 512], P(None, 'dp')
- vector_first: float32 [6, 512], P(None, 'dp')
- vector_second: float32 [6, 512], P(None, 'dp'), as said below
Outputs:
- block_output: bfloat16 [16, 1024, 512], P('dp')
- input_gradient: float32 [16, 1024, 512], P('dp')
- encoder_gradient: float32 [16, 1024, 512], P('dp')
- new_master: float32 [2, 256, 128, 64], P('tensor', 'dp')
- new_first_moment: float32 [2, 256, 128, 64], P('tensor', 'dp')
- new_second_moment: float32 [2, 256, 128, 64], P('tensor', 'dp')
- new_row_statistics: float32 [2, 256, 128, 128], P('tensor', 'dp')
- new_column_statistics: float32 [2, 256, 64, 64], P('tensor', 'dp')
- new_row_basis: float32 [2, 256, 128, 128], P('tensor', 'dp')
- new_column_basis: float32 [2, 256, 64, 64], P('tensor', 'dp')
- new_vectors: float32 [6, 512], P(None, 'dp')
- new_vector_first: float32 [6, 512], P(None, 'dp')
- new_vector_second: float32 [6, 512], P(None, 'dp')
The draws below stay inside these ranges and needn't reach their ends.
Inputs may be any that keep to these rules, and one draw needn't show every extreme that they name: `block_slots`: each number appears exactly once. `decoder_segments`: within a sequence the numbers never fall; each of the 4 documents has 1 to 512 tokens, one exactly that many. `encoder_segments`: within a sequence the numbers never fall; each of the 4 documents has 1 to 512 positions, one exactly that many. `second_moment`: every entry is positive. `vector_second`: every entry is positive.
All inputs are finite; a program needn't handle non-finite values.
Results may differ from the reference program's by a relative error of at most 0.029.
Values may be sent and summed in bfloat16 or wider, within the bound.
No kernel may reach another device: no remote copies, remote signals or barrier semaphores. Data moves between devices by JAX's collectives and lax.ppermute only.
A program may use at most 128 MiB of HBM per device.

```python
import math
import jax
import jax.numpy as jnp
import numpy as np
from jax import lax

D = 512
H = 8
HD = 64
FF = 2048
LEN = 1024
ENC_LEN = 1024
DOCS = 4
BR = 128
STEP = 10
ROWS = 16
HEADS_DEV = 4
FF_DEV = 1024
COLS_DEV = 4096
BLK_T = 256
SLICES = 2


def slot_table(key):
    return jax.random.permutation(jax.random.fold_in(key, 11), BLK_T).astype(jnp.int32)


def slot_kinds(key):
    slot_list = slot_table(key)
    block_of_slot = jnp.zeros((BLK_T,), jnp.int32).at[slot_list].set(jnp.arange(BLK_T, dtype=jnp.int32))
    column = block_of_slot % (COLS_DEV // HD) * HD
    head_width = HEADS_DEV * HD
    return jnp.where(column < 8 * head_width, column // head_width, jnp.where(column < 8 * head_width + FF_DEV, 8, 9))


def kind_table(entries, key):
    lookup = jnp.array(entries, jnp.float32)
    return lookup[slot_kinds(key)].reshape(1, BLK_T, 1, 1)


def weight_spread(key):
    drawn = D ** (-0.5)
    output_scale = 4.0 * (H * HD) ** (-0.5)
    return kind_table([drawn, drawn, drawn, output_scale, drawn, drawn, drawn, output_scale, drawn, FF ** (-0.5)], key)


def grad_spread(key):
    return kind_table([0.05, 0.05, 0.1, 0.1, 0.05, 0.05, 0.1, 0.1, 0.25, 0.5], key) * (ROWS * LEN) ** 0.5


def draw_block_slots(key, part):
    return slot_table(key)


def draw_master(key, part):
    return jax.random.normal(jax.random.fold_in(key, 21), (SLICES, BLK_T, BR, HD), jnp.float32) * weight_spread(key)


def draw_first_moment(key, part):
    return jax.random.normal(jax.random.fold_in(key, 22), (SLICES, BLK_T, BR, HD), jnp.float32) * grad_spread(key)


def draw_second_moment(key, part):
    factor = jax.random.uniform(jax.random.fold_in(key, 23), (SLICES, BLK_T, BR, HD), jnp.float32, 1.0, 4.0)
    return factor * grad_spread(key) ** 2


def statistics(key, salt, size, other):
    spread = grad_spread(key) ** 2 * other
    diagonal = jax.random.uniform(jax.random.fold_in(key, salt), (SLICES, BLK_T, size), jnp.float32, 1.0, 4.0)
    random_part = jax.random.normal(jax.random.fold_in(key, salt + 1), (SLICES, BLK_T, size, size), jnp.float32)
    symmetric = 0.5 * (random_part + jnp.swapaxes(random_part, -1, -2)) * 0.04
    return (symmetric + jnp.eye(size, dtype=jnp.float32) * diagonal[..., None]) * spread


def draw_row_statistics(key, part):
    return statistics(key, 24, BR, HD)


def draw_column_statistics(key, part):
    return statistics(key, 26, HD, BR)


def draw_row_basis(key, part):
    random_part = jax.random.normal(jax.random.fold_in(key, 28), (SLICES, BLK_T, BR, BR), jnp.float32)
    return jnp.eye(BR, dtype=jnp.float32) + random_part * (0.5 * BR ** (-0.5))


def draw_column_basis(key, part):
    random_part = jax.random.normal(jax.random.fold_in(key, 29), (SLICES, BLK_T, HD, HD), jnp.float32)
    return jnp.eye(HD, dtype=jnp.float32) + random_part * (0.5 * HD ** (-0.5))


def draw_vectors(key, part):
    gain_rows = jax.random.uniform(jax.random.fold_in(key, 31), (6, D), jnp.float32, 0.5, 1.5)
    shift_rows = jax.random.normal(jax.random.fold_in(key, 32), (6, D), jnp.float32) * 0.3
    row_index = jnp.arange(6)[:, None]
    return jnp.where(row_index % 2 == 0, gain_rows, shift_rows)


def draw_vector_first(key, part):
    return jax.random.normal(jax.random.fold_in(key, 33), (6, D), jnp.float32) * (ROWS * LEN) ** 0.5


def draw_vector_second(key, part):
    factor = jax.random.uniform(jax.random.fold_in(key, 34), (6, D), jnp.float32, 1.0, 4.0)
    return factor * (ROWS * LEN)


def shard_levels(key, dims, split, smallest, top_value):
    factor_of = 1.0
    for dim, blocks in split:
        steps = jax.random.uniform(jax.random.fold_in(jax.random.fold_in(key, 6), dim), (blocks,), jnp.float32, smallest / len(split), top_value / len(split))
        factor_of = factor_of * jnp.repeat(jnp.exp(steps), dims[dim] // blocks).reshape((-1,) + (1,) * (len(dims) - 1 - dim))
    return factor_of


def split_up(number_of, total, bound, skew):
    portions = [(1 << 20) // math.isqrt(rank ** skew) + 1 for rank in range(2, number_of + 1)]
    surplus, given = total - bound - (number_of - 1), [1] * (number_of - 1)
    while surplus > 0:
        free = [i for i in range(number_of - 1) if given[i] < bound]
        mass, budget = sum([portions[i] for i in free]), surplus
        for i in free:
            more = min(bound - given[i], max(1, budget * portions[i] // mass), surplus)
            given[i] = given[i] + more
            surplus = surplus - more
    return np.array([bound] + given)


def ragged_sizes(key, count, total, reach, skew):
    if count == 2:
        one = jax.random.randint(key, (), max(1, total - reach), min(reach, total - 1) + 1)
        return jnp.stack([one, total - one])
    lengths = jnp.asarray(split_up(count, total, reach, skew), jnp.int32)
    twos = (count - 1) // 2
    source_of, receiver = lengths[1:1 + 2 * twos:2], lengths[2:2 + 2 * twos:2]
    slack = jnp.minimum(source_of - 1, reach - receiver)
    shifted = jax.random.randint(jax.random.fold_in(key, 1), (twos,), 0, 1 << 20) % (slack + 1)
    lengths = lengths.at[1:1 + 2 * twos:2].set(source_of - shifted).at[2:2 + 2 * twos:2].set(receiver + shifted)
    return lengths[jax.random.permutation(jax.random.fold_in(key, 2), count)]


def normal_values(own_key, dims, deviation, most, cuts=(), held_as=jnp.bfloat16):
    values = deviation * jax.random.normal(own_key, dims, jnp.float32)
    if cuts:
        values = values * shard_levels(own_key, dims, cuts, -0.22, 0.18)
    return jnp.clip(values, -most, most).astype(held_as)


def setup_inputs(seed: int = 0) -> dict:
    keys = jax.random.split(jax.random.key(seed), 17)
    return {
        "decoder_input": normal_values(keys[0], (ROWS, LEN, D), 1.0, 6.0, ((0, 16),)),
        "encoder_states": normal_values(keys[1], (ROWS, ENC_LEN, D), 1.0, 6.0, ((0, 16),)),
        "decoder_segments": jax.vmap(lambda own: jnp.searchsorted(jnp.cumsum(ragged_sizes(own, DOCS, LEN, LEN // 2, 2)), jnp.arange(LEN), side="right"))(jax.random.split(keys[2], ROWS)).reshape((ROWS, LEN)).astype(jnp.int32),
        "encoder_segments": jax.vmap(lambda own: jnp.searchsorted(jnp.cumsum(ragged_sizes(own, DOCS, ENC_LEN, ENC_LEN // 2, 2)), jnp.arange(ENC_LEN), side="right"))(jax.random.split(keys[3], ROWS)).reshape((ROWS, ENC_LEN)).astype(jnp.int32),
        "output_cotangent": normal_values(keys[4], (ROWS, LEN, D), 1.0, 6.0, ((0, 16),)),
        "block_slots": draw_block_slots(jax.random.fold_in(keys[16], 71), 0),
        "master": draw_master(jax.random.fold_in(keys[16], 71), 0),
        "first_moment": draw_first_moment(jax.random.fold_in(keys[16], 71), 0),
        "second_moment": draw_second_moment(jax.random.fold_in(keys[16], 71), 0),
        "row_statistics": draw_row_statistics(jax.random.fold_in(keys[16], 71), 0),
        "column_statistics": draw_column_statistics(jax.random.fold_in(keys[16], 71), 0),
        "row_basis": draw_row_basis(jax.random.fold_in(keys[16], 71), 0),
        "column_basis": draw_column_basis(jax.random.fold_in(keys[16], 71), 0),
        "vectors": draw_vectors(jax.random.fold_in(keys[16], 71), 0),
        "vector_first": draw_vector_first(jax.random.fold_in(keys[16], 71), 0),
        "vector_second": draw_vector_second(jax.random.fold_in(keys[16], 71), 0),
    }


PRECISE = lax.Precision.HIGHEST
NEGATIVE = -1e+30
EPS_NORM = 1e-05
MOMENT_DECAY = 0.5
LEARN_RATE = 0.04
WEIGHT_DECAY = 0.01
VECTOR_RATE = 0.25
ADAM_EPS = 1e-08
newton_turns = 8

@jax.custom_vjp
def low(v):
    return lax.optimization_barrier(v.astype(jnp.bfloat16)).astype(jnp.float32)

@jax.custom_vjp
def low_back(v):
    return v

def low_keep(v):
    return (low(v), None)

def low_pass(kept, grad):
    return (grad,)

def back_keep(v):
    return (v, None)

def back_low(kept, grad):
    return (low(grad),)
low.defvjp(low_keep, low_pass)
low_back.defvjp(back_keep, back_low)

def round_both(values):
    return low_back(low(values))

def layer_norm(inputs, gain, shift):
    center = inputs - lax.optimization_barrier(jnp.mean(inputs, axis=-1, keepdims=True))
    spread = lax.optimization_barrier(jnp.mean(center * center, axis=-1, keepdims=True))
    return center * lax.rsqrt(spread + EPS_NORM) * gain + shift

def attend(queries, key_rows, values, allowed):
    slice_count = queries.shape[0]
    length = queries.shape[1]
    query_heads = queries.reshape(slice_count, length, HEADS_DEV, HD)
    key_heads = key_rows.reshape(slice_count, key_rows.shape[1], HEADS_DEV, HD)
    value_heads = values.reshape(slice_count, values.shape[1], HEADS_DEV, HD)
    scores = low_back(jnp.einsum('sqhe,skhe->shqk', query_heads, key_heads, precision=PRECISE) * HD ** (-0.5))
    scores = jnp.where(allowed, scores, NEGATIVE)
    expons = jnp.exp(scores - lax.optimization_barrier(jnp.max(scores, axis=-1, keepdims=True)))
    chances = low(expons / lax.optimization_barrier(jnp.sum(expons, axis=-1, keepdims=True)))
    context = jnp.einsum('shqk,skhe->sqhe', chances, value_heads, precision=PRECISE)
    return round_both(context.reshape(slice_count, length, HEADS_DEV * HD))

def merge_slices(terms_in, matrix):
    partial_value = jnp.einsum('sta,sda->std', terms_in, matrix, precision=PRECISE)
    return low_back(lax.optimization_barrier(jnp.sum(low(partial_value), axis=0)))

def row_forward(inputs, encoded, weight_all, vector_all, decoder_ids, encoder_ids):
    weights = low(weight_all)
    gains = low(vector_all)
    head_width = HEADS_DEV * HD

    def column_run(number):
        return weights[:, :, number * head_width:(number + 1) * head_width]

    def project(source, matrix):
        return round_both(jnp.einsum('td,sda->sta', source, matrix, precision=PRECISE))
    places = jnp.arange(LEN)
    self_allowed = (decoder_ids[:, None] == decoder_ids[None, :]) & (places[None, :] <= places[:, None])
    cross_allowed = decoder_ids[:, None] == encoder_ids[None, :]
    self_context = attend(project(inputs, column_run(0)), project(inputs, column_run(1)), project(inputs, column_run(2)), self_allowed)
    normed_one = layer_norm(inputs + merge_slices(self_context, column_run(3)), gains[0], gains[1])
    normed_one_low = low(normed_one)
    cross_context = attend(project(normed_one_low, column_run(4)), project(encoded, column_run(5)), project(encoded, column_run(6)), cross_allowed)
    normed_two = layer_norm(normed_one + merge_slices(cross_context, column_run(7)), gains[2], gains[3])
    normed_two_low = low(normed_two)
    up_values = low_back(jnp.einsum('td,sdf->stf', normed_two_low, weights[:, :, 8 * head_width:8 * head_width + FF_DEV], precision=PRECISE))
    hidden = low(jax.nn.gelu(up_values))
    feed = merge_slices(hidden, weights[:, :, 8 * head_width + FF_DEV:])
    return layer_norm(normed_two + feed, gains[4], gains[5])

def assemble(master, block_slots):
    blocks = jnp.take(master, block_slots, axis=1)
    blocks = blocks.reshape(SLICES, D // BR, COLS_DEV // HD, BR, HD).transpose(0, 1, 3, 2, 4)
    return blocks.reshape(SLICES, D, COLS_DEV)

def disassemble(gradient, block_slots):
    blocks = gradient.reshape(SLICES, D // BR, BR, COLS_DEV // HD, HD).transpose(0, 1, 3, 2, 4)
    blocks = blocks.reshape(SLICES, BLK_T, BR, HD)
    return jnp.zeros_like(blocks).at[:, block_slots].set(blocks)

def orthonormal(matrix):
    norm_value = jnp.sqrt(lax.optimization_barrier(jnp.sum(matrix * matrix, axis=(-2, -1), keepdims=True)) + 1e-06)
    current = matrix / norm_value
    for repeat in range(newton_turns):
        gram = jnp.einsum('...ji,...jk->...ik', current, current, precision=PRECISE)
        current = 1.5 * current - 0.5 * jnp.einsum('...ij,...jk->...ik', current, gram, precision=PRECISE)
    return current

def soap_step(gradient, weight, first, second, left, right, left_basis, right_basis):
    left_new = MOMENT_DECAY * left + (1.0 - MOMENT_DECAY) * jnp.einsum('...ij,...kj->...ik', gradient, gradient, precision=PRECISE)
    right_new = MOMENT_DECAY * right + (1.0 - MOMENT_DECAY) * jnp.einsum('...ji,...jk->...ik', gradient, gradient, precision=PRECISE)
    left_turn = orthonormal(jnp.einsum('...ij,...jk->...ik', left_new, left_basis, precision=PRECISE))
    right_turn = orthonormal(jnp.einsum('...ij,...jk->...ik', right_new, right_basis, precision=PRECISE))
    partway = jnp.einsum('...ji,...jk->...ik', left_turn, gradient, precision=PRECISE)
    turned = jnp.einsum('...ik,...kl->...il', partway, right_turn, precision=PRECISE)
    first_new = MOMENT_DECAY * first + (1.0 - MOMENT_DECAY) * turned
    second_new = MOMENT_DECAY * second + (1.0 - MOMENT_DECAY) * turned * turned
    correction = 1.0 - MOMENT_DECAY ** STEP
    direction = first_new / correction / (jnp.sqrt(second_new / correction) + ADAM_EPS)
    partback = jnp.einsum('...ij,...jk->...ik', left_turn, direction, precision=PRECISE)
    backward_step = jnp.einsum('...ik,...lk->...il', partback, right_turn, precision=PRECISE)
    weight_new = weight * (1.0 - LEARN_RATE * WEIGHT_DECAY) - LEARN_RATE * backward_step
    return (weight_new, first_new, second_new, left_new, right_new, left_turn, right_turn)

def adam_vector(gradient, weight, first, second):
    first_new = MOMENT_DECAY * first + (1.0 - MOMENT_DECAY) * gradient
    second_new = MOMENT_DECAY * second + (1.0 - MOMENT_DECAY) * gradient * gradient
    correction = 1.0 - MOMENT_DECAY ** STEP
    weight_new = weight - VECTOR_RATE * (first_new / correction) / (jnp.sqrt(second_new / correction) + ADAM_EPS)
    return (weight_new, first_new, second_new)

def reference(decoder_input, encoder_states, decoder_segments, encoder_segments, output_cotangent, block_slots, master, first_moment, second_moment, row_statistics, column_statistics, row_basis, column_basis, vectors, vector_first, vector_second):
    weight_all = assemble(master, block_slots)

    def one_row(running, row_items):
        inputs, encoded, decoder_ids, encoder_ids, cotangent = row_items

        def one_layer(input_full, encoded_full, weight_full, vector_full):
            return row_forward(input_full, encoded_full, weight_full, vector_full, decoder_ids, encoder_ids)
        output, pullback = jax.vjp(one_layer, inputs.astype(jnp.float32), encoded.astype(jnp.float32), weight_all, vectors)
        grad_input, grad_encoder, grad_weight, grad_vector = pullback(cotangent.astype(jnp.float32))
        return ((running[0] + grad_weight, running[1] + grad_vector), (output.astype(jnp.bfloat16), grad_input, grad_encoder))
    start_sums = (jnp.zeros_like(weight_all), jnp.zeros_like(vectors))
    sums, row_outputs = lax.scan(one_row, start_sums, (decoder_input, encoder_states, decoder_segments, encoder_segments, output_cotangent))
    block_output, input_gradient, encoder_gradient = row_outputs
    by_slot = disassemble(sums[0], block_slots)
    updated = soap_step(by_slot, master, first_moment, second_moment, row_statistics, column_statistics, row_basis, column_basis)
    vector_new = adam_vector(sums[1], vectors, vector_first, vector_second)
    return (block_output, input_gradient, encoder_gradient, updated[0], updated[1], updated[2], updated[3], updated[4], updated[5], updated[6], vector_new[0], vector_new[1], vector_new[2])
```

```python
import jax
import jax.numpy as jnp
from jax import lax
from jax.sharding import PartitionSpec as P

HD = 64
FF = 2048
STEP = 10

PRECISE = lax.Precision.HIGHEST
NEGATIVE = -1e30
EPS_NORM = 1e-05
MOMENT_DECAY = 0.5
LEARN_RATE = 0.04
WEIGHT_DECAY = 0.01
VECTOR_RATE = 0.25
ADAM_EPS = 1e-08
NEWTON_TURNS = 8
VECTOR_ROWS = 16
F32 = jnp.float32
BF16 = jnp.bfloat16


def nn(left, right):
    return lax.dot_general(left, right, (((1,), (0,)), ((), ())), preferred_element_type=F32)


def nt(left, right):
    return lax.dot_general(left, right, (((1,), (1,)), ((), ())), preferred_element_type=F32)


def tn(left, right):
    return lax.dot_general(left, right, (((0,), (0,)), ((), ())), preferred_element_type=F32)


def low(values):
    return values.astype(BF16)


def normalise(inputs):
    center = inputs - jnp.mean(inputs, axis=-1, keepdims=True)
    spread = jnp.mean(center * center, axis=-1, keepdims=True)
    inverse = lax.rsqrt(spread + EPS_NORM)
    return center * inverse, inverse


def normalise_back(grad, hat, inverse, gain):
    scaled = grad * gain
    inner = (
        scaled
        - jnp.mean(scaled, axis=-1, keepdims=True)
        - hat * jnp.mean(scaled * hat, axis=-1, keepdims=True)
    )
    return (
        inner * inverse,
        jnp.sum(grad * hat, axis=0, keepdims=True),
        jnp.sum(grad, axis=0, keepdims=True),
    )


def attend(queries, key_rows, values, allowed):
    heads = queries.shape[1] // HD
    q = queries.reshape(-1, heads, HD)
    k = key_rows.reshape(-1, heads, HD)
    v = values.reshape(-1, heads, HD)
    scores = jnp.einsum("qhe,khe->hqk", q, k, preferred_element_type=F32) * HD**-0.5
    scores = jnp.where(allowed[None], scores, NEGATIVE)
    expons = jnp.exp(scores - jnp.max(scores, axis=-1, keepdims=True))
    chances = expons / jnp.sum(expons, axis=-1, keepdims=True)
    context = jnp.einsum("hqk,khe->qhe", low(chances), v, preferred_element_type=F32)
    return low(context.reshape(queries.shape)), chances


def attend_back(queries, key_rows, values, chances, grad_context):
    heads = queries.shape[1] // HD
    q = queries.reshape(-1, heads, HD)
    k = key_rows.reshape(-1, heads, HD)
    v = values.reshape(-1, heads, HD)
    g = grad_context.reshape(-1, heads, HD)
    grad_chances = jnp.einsum("qhe,khe->hqk", g, v, preferred_element_type=F32)
    grad_values = jnp.einsum("hqk,qhe->khe", low(chances), g, preferred_element_type=F32)
    grad_scores = low(
        chances * (grad_chances - jnp.sum(grad_chances * chances, axis=-1, keepdims=True))
    )
    grad_query = jnp.einsum("hqk,khe->qhe", grad_scores, k, preferred_element_type=F32) * HD**-0.5
    grad_keys = jnp.einsum("hqk,qhe->khe", grad_scores, q, preferred_element_type=F32) * HD**-0.5
    return (
        low(grad_query.reshape(queries.shape)),
        low(grad_keys.reshape(key_rows.shape)),
        low(grad_values.reshape(values.shape)),
    )


def both(weights, number, width):
    rows = weights[:, number * width : (number + 1) * width]
    return rows.reshape(-1, weights.shape[2])


def orthonormal(matrix):
    norm_value = jnp.sqrt(jnp.sum(matrix * matrix, axis=(-2, -1), keepdims=True) + 1e-06)
    current = matrix / norm_value
    for _ in range(NEWTON_TURNS):
        gram = jnp.einsum("...ji,...jk->...ik", current, current, precision=PRECISE)
        current = 1.5 * current - 0.5 * jnp.einsum(
            "...ij,...jk->...ik", current, gram, precision=PRECISE
        )
    return current


def soap_step(gradient, weight, first, second, left, right, left_basis, right_basis):
    left_new = MOMENT_DECAY * left + (1.0 - MOMENT_DECAY) * jnp.einsum(
        "...ij,...kj->...ik", gradient, gradient, precision=PRECISE
    )
    right_new = MOMENT_DECAY * right + (1.0 - MOMENT_DECAY) * jnp.einsum(
        "...ji,...jk->...ik", gradient, gradient, precision=PRECISE
    )
    left_turn = orthonormal(
        jnp.einsum("...ij,...jk->...ik", left_new, left_basis, precision=PRECISE)
    )
    right_turn = orthonormal(
        jnp.einsum("...ij,...jk->...ik", right_new, right_basis, precision=PRECISE)
    )
    partway = jnp.einsum("...ji,...jk->...ik", left_turn, gradient, precision=PRECISE)
    turned = jnp.einsum("...ik,...kl->...il", partway, right_turn, precision=PRECISE)
    first_new = MOMENT_DECAY * first + (1.0 - MOMENT_DECAY) * turned
    second_new = MOMENT_DECAY * second + (1.0 - MOMENT_DECAY) * turned * turned
    correction = 1.0 - MOMENT_DECAY**STEP
    direction = first_new / correction / (jnp.sqrt(second_new / correction) + ADAM_EPS)
    partback = jnp.einsum("...ij,...jk->...ik", left_turn, direction, precision=PRECISE)
    backward_step = jnp.einsum("...ik,...lk->...il", partback, right_turn, precision=PRECISE)
    weight_new = weight * (1.0 - LEARN_RATE * WEIGHT_DECAY) - LEARN_RATE * backward_step
    return (weight_new, first_new, second_new, left_new, right_new, left_turn, right_turn)


def adam_vector(gradient, weight, first, second):
    first_new = MOMENT_DECAY * first + (1.0 - MOMENT_DECAY) * gradient
    second_new = MOMENT_DECAY * second + (1.0 - MOMENT_DECAY) * gradient * gradient
    correction = 1.0 - MOMENT_DECAY**STEP
    weight_new = weight - VECTOR_RATE * (first_new / correction) / (
        jnp.sqrt(second_new / correction) + ADAM_EPS
    )
    return (weight_new, first_new, second_new)


def own_rows(values, index, chunk):
    early = lax.dynamic_slice_in_dim(values, index * chunk, chunk, 0)
    late = lax.dynamic_slice_in_dim(values, (3 - index) * chunk, chunk, 0)
    return jnp.concatenate([early, late], axis=0)


def in_order(mine, other, index, chunk):
    inner = jnp.where(index == 0, other, mine)
    outer = jnp.where(index == 0, mine, other)
    return jnp.concatenate([outer[:chunk], inner, outer[chunk:]], axis=0)


def per_device(
    decoder_input,
    encoder_states,
    decoder_segments,
    encoder_segments,
    output_cotangent,
    block_slots,
    master,
    first_moment,
    second_moment,
    row_statistics,
    column_statistics,
    row_basis,
    column_basis,
    vectors,
    vector_first,
    vector_second,
):
    core = lax.axis_index("tensor")
    cores = lax.axis_size("tensor")
    rings = lax.axis_size("dp")
    swap = [(0, 1), (1, 0)]
    owned_count, block_height = master.shape[1], master.shape[2]
    vector_cols = vectors.shape[1]
    length, width = decoder_input.shape[1], decoder_input.shape[2]
    row_count = width // block_height
    block_total = block_slots.shape[0]
    column_count = block_total // row_count
    hidden_width = FF // cores
    head_width = (column_count * HD - 2 * hidden_width) // 8
    chunk = length // 4

    payload = low(master[0]).transpose(0, 2, 1).reshape(owned_count * HD, block_height)
    small = jnp.pad(
        low(vectors).reshape(-1), (0, VECTOR_ROWS * block_height - vectors.size)
    ).reshape(VECTOR_ROWS, block_height)
    gathered = lax.all_gather(
        jnp.concatenate([payload, small], axis=0), ("dp", "tensor"), axis=0, tiled=False
    )
    gathered = gathered.reshape(rings, cores, owned_count * HD + VECTOR_ROWS, block_height)
    vector_rows = (
        gathered[:, 0, owned_count * HD :]
        .reshape(rings, -1)[:, : vectors.size]
        .reshape(rings, 6, vector_cols)
        .transpose(1, 0, 2)
        .reshape(6, width)
        .astype(F32)
    )
    blocks = gathered[:, :, : owned_count * HD].reshape(
        rings, cores, owned_count, HD, block_height
    )
    blocks = blocks.transpose(1, 0, 2, 3, 4).reshape(cores, block_total, HD, block_height)
    blocks = jnp.take(blocks, block_slots, axis=1, mode="clip")
    weights = (
        blocks.reshape(cores, row_count, column_count, HD, block_height)
        .transpose(0, 2, 3, 1, 4)
        .reshape(cores, column_count * HD, width)
    )

    def kind(number):
        return both(weights, number, head_width)

    upper = weights[:, 8 * head_width : 8 * head_width + hidden_width].reshape(-1, width)
    lower = weights[:, 8 * head_width + hidden_width :].reshape(-1, width)

    tokens, encoder_rows = decoder_input[0], encoder_states[0]
    ids, encoder_ids = decoder_segments[0], encoder_segments[0]
    own_tokens = own_rows(tokens, core, chunk)
    own_ids = own_rows(ids, core, chunk)
    places = jnp.arange(length)
    own_places = own_rows(places, core, chunk)
    self_allowed = (own_ids[:, None] == ids[None, :]) & (places[None, :] <= own_places[:, None])
    cross_allowed = own_ids[:, None] == encoder_ids[None, :]
    sq = low(nt(own_tokens, kind(0)))
    sk = low(nt(tokens, kind(1)))
    sv = low(nt(tokens, kind(2)))
    self_context, self_chances = attend(sq, sk, sv, self_allowed)
    hat_one, inverse_one = normalise(own_tokens.astype(F32) + nn(self_context, kind(3)))
    y_one = hat_one * vector_rows[0] + vector_rows[1]
    y_one_low = low(y_one)
    cq = low(nt(y_one_low, kind(4)))
    ck = low(nt(encoder_rows, kind(5)))
    cv = low(nt(encoder_rows, kind(6)))
    cross_context, cross_chances = attend(cq, ck, cv, cross_allowed)
    hat_two, inverse_two = normalise(y_one + nn(cross_context, kind(7)))
    y_two = hat_two * vector_rows[2] + vector_rows[3]
    y_two_low = low(y_two)
    up_values = nt(y_two_low, upper)
    hidden, gelu_back = jax.vjp(jax.nn.gelu, up_values)
    hidden = low(hidden)
    hat_three, inverse_three = normalise(y_two + nn(hidden, lower))
    own_output = low(hat_three * vector_rows[4] + vector_rows[5])

    cotangent = own_rows(output_cotangent[0], core, chunk).astype(F32)
    grad_three, gain_three, shift_three = normalise_back(
        cotangent, hat_three, inverse_three, vector_rows[4]
    )
    grad_low = low(grad_three)
    grad_up = low(gelu_back(nt(grad_low, lower))[0])
    grad_lower = tn(hidden, grad_low)
    grad_upper = tn(grad_up, y_two_low)
    grad_two, gain_two, shift_two = normalise_back(
        grad_three + nn(grad_up, upper), hat_two, inverse_two, vector_rows[2]
    )
    grad_low = low(grad_two)
    grad_cross_out = tn(cross_context, grad_low)
    gq, gk, gv = attend_back(cq, ck, cv, cross_chances, low(nt(grad_low, kind(7))))
    grad_cross = [tn(gq, y_one_low), tn(gk, encoder_rows), tn(gv, encoder_rows), grad_cross_out]
    part_encoder = low(nn(gk, kind(5)) + nn(gv, kind(6)))
    grad_one, gain_one, shift_one = normalise_back(
        grad_two + nn(gq, kind(4)), hat_one, inverse_one, vector_rows[0]
    )
    grad_low = low(grad_one)
    grad_self_out = tn(self_context, grad_low)
    gq, gk, gv = attend_back(sq, sk, sv, self_chances, low(nt(grad_low, kind(3))))
    grad_self = [tn(gq, own_tokens), tn(gk, tokens), tn(gv, tokens), grad_self_out]
    own_input = grad_one + nn(gq, kind(0))
    part_input = low(nn(gk, kind(1)) + nn(gv, kind(2)))

    half_input, half_encoder, half_output, half_own = lax.ppermute(
        (part_input, part_encoder, own_output, low(own_input)), "tensor", swap
    )
    block_output = in_order(own_output, half_output, core, chunk)
    input_gradient = (
        in_order(own_input, half_own.astype(F32), core, chunk)
        + part_input.astype(F32)
        + half_input.astype(F32)
    )
    encoder_gradient = part_encoder.astype(F32) + half_encoder.astype(F32)

    parts = [part.reshape(cores, -1, width) for part in grad_self + grad_cross]
    parts += [grad_upper.reshape(cores, -1, width), grad_lower.reshape(cores, -1, width)]
    grad_weights = low(jnp.concatenate(parts, axis=1))
    grad_blocks = (
        grad_weights.reshape(cores, column_count, HD, row_count, block_height)
        .transpose(0, 3, 1, 2, 4)
        .reshape(cores, block_total, HD, block_height)
    )
    inverse = (
        jnp.zeros((block_total,), jnp.int32)
        .at[block_slots]
        .set(jnp.arange(block_total, dtype=jnp.int32))
    )
    by_slot = jnp.take(grad_blocks, inverse, axis=1, mode="clip")
    by_slot = by_slot.reshape(cores, rings, owned_count * HD, block_height)
    grad_vectors = jnp.concatenate(
        [gain_one, shift_one, gain_two, shift_two, gain_three, shift_three], axis=0
    )
    small = low(grad_vectors).reshape(6, rings, vector_cols).transpose(1, 0, 2).reshape(rings, -1)
    small = jnp.pad(small, ((0, 0), (0, VECTOR_ROWS * block_height - vectors.size)))
    small = jnp.broadcast_to(
        small.reshape(1, rings, VECTOR_ROWS, block_height),
        (cores, rings, VECTOR_ROWS, block_height),
    )
    terms = jnp.concatenate([by_slot, small], axis=2)
    mine = lax.dynamic_index_in_dim(terms, core, 0, False)
    sent = lax.dynamic_index_in_dim(terms, 1 - core, 0, False)
    arrived = lax.ppermute(sent, "tensor", swap)
    mine = low(mine.astype(F32) + arrived.astype(F32))
    summed = lax.psum_scatter(mine, "dp", scatter_dimension=0, tiled=True)[0].astype(F32)
    owned = summed[: owned_count * HD].reshape(owned_count, HD, block_height).transpose(0, 2, 1)
    vector_owned = summed[owned_count * HD :].reshape(-1)[: vectors.size].reshape(vectors.shape)

    updated = soap_step(
        owned,
        master[0],
        first_moment[0],
        second_moment[0],
        row_statistics[0],
        column_statistics[0],
        row_basis[0],
        column_basis[0],
    )
    vector_new = adam_vector(vector_owned, vectors, vector_first, vector_second)
    return (
        block_output[None],
        input_gradient[None],
        encoder_gradient[None],
        updated[0][None],
        updated[1][None],
        updated[2][None],
        updated[3][None],
        updated[4][None],
        updated[5][None],
        updated[6][None],
        vector_new[0],
        vector_new[1],
        vector_new[2],
    )


def solution(mesh):
    blocks = P("tensor", "dp", None, None)
    rows = P("dp", None, None)
    return jax.shard_map(
        per_device,
        mesh=mesh,
        in_specs=(rows, rows, P("dp", None), P("dp", None), rows, P())
        + (blocks,) * 7
        + (P(None, "dp"),) * 3,
        out_specs=(rows,) * 3 + (blocks,) * 7 + (P(None, "dp"),) * 3,
        check_vma=False,
    )
```

```python
import functools

import jax
import jax.numpy as jnp
from jax import lax
from jax.experimental import pallas as pl
from jax.experimental.pallas import tpu as pltpu
from jax.sharding import PartitionSpec as P

HD = 64
FF = 2048
STEP = 10

PRECISE = lax.Precision.HIGHEST
NEGATIVE = -1e30
EPS_NORM = 1e-05
MOMENT_DECAY = 0.5
LEARN_RATE = 0.04
WEIGHT_DECAY = 0.01
VECTOR_RATE = 0.25
ADAM_EPS = 1e-08
NEWTON_TURNS = 8
VECTOR_ROWS = 16
MIB = 2**20
F32 = jnp.float32
BF16 = jnp.bfloat16
VMEM = pl.BlockSpec(memory_space=pltpu.VMEM)
SMEM = pl.BlockSpec(memory_space=pltpu.SMEM)


def nn(left, right):
    return lax.dot_general(left, right, (((1,), (0,)), ((), ())), preferred_element_type=F32)


def nt(left, right):
    return lax.dot_general(left, right, (((1,), (1,)), ((), ())), preferred_element_type=F32)


def tn(left, right):
    return lax.dot_general(left, right, (((0,), (0,)), ((), ())), preferred_element_type=F32)


def low(values):
    return values.astype(BF16)


def span(number, size):
    return slice(number * size, (number + 1) * size)


def rows_at(number, size):
    return pl.ds(pl.multiple_of(number * size, size), size)


def shape(*dims, dtype=F32):
    return jax.ShapeDtypeStruct(dims, dtype)


def limit(mib):
    return pltpu.CompilerParams(vmem_limit_bytes=mib * MIB)


def block_places(columns, cores):
    hidden = FF // cores // HD
    heads = (columns - 2 * hidden) // 8
    places = []
    for column in range(columns):
        if column < 8 * heads:
            places.append((column // heads, column % heads * HD))
        else:
            column -= 8 * heads
            places.append((8 + column // hidden, column % hidden * HD))
    return places, heads * HD, hidden * HD


def assemble_kernel(rows_ref, gathered_ref, self_ref, cross_ref, feed_ref, vec_ref,
                    *, cores, per_core, group):
    height = gathered_ref.shape[1]
    row_count = self_ref.shape[1] // height
    columns = rows_ref.shape[0] // row_count
    places, head_rows, hidden_rows = block_places(columns, cores)
    for core in range(cores):
        for row in range(row_count):
            for column in range(columns):
                kind, inner = places[column]
                size = head_rows if kind < 8 else hidden_rows
                w_ref = self_ref if kind < 4 else cross_ref if kind < 8 else feed_ref
                target = (kind % 4 * cores + core) * size + inner
                source = pl.multiple_of(rows_ref[row * columns + column] + core * per_core, 16)
                w_ref[target : target + HD, span(row, height)] = gathered_ref[pl.ds(source, HD), :]
    rings = gathered_ref.shape[0] // per_core // cores
    for part in range(row_count):
        total = jnp.zeros((VECTOR_ROWS, height), F32)
        for ring in range(part * group, (part + 1) * group):
            if ring < rings:
                end = (ring * cores + 1) * per_core
                total = total + gathered_ref[end - VECTOR_ROWS : end, :].astype(F32)
        vec_ref[:, span(part, height)] = total


def assemble(rows, gathered, cores, per_core, width, group):
    return pl.pallas_call(
        functools.partial(assemble_kernel, cores=cores, per_core=per_core, group=group),
        out_shape=(
            shape(4 * width, width, dtype=BF16),
            shape(4 * width, width, dtype=BF16),
            shape(2 * FF, width, dtype=BF16),
            shape(VECTOR_ROWS, width),
        ),
        in_specs=[SMEM, VMEM],
        out_specs=[VMEM] * 4,
        compiler_params=limit(32),
        name="assemble",
    )(rows, gathered)


def scatter_kernel(rows_ref, ff_ref, ff_in_ref, cross_ref, cross_in_ref, self_ref, self_in_ref,
                   vec_ref, vec_in_ref, out_ref, *, cores, per_ring, group):
    height = out_ref.shape[1]
    row_count = self_ref.shape[1] // height
    columns = rows_ref.shape[0] // row_count
    places, head_rows, hidden_rows = block_places(columns, cores)
    for row in range(row_count):
        lanes = span(row, height)
        for column in range(columns):
            kind, inner = places[column]
            if kind < 4:
                one, two, start = self_ref, self_in_ref, kind * head_rows
            elif kind < 8:
                one, two, start = cross_ref, cross_in_ref, (kind - 4) * head_rows
            else:
                one, two, start = ff_ref, ff_in_ref, (kind - 8) * hidden_rows
            source = slice(start + inner, start + inner + HD)
            target = pl.multiple_of(rows_ref[row * columns + column], 16)
            total = one[source, lanes].astype(F32) + two[source, lanes].astype(F32)
            out_ref[pl.ds(target, HD), :] = low(total)
    total = low(vec_ref[...] + vec_in_ref[...])
    for ring in range(out_ref.shape[0] // per_ring):
        end = (ring + 1) * per_ring
        out_ref[end - VECTOR_ROWS : end, :] = total[:, span(ring // group, height)]


def scatter(rows, terms, cores, rings, per_ring, height, group):
    return pl.pallas_call(
        functools.partial(scatter_kernel, cores=cores, per_ring=per_ring, group=group),
        out_shape=shape(rings * per_ring, height, dtype=BF16),
        in_specs=[SMEM] + [VMEM] * 8,
        out_specs=VMEM,
        compiler_params=limit(32),
        name="scatter",
    )(rows, *terms)


def norm_forward(total_ref, vec_ref, first, hat_ref, inverse_ref, out_ref, step=64):
    gain, shift = vec_ref[first : first + 1], vec_ref[first + 1 : first + 2]

    def body(number, carry):
        rows = rows_at(number, step)
        values = total_ref[rows]
        center = values - jnp.mean(values, axis=1, keepdims=True)
        inverse = lax.rsqrt(jnp.mean(center * center, axis=1, keepdims=True) + EPS_NORM)
        hat = center * inverse
        hat_ref[rows] = hat
        inverse_ref[rows] = inverse
        out_ref[rows] = (hat * gain + shift).astype(out_ref.dtype)
        return carry

    lax.fori_loop(0, total_ref.shape[0] // step, body, 0)


def norm_backward(grad_ref, hat_ref, inverse_ref, gain, out_ref, step=64):
    width = grad_ref.shape[1]

    def body(number, carry):
        rows = rows_at(number, step)
        grad, hat = grad_ref[rows].astype(F32), hat_ref[rows]
        scaled = grad * gain
        middle = jnp.mean(scaled, axis=1, keepdims=True)
        slope = jnp.mean(scaled * hat, axis=1, keepdims=True)
        out_ref[rows] = (scaled - middle - hat * slope) * inverse_ref[rows]
        return (
            carry[0] + jnp.sum((grad * hat).reshape(step // 8, 8, width), axis=0),
            carry[1] + jnp.sum(grad.reshape(step // 8, 8, width), axis=0),
        )

    zeros = jnp.zeros((8, width), F32)
    sums = lax.fori_loop(0, grad_ref.shape[0] // step, body, (zeros, zeros))
    return [jnp.sum(one, axis=0, keepdims=True) for one in sums]


def split_heads(source_ref, masked_ref, factor):
    for head in range(masked_ref.shape[0]):
        pair = source_ref[:, span(head // 2, 2 * HD)]
        lane = lax.broadcasted_iota(jnp.int32, pair.shape, 1)
        here = (lane >= HD) if head % 2 else (lane < HD)
        masked_ref[head] = jnp.where(here, pair, jnp.zeros_like(pair)) * jnp.asarray(factor, BF16)


def staged(count, early, middle, late, ahead=2, lag=2):
    ready = [early(number) for number in range(min(ahead, count))]
    held = []
    for number in range(count):
        now = ready.pop(0)
        if number + ahead < count:
            ready.append(early(number + ahead))
        held.append((number, middle(number, now)))
        if len(held) > lag:
            late(*held.pop(0))
    while held:
        late(*held.pop(0))


def attend_forward(bounds_ref, bias_ref, masked_q, k_ref, vt_ref, m_ref, l_ref, acc_ref, lse_ref,
                   ctxt_ref):
    heads, chunk = m_ref.shape
    for part in range(lse_ref.shape[1] // chunk):
        cols = span(part, chunk)
        m_ref[...] = jnp.full(m_ref.shape, NEGATIVE, F32)
        l_ref[...] = jnp.zeros(l_ref.shape, F32)
        acc_ref[...] = jnp.zeros(acc_ref.shape, F32)

        def body(number, carry):
            keys = rows_at(number, chunk)
            bias = bias_ref[keys, cols]

            def early(head):
                return nt(k_ref[keys, span(head // 2, 2 * HD)], masked_q[head, cols]) + bias

            def middle(head, scores):
                row = slice(head, head + 1)
                before = m_ref[row]
                highest = jnp.maximum(before, jnp.max(scores, axis=0, keepdims=True))
                shrink = jnp.exp(before - highest)
                expons = jnp.exp(scores - highest)
                l_ref[row] = l_ref[row] * shrink + jnp.sum(expons, axis=0, keepdims=True)
                m_ref[row] = highest
                return shrink, low(expons)

            def late(head, pair):
                rows = span(head, HD)
                acc_ref[rows] = acc_ref[rows] * pair[0] + nn(vt_ref[rows, keys], pair[1])

            staged(heads, early, middle, late)
            return carry

        lax.fori_loop(bounds_ref[2 * part], bounds_ref[2 * part + 1], body, 0)
        for head in range(heads):
            rows = span(head, HD)
            ctxt_ref[rows, cols] = low(acc_ref[rows] / l_ref[head : head + 1])
        lse_ref[:, cols] = m_ref[...] + jnp.log(l_ref[...])


def forward_kernel(bounds_ref, x_ref, own_ref, w_ref, bias_ref, vec_ref,
                   q_ref, k_ref, lse_ref, ctxt_ref, hat_ref, inverse_ref, y_ref,
                   masked_q, vt_ref, m_ref, l_ref, acc_ref, *, first):
    width = w_ref.shape[1]
    chunk = m_ref.shape[1]
    q_ref[...] = low(nt(low(own_ref[...]), w_ref[span(0, width)]))
    split_heads(q_ref, masked_q, HD**-0.5)
    for part in range(k_ref.shape[0] // chunk):
        rows = span(part, chunk)
        k_ref[rows] = low(nt(x_ref[rows], w_ref[span(1, width)]))
        vt_ref[:, rows] = low(nt(w_ref[span(2, width)], x_ref[rows]))
    attend_forward(
        bounds_ref, bias_ref, masked_q, k_ref, vt_ref, m_ref, l_ref, acc_ref, lse_ref, ctxt_ref
    )
    y_ref[...] = own_ref[...].astype(F32) + tn(ctxt_ref[...], w_ref[span(3, width)])
    norm_forward(y_ref, vec_ref, first, hat_ref, inverse_ref, y_ref)


def call_forward(bounds, x, own, weights, bias, vec, first, name):
    keys, queries = bias.shape
    width = weights.shape[1]
    heads, chunk = width // HD, keys // 4
    return pl.pallas_call(
        functools.partial(forward_kernel, first=first),
        out_shape=(
            shape(queries, width, dtype=BF16),
            shape(keys, width, dtype=BF16),
            shape(heads, queries),
            shape(width, queries, dtype=BF16),
            shape(queries, width),
            shape(queries, 1),
            shape(queries, width),
        ),
        in_specs=[SMEM, VMEM, VMEM, VMEM, VMEM, VMEM],
        out_specs=[VMEM] * 7,
        scratch_shapes=[
            pltpu.VMEM((heads, queries, 2 * HD), BF16),
            pltpu.VMEM((width, keys), BF16),
            pltpu.VMEM((heads, chunk), F32),
            pltpu.VMEM((heads, chunk), F32),
            pltpu.VMEM((width, chunk), F32),
        ],
        compiler_params=limit(48),
        name=name,
    )(bounds, x, own, weights, bias, vec)


def backward_kernel(scalars_ref, x_ref, own_ref, w_ref, bias_ref, vec_ref, grad_ref, q_ref, k_ref,
                    lse_ref, ctxt_ref, *rest, first):
    if first is not None:
        hat_ref, inverse_ref, *rest = rest
        mine_ref, sent_ref, part_ref, next_ref, norms_ref, *rest = rest
    else:
        mine_ref, sent_ref, part_ref, *rest = rest
        next_ref = None
    masked_q, masked_g, v_ref, kt_ref, delta_ref, dqt_ref, dk_ref, dv_ref, dq_ref, out_ref = rest
    heads, queries = lse_ref.shape
    width = w_ref.shape[1]
    chunk = queries // 2
    core = scalars_ref[4]
    half = width // 2

    def keep(kind, gradient):
        out_ref[...] = low(gradient)
        mine_ref[span(kind, half)] = out_ref[rows_at(core, half)]
        sent_ref[span(kind, half)] = out_ref[rows_at(1 - core, half)]

    queries_low = low(own_ref[...])
    grad_low = low(grad_ref[...])
    w_out = w_ref[span(3, width)]
    keep(3, nn(ctxt_ref[...], grad_low))
    out_ref[...] = low(nt(grad_low, w_out))
    split_heads(out_ref, masked_g, 1.0)
    split_heads(q_ref, masked_q, HD**-0.5)
    grad_t = low(nt(w_out, grad_low)).astype(F32) * ctxt_ref[...].astype(F32)
    for head in range(heads):
        delta_ref[head : head + 1] = jnp.sum(grad_t[span(head, HD)], axis=0, keepdims=True)
    for part in range(k_ref.shape[0] // chunk):
        rows = span(part, chunk)
        v_ref[rows] = low(nt(x_ref[rows], w_ref[span(2, width)]))
        kt_ref[:, rows] = low(nt(w_ref[span(1, width)], x_ref[rows]))
    dqt_ref[...] = jnp.zeros(dqt_ref.shape, F32)
    dk_ref[...] = jnp.zeros(dk_ref.shape, F32)
    dv_ref[...] = jnp.zeros(dv_ref.shape, F32)
    for part in range(2):
        cols = span(part, chunk)

        def body(number, carry):
            keys = rows_at(number, chunk)
            bias = bias_ref[keys, cols]

            def early(head):
                pair = span(head // 2, 2 * HD)
                return (
                    nt(k_ref[keys, pair], masked_q[head, cols]) + bias,
                    nt(v_ref[keys, pair], masked_g[head, cols]),
                )

            def middle(head, both):
                row = slice(head, head + 1)
                chances = jnp.exp(both[0] - lse_ref[row, cols])
                return low(chances), low(chances * (both[1] - delta_ref[row, cols]))

            def late(head, both):
                pair, rows = span(head // 2, 2 * HD), span(head, HD)
                dv_ref[keys, pair] += nn(both[0], masked_g[head, cols])
                dk_ref[keys, pair] += nn(both[1], masked_q[head, cols])
                dqt_ref[rows, cols] += nn(kt_ref[rows, keys], both[1])

            staged(heads, early, middle, late)
            return carry

        lax.fori_loop(scalars_ref[2 * part], scalars_ref[2 * part + 1], body, 0)
    dqt = low(dqt_ref[...] * HD**-0.5)
    keep(0, nn(dqt, queries_low))
    dk, dv = low(dk_ref[...]), low(dv_ref[...])
    keep(1, tn(dk, x_ref[...]))
    keep(2, tn(dv, x_ref[...]))
    dq_ref[...] = grad_ref[...] + tn(dqt, w_ref[span(0, width)])
    if first is not None:
        part_ref[...] = low(nn(dk, w_ref[span(1, width)]) + nn(dv, w_ref[span(2, width)]))
        sums = norm_backward(dq_ref, hat_ref, inverse_ref, vec_ref[first : first + 1], next_ref)
        norms_ref[0:1] = sums[0]
        norms_ref[1:2] = sums[1]
    else:
        dk_ref[...] = nn(dk, w_ref[span(1, width)]) + nn(dv, w_ref[span(2, width)])
        for part, place in enumerate((core, 3 - core)):
            dk_ref[rows_at(place, chunk)] += dq_ref[span(part, chunk)]
        part_ref[...] = low(dk_ref[...])


def call_backward(scalars, x, own, weights, bias, vec, grad, saved, norm, first, name):
    keys, queries = bias.shape
    width = weights.shape[1]
    heads = width // HD
    outs = [
        shape(2 * width, width, dtype=BF16),
        shape(2 * width, width, dtype=BF16),
        shape(keys, width, dtype=BF16),
    ]
    if first is not None:
        outs += [shape(queries, width), shape(2, width)]
    return pl.pallas_call(
        functools.partial(backward_kernel, first=first),
        out_shape=outs,
        in_specs=[SMEM, VMEM, VMEM, VMEM]
        + [VMEM] * (3 + len(saved) + len(norm)),
        out_specs=[VMEM] * len(outs),
        scratch_shapes=[
            pltpu.VMEM((heads, queries, 2 * HD), BF16),
            pltpu.VMEM((heads, queries, 2 * HD), BF16),
            pltpu.VMEM((keys, width), BF16),
            pltpu.VMEM((width, keys), BF16),
            pltpu.VMEM((heads, queries), F32),
            pltpu.VMEM((width, queries), F32),
            pltpu.VMEM((keys, width), F32),
            pltpu.VMEM((keys, width), F32),
            pltpu.VMEM((queries, width), F32),
            pltpu.VMEM((width, width), BF16),
        ],
        compiler_params=limit(48),
        name=name,
    )(scalars, x, own, weights, bias, vec, grad, *saved, *norm)


def gelu_both(values):
    scale = (2.0 / jnp.pi) ** 0.5
    square = values * values
    bend = jnp.tanh(values * (scale + scale * 0.044715 * square))
    half = 0.5 + 0.5 * bend
    slope = half + (0.5 * values) * (1.0 - bend * bend) * (scale + 3.0 * scale * 0.044715 * square)
    return values * half, slope


def feed_kernel(core_ref, y_ref, w_ref, vec_ref, cot_ref, hat_two, inverse_two,
                block_ref, next_ref, mine_ref, sent_ref, norms_ref,
                low_ref, hid_ref, slope_ref, total_ref, hat_ref, inverse_ref, grad_low,
                *, step):
    core = core_ref[4]
    hidden = w_ref.shape[0] // 2
    half = hidden // 2
    chunks = hidden // step
    low_ref[...] = low(y_ref[...])
    total_ref[...] = y_ref[...]

    def early(number):
        return nt(w_ref[span(number, step)], low_ref[...])

    def middle(number, up):
        hid, slope = gelu_both(up)
        hid_ref[span(number, step)] = low(hid)
        slope_ref[span(number, step)] = slope

    def late(number, _):
        lower = w_ref[hidden + number * step : hidden + (number + 1) * step]
        total_ref[...] += tn(hid_ref[span(number, step)], lower)

    staged(chunks, early, middle, late, 1, 1)
    norm_forward(total_ref, vec_ref, 4, hat_ref, inverse_ref, block_ref)
    sums = norm_backward(cot_ref, hat_ref, inverse_ref, vec_ref[4:5], total_ref)
    norms_ref[2:3] = sums[0]
    norms_ref[3:4] = sums[1]
    grad_low[...] = low(total_ref[...])

    def place(number):
        inner = number % (chunks // 2)
        row = (core if number < chunks // 2 else 1 - core) * half + inner * step
        return inner, pl.multiple_of(row, step)

    def down(number):
        row = place(number)[1]
        return nt(w_ref[pl.ds(pl.multiple_of(hidden + row, step), step)], grad_low[...])

    def turn(number, grad_hidden):
        return low(slope_ref[pl.ds(place(number)[1], step)] * grad_hidden)

    def sums_of(number, grad_up):
        inner, row = place(number)
        rows = pl.ds(row, step)
        kept = mine_ref if number < chunks // 2 else sent_ref
        kept[span(inner, step)] = low(nn(grad_up, low_ref[...]))
        kept[half + inner * step : half + (inner + 1) * step] = low(nn(hid_ref[rows], grad_low[...]))
        total_ref[...] += tn(grad_up, w_ref[rows])

    staged(chunks, down, turn, sums_of, 1, 1)
    sums = norm_backward(total_ref, hat_two, inverse_two, vec_ref[2:3], next_ref)
    norms_ref[0:1] = sums[0]
    norms_ref[1:2] = sums[1]


def call_feed(scalars, y, weights, vec, cotangent, hat, inverse):
    queries, width = y.shape
    hidden = FF
    return pl.pallas_call(
        functools.partial(feed_kernel, step=256),
        out_shape=(
            shape(queries, width, dtype=BF16),
            shape(queries, width),
            shape(hidden, width, dtype=BF16),
            shape(hidden, width, dtype=BF16),
            shape(4, width),
        ),
        in_specs=[SMEM, VMEM, VMEM] + [VMEM] * 4,
        out_specs=[VMEM] * 5,
        scratch_shapes=[
            pltpu.VMEM((queries, width), BF16),
            pltpu.VMEM((hidden, queries), BF16),
            pltpu.VMEM((hidden, queries), F32),
            pltpu.VMEM((queries, width), F32),
            pltpu.VMEM((queries, width), F32),
            pltpu.VMEM((queries, 1), F32),
            pltpu.VMEM((queries, width), BF16),
        ],
        compiler_params=limit(48),
        name="feed",
    )(scalars, y, weights, vec, cotangent, hat, inverse)


def orthonormal(matrix):
    norm_value = jnp.sqrt(jnp.sum(matrix * matrix, axis=(-2, -1), keepdims=True) + 1e-06)
    current = matrix / norm_value
    for _ in range(NEWTON_TURNS):
        gram = jnp.einsum("...ji,...jk->...ik", current, current, precision=PRECISE)
        current = 1.5 * current - 0.5 * jnp.einsum(
            "...ij,...jk->...ik", current, gram, precision=PRECISE
        )
    return current


def soap_step(gradient, weight, first, second, left, right, left_basis, right_basis):
    left_new = MOMENT_DECAY * left + (1.0 - MOMENT_DECAY) * jnp.einsum(
        "...ij,...kj->...ik", gradient, gradient, precision=PRECISE
    )
    right_new = MOMENT_DECAY * right + (1.0 - MOMENT_DECAY) * jnp.einsum(
        "...ji,...jk->...ik", gradient, gradient, precision=PRECISE
    )
    left_turn = orthonormal(
        jnp.einsum("...ij,...jk->...ik", left_new, left_basis, precision=PRECISE)
    )
    right_turn = orthonormal(
        jnp.einsum("...ij,...jk->...ik", right_new, right_basis, precision=PRECISE)
    )
    partway = jnp.einsum("...ji,...jk->...ik", left_turn, gradient, precision=PRECISE)
    turned = jnp.einsum("...ik,...kl->...il", partway, right_turn, precision=PRECISE)
    first_new = MOMENT_DECAY * first + (1.0 - MOMENT_DECAY) * turned
    second_new = MOMENT_DECAY * second + (1.0 - MOMENT_DECAY) * turned * turned
    correction = 1.0 - MOMENT_DECAY**STEP
    direction = first_new / correction / (jnp.sqrt(second_new / correction) + ADAM_EPS)
    partback = jnp.einsum("...ij,...jk->...ik", left_turn, direction, precision=PRECISE)
    backward_step = jnp.einsum("...ik,...lk->...il", partback, right_turn, precision=PRECISE)
    weight_new = weight * (1.0 - LEARN_RATE * WEIGHT_DECAY) - LEARN_RATE * backward_step
    return (weight_new, first_new, second_new, left_new, right_new, left_turn, right_turn)


def adam_vector(gradient, weight, first, second):
    first_new = MOMENT_DECAY * first + (1.0 - MOMENT_DECAY) * gradient
    second_new = MOMENT_DECAY * second + (1.0 - MOMENT_DECAY) * gradient * gradient
    correction = 1.0 - MOMENT_DECAY**STEP
    weight_new = weight - VECTOR_RATE * (first_new / correction) / (
        jnp.sqrt(second_new / correction) + ADAM_EPS
    )
    return (weight_new, first_new, second_new)


def own_rows(values, index, chunk):
    early = lax.dynamic_slice_in_dim(values, index * chunk, chunk, 0)
    late = lax.dynamic_slice_in_dim(values, (3 - index) * chunk, chunk, 0)
    return jnp.concatenate([early, late], axis=0)


def in_order(mine, other, index, chunk):
    inner = jnp.where(index == 0, other, mine)
    outer = jnp.where(index == 0, mine, other)
    return jnp.concatenate([outer[:chunk], inner, outer[chunk:]], axis=0)


def key_bounds(key_ids, query_ids, chunk):
    edges = []
    for part in range(2):
        rows = query_ids[part * chunk : (part + 1) * chunk]
        lowest = jnp.sum((key_ids < rows[0]).astype(jnp.int32))
        highest = jnp.sum((key_ids <= rows[-1]).astype(jnp.int32))
        edges += [lowest // chunk, (highest + chunk - 1) // chunk]
    return edges


def per_device(
    decoder_input,
    encoder_states,
    decoder_segments,
    encoder_segments,
    output_cotangent,
    block_slots,
    master,
    first_moment,
    second_moment,
    row_statistics,
    column_statistics,
    row_basis,
    column_basis,
    vectors,
    vector_first,
    vector_second,
):
    core = lax.axis_index("tensor")
    cores = lax.axis_size("tensor")
    ring, rings = lax.axis_index("dp"), lax.axis_size("dp")
    swap = [(0, 1), (1, 0)]
    owned_count, block_height = master.shape[1], master.shape[2]
    vector_cols = vectors.shape[1]
    length, width = decoder_input.shape[1], decoder_input.shape[2]
    row_count = width // block_height
    block_total = block_slots.shape[0]
    column_count = block_total // row_count
    chunk = length // 4
    per_ring = owned_count * HD + VECTOR_ROWS
    group = block_height // vector_cols

    payload = low(master[0]).transpose(0, 2, 1).reshape(owned_count * HD, block_height)
    lane = jnp.arange(block_height) // vector_cols
    here = lane == ring % group
    small = jnp.where(here[None], jnp.tile(low(vectors), (1, group)), jnp.zeros((), BF16))
    small = jnp.pad(small, ((0, VECTOR_ROWS - vectors.shape[0]), (0, 0)))
    gathered = lax.all_gather(
        jnp.concatenate([payload, small], axis=0), ("dp", "tensor"), axis=0, tiled=True
    )
    slot_rows = block_slots % owned_count * HD
    w_self, w_cross, w_feed, vec = assemble(
        block_slots // owned_count * (cores * per_ring) + slot_rows,
        gathered,
        cores,
        per_ring,
        width,
        group,
    )

    tokens, encoder_rows = decoder_input[0], encoder_states[0]
    ids, encoder_ids = decoder_segments[0], encoder_segments[0]
    own_tokens = own_rows(tokens, core, chunk)
    own_ids = own_rows(ids, core, chunk)
    own_cotangent = own_rows(output_cotangent[0], core, chunk)
    places = jnp.arange(length, dtype=jnp.int32)
    own_places = own_rows(places, core, chunk)
    self_allowed = (ids[:, None] == own_ids[None, :]) & (places[:, None] <= own_places[None, :])
    self_bias = jnp.where(self_allowed, 0.0, NEGATIVE).astype(F32)
    cross_bias = jnp.where(encoder_ids[:, None] == own_ids[None, :], 0.0, NEGATIVE).astype(F32)
    self_edges = key_bounds(ids, own_ids, chunk)
    self_scalars = jnp.stack([self_edges[0], core + 1, self_edges[2], 4 - core, core])
    cross_scalars = jnp.stack(key_bounds(encoder_ids, own_ids, chunk) + [core])

    *self_saved, hat_one, inverse_one, y_one = call_forward(
        self_scalars, tokens, own_tokens, w_self, self_bias, vec, 0, "self_forward"
    )
    *cross_saved, hat_two, inverse_two, y_two = call_forward(
        cross_scalars, encoder_rows, y_one, w_cross, cross_bias, vec, 2, "cross_forward"
    )
    own_output, grad_two, ff_mine, ff_sent, norms_late = call_feed(
        self_scalars, y_two, w_feed, vec, own_cotangent, hat_two, inverse_two
    )
    cross_mine, cross_sent, part_encoder, grad_one, norms_early = call_backward(
        cross_scalars,
        encoder_rows,
        y_one,
        w_cross,
        cross_bias,
        vec,
        grad_two,
        cross_saved,
        [hat_one, inverse_one],
        0,
        "cross_backward",
    )
    self_mine, self_sent, part_input = call_backward(
        self_scalars,
        tokens,
        own_tokens,
        w_self,
        self_bias,
        vec,
        grad_one,
        self_saved,
        [],
        None,
        "self_backward",
    )
    norms = jnp.concatenate(
        [norms_early, norms_late, jnp.zeros((VECTOR_ROWS - 6, width), F32)], axis=0
    )

    ff_in, half_output = lax.ppermute((ff_sent, own_output), "tensor", swap)
    cross_in, half_encoder, norms_in = lax.ppermute(
        (cross_sent, part_encoder, norms), "tensor", swap
    )
    self_in, half_input = lax.ppermute((self_sent, part_input), "tensor", swap)
    block_output = in_order(own_output, half_output, core, chunk)
    input_gradient = part_input.astype(F32) + half_input.astype(F32)
    encoder_gradient = part_encoder.astype(F32) + half_encoder.astype(F32)

    terms = scatter(
        block_slots // owned_count * per_ring + slot_rows,
        (ff_mine, ff_in, cross_mine, cross_in, self_mine, self_in, norms, norms_in),
        cores,
        rings,
        per_ring,
        block_height,
        group,
    )
    summed = lax.psum_scatter(terms, "dp", scatter_dimension=0, tiled=True).astype(F32)
    owned = summed[: owned_count * HD].reshape(owned_count, HD, block_height).transpose(0, 2, 1)
    vector_owned = jnp.sum(
        jnp.where(here[None], summed[owned_count * HD : owned_count * HD + 6], 0.0).reshape(
            6, group, vector_cols
        ),
        axis=1,
    )

    updated = soap_step(
        owned,
        master[0],
        first_moment[0],
        second_moment[0],
        row_statistics[0],
        column_statistics[0],
        row_basis[0],
        column_basis[0],
    )
    vector_new = adam_vector(vector_owned, vectors, vector_first, vector_second)
    return (
        block_output[None],
        input_gradient[None],
        encoder_gradient[None],
        updated[0][None],
        updated[1][None],
        updated[2][None],
        updated[3][None],
        updated[4][None],
        updated[5][None],
        updated[6][None],
        vector_new[0],
        vector_new[1],
        vector_new[2],
    )


def solution(mesh):
    blocks = P("tensor", "dp", None, None)
    rows = P("dp", None, None)
    return jax.shard_map(
        per_device,
        mesh=mesh,
        in_specs=(rows, rows, P("dp", None), P("dp", None), rows, P())
        + (blocks,) * 7
        + (P(None, "dp"),) * 3,
        out_specs=(rows,) * 3 + (blocks,) * 7 + (P(None, "dp"),) * 3,
        check_vma=False,
    )
```

```python
import functools

import jax
import jax.numpy as jnp
from jax import lax
from jax.experimental import pallas as pl
from jax.experimental.pallas import tpu as pltpu
from jax.sharding import PartitionSpec as P

HD = 64
FF = 2048
STEP = 10

NEGATIVE = -1e30
EPS_NORM = 1e-05
MOMENT_DECAY = 0.5
LEARN_RATE = 0.04
WEIGHT_DECAY = 0.01
VECTOR_RATE = 0.25
ADAM_EPS = 1e-08
NEWTON_TURNS = 8
VECTOR_ROWS = 16
MIB = 2**20
F32 = jnp.float32
BF16 = jnp.bfloat16
VMEM = pl.BlockSpec(memory_space=pltpu.VMEM)
SMEM = pl.BlockSpec(memory_space=pltpu.SMEM)


def nn(left, right):
    return lax.dot_general(left, right, (((1,), (0,)), ((), ())), preferred_element_type=F32)


def nt(left, right):
    return lax.dot_general(left, right, (((1,), (1,)), ((), ())), preferred_element_type=F32)


def tn(left, right):
    return lax.dot_general(left, right, (((0,), (0,)), ((), ())), preferred_element_type=F32)


def low(values):
    return values.astype(BF16)


def span(number, size):
    return slice(number * size, (number + 1) * size)


def rows_at(number, size):
    return pl.ds(pl.multiple_of(number * size, size), size)


def shape(*dims, dtype=F32):
    return jax.ShapeDtypeStruct(dims, dtype)


def limit(mib):
    return pltpu.CompilerParams(vmem_limit_bytes=mib * MIB)


def block_places(columns, cores):
    hidden = FF // cores // HD
    heads = (columns - 2 * hidden) // 8
    places = []
    for column in range(columns):
        if column < 8 * heads:
            places.append((column // heads, column % heads * HD))
        else:
            column -= 8 * heads
            places.append((8 + column // hidden, column % hidden * HD))
    return places, heads * HD, hidden * HD


def assemble_kernel(rows_ref, gathered_ref, self_ref, cross_ref, feed_ref, vec_ref,
                    *, cores, per_core, group):
    height = gathered_ref.shape[1]
    row_count = self_ref.shape[1] // height
    columns = rows_ref.shape[0] // row_count
    places, head_rows, hidden_rows = block_places(columns, cores)
    for core in range(cores):
        for row in range(row_count):
            for column in range(columns):
                kind, inner = places[column]
                size = head_rows if kind < 8 else hidden_rows
                w_ref = self_ref if kind < 4 else cross_ref if kind < 8 else feed_ref
                target = (kind % 4 * cores + core) * size + inner
                source = pl.multiple_of(rows_ref[row * columns + column] + core * per_core, 16)
                w_ref[target : target + HD, span(row, height)] = gathered_ref[pl.ds(source, HD), :]
    rings = gathered_ref.shape[0] // per_core // cores
    for part in range(row_count):
        total = jnp.zeros((VECTOR_ROWS, height), F32)
        for ring in range(part * group, (part + 1) * group):
            if ring < rings:
                end = (ring * cores + 1) * per_core
                total = total + gathered_ref[end - VECTOR_ROWS : end, :].astype(F32)
        vec_ref[:, span(part, height)] = total


def assemble(rows, gathered, cores, per_core, width, group):
    return pl.pallas_call(
        functools.partial(assemble_kernel, cores=cores, per_core=per_core, group=group),
        out_shape=(
            shape(4 * width, width, dtype=BF16),
            shape(4 * width, width, dtype=BF16),
            shape(2 * FF, width, dtype=BF16),
            shape(VECTOR_ROWS, width),
        ),
        in_specs=[SMEM, VMEM],
        out_specs=[VMEM] * 4,
        compiler_params=limit(32),
        name="assemble",
    )(rows, gathered)


def scatter_kernel(rows_ref, ff_ref, ff_in_ref, cross_ref, cross_in_ref, self_ref, self_in_ref,
                   vec_ref, vec_in_ref, out_ref, *, cores, per_ring, group):
    height = out_ref.shape[1]
    row_count = self_ref.shape[1] // height
    columns = rows_ref.shape[0] // row_count
    places, head_rows, hidden_rows = block_places(columns, cores)
    for row in range(row_count):
        lanes = span(row, height)
        for column in range(columns):
            kind, inner = places[column]
            if kind < 4:
                one, two, start = self_ref, self_in_ref, kind * head_rows
            elif kind < 8:
                one, two, start = cross_ref, cross_in_ref, (kind - 4) * head_rows
            else:
                one, two, start = ff_ref, ff_in_ref, (kind - 8) * hidden_rows
            source = slice(start + inner, start + inner + HD)
            target = pl.multiple_of(rows_ref[row * columns + column], 16)
            total = one[source, lanes].astype(F32) + two[source, lanes].astype(F32)
            out_ref[pl.ds(target, HD), :] = low(total)
    total = low(vec_ref[...] + vec_in_ref[...])
    for ring in range(out_ref.shape[0] // per_ring):
        end = (ring + 1) * per_ring
        out_ref[end - VECTOR_ROWS : end, :] = total[:, span(ring // group, height)]


def scatter(rows, terms, cores, rings, per_ring, height, group):
    return pl.pallas_call(
        functools.partial(scatter_kernel, cores=cores, per_ring=per_ring, group=group),
        out_shape=shape(rings * per_ring, height, dtype=BF16),
        in_specs=[SMEM] + [VMEM] * 8,
        out_specs=VMEM,
        compiler_params=limit(32),
        name="scatter",
    )(rows, *terms)


def norm_forward(total_ref, vec_ref, first, hat_ref, inverse_ref, out_ref, step=64):
    gain, shift = vec_ref[first : first + 1], vec_ref[first + 1 : first + 2]

    def body(number, carry):
        rows = rows_at(number, step)
        values = total_ref[rows]
        center = values - jnp.mean(values, axis=1, keepdims=True)
        inverse = lax.rsqrt(jnp.mean(center * center, axis=1, keepdims=True) + EPS_NORM)
        hat = center * inverse
        hat_ref[rows] = hat
        inverse_ref[rows] = inverse
        out_ref[rows] = (hat * gain + shift).astype(out_ref.dtype)
        return carry

    lax.fori_loop(0, total_ref.shape[0] // step, body, 0)


def norm_backward(grad_ref, hat_ref, inverse_ref, gain, out_ref, step=64):
    width = grad_ref.shape[1]

    def body(number, carry):
        rows = rows_at(number, step)
        grad, hat = grad_ref[rows].astype(F32), hat_ref[rows]
        scaled = grad * gain
        middle = jnp.mean(scaled, axis=1, keepdims=True)
        slope = jnp.mean(scaled * hat, axis=1, keepdims=True)
        out_ref[rows] = (scaled - middle - hat * slope) * inverse_ref[rows]
        return (
            carry[0] + jnp.sum((grad * hat).reshape(step // 8, 8, width), axis=0),
            carry[1] + jnp.sum(grad.reshape(step // 8, 8, width), axis=0),
        )

    zeros = jnp.zeros((8, width), F32)
    sums = lax.fori_loop(0, grad_ref.shape[0] // step, body, (zeros, zeros))
    return [jnp.sum(one, axis=0, keepdims=True) for one in sums]


def split_heads(source_ref, masked_ref, factor):
    for head in range(masked_ref.shape[0]):
        pair = source_ref[:, span(head // 2, 2 * HD)]
        lane = lax.broadcasted_iota(jnp.int32, pair.shape, 1)
        here = (lane >= HD) if head % 2 else (lane < HD)
        masked_ref[head] = jnp.where(here, pair, jnp.zeros_like(pair)) * jnp.asarray(factor, BF16)


def staged(count, early, middle, late, ahead=2, lag=2):
    ready = [early(number) for number in range(min(ahead, count))]
    held = []
    for number in range(count):
        now = ready.pop(0)
        if number + ahead < count:
            ready.append(early(number + ahead))
        held.append((number, middle(number, now)))
        if len(held) > lag:
            late(*held.pop(0))
    while held:
        late(*held.pop(0))


def attend_forward(bounds_ref, bias_ref, masked_q, k_ref, vt_ref, m_ref, l_ref, acc_ref, lse_ref,
                   ctxt_ref):
    heads, chunk = m_ref.shape
    for part in range(lse_ref.shape[1] // chunk):
        cols = span(part, chunk)
        m_ref[...] = jnp.full(m_ref.shape, NEGATIVE, F32)
        l_ref[...] = jnp.zeros(l_ref.shape, F32)
        acc_ref[...] = jnp.zeros(acc_ref.shape, F32)

        def body(number, carry):
            keys = rows_at(number, chunk)
            bias = bias_ref[keys, cols]

            def early(head):
                return nt(k_ref[keys, span(head // 2, 2 * HD)], masked_q[head, cols]) + bias

            def middle(head, scores):
                row = slice(head, head + 1)
                before = m_ref[row]
                highest = jnp.maximum(before, jnp.max(scores, axis=0, keepdims=True))
                shrink = jnp.exp(before - highest)
                expons = jnp.exp(scores - highest)
                l_ref[row] = l_ref[row] * shrink + jnp.sum(expons, axis=0, keepdims=True)
                m_ref[row] = highest
                return shrink, low(expons)

            def late(head, pair):
                rows = span(head, HD)
                acc_ref[rows] = acc_ref[rows] * pair[0] + nn(vt_ref[rows, keys], pair[1])

            staged(heads, early, middle, late)
            return carry

        lax.fori_loop(bounds_ref[2 * part], bounds_ref[2 * part + 1], body, 0)
        for head in range(heads):
            rows = span(head, HD)
            ctxt_ref[rows, cols] = low(acc_ref[rows] / l_ref[head : head + 1])
        lse_ref[:, cols] = m_ref[...] + jnp.log(l_ref[...])


def forward_kernel(bounds_ref, x_ref, own_ref, w_ref, bias_ref, vec_ref,
                   q_ref, k_ref, lse_ref, ctxt_ref, hat_ref, inverse_ref, y_ref,
                   masked_q, vt_ref, m_ref, l_ref, acc_ref, *, first):
    width = w_ref.shape[1]
    chunk = m_ref.shape[1]
    q_ref[...] = low(nt(low(own_ref[...]), w_ref[span(0, width)]))
    split_heads(q_ref, masked_q, HD**-0.5)
    for part in range(k_ref.shape[0] // chunk):
        rows = span(part, chunk)
        k_ref[rows] = low(nt(x_ref[rows], w_ref[span(1, width)]))
        vt_ref[:, rows] = low(nt(w_ref[span(2, width)], x_ref[rows]))
    attend_forward(
        bounds_ref, bias_ref, masked_q, k_ref, vt_ref, m_ref, l_ref, acc_ref, lse_ref, ctxt_ref
    )
    y_ref[...] = own_ref[...].astype(F32) + tn(ctxt_ref[...], w_ref[span(3, width)])
    norm_forward(y_ref, vec_ref, first, hat_ref, inverse_ref, y_ref)


def call_forward(bounds, x, own, weights, bias, vec, first, name):
    keys, queries = bias.shape
    width = weights.shape[1]
    heads, chunk = width // HD, keys // 4
    return pl.pallas_call(
        functools.partial(forward_kernel, first=first),
        out_shape=(
            shape(queries, width, dtype=BF16),
            shape(keys, width, dtype=BF16),
            shape(heads, queries),
            shape(width, queries, dtype=BF16),
            shape(queries, width),
            shape(queries, 1),
            shape(queries, width),
        ),
        in_specs=[SMEM, VMEM, VMEM, VMEM, VMEM, VMEM],
        out_specs=[VMEM] * 7,
        scratch_shapes=[
            pltpu.VMEM((heads, queries, 2 * HD), BF16),
            pltpu.VMEM((width, keys), BF16),
            pltpu.VMEM((heads, chunk), F32),
            pltpu.VMEM((heads, chunk), F32),
            pltpu.VMEM((width, chunk), F32),
        ],
        compiler_params=limit(48),
        name=name,
    )(bounds, x, own, weights, bias, vec)


def backward_kernel(scalars_ref, x_ref, own_ref, w_ref, bias_ref, vec_ref, grad_ref, q_ref, k_ref,
                    lse_ref, ctxt_ref, *rest, first):
    if first is not None:
        hat_ref, inverse_ref, *rest = rest
        mine_ref, sent_ref, part_ref, next_ref, norms_ref, *rest = rest
    else:
        mine_ref, sent_ref, part_ref, *rest = rest
        next_ref = None
    masked_q, masked_g, v_ref, kt_ref, delta_ref, dqt_ref, dk_ref, dv_ref, dq_ref, out_ref = rest
    heads, queries = lse_ref.shape
    width = w_ref.shape[1]
    chunk = queries // 2
    core = scalars_ref[4]
    half = width // 2

    def keep(kind, gradient):
        out_ref[...] = low(gradient)
        mine_ref[span(kind, half)] = out_ref[rows_at(core, half)]
        sent_ref[span(kind, half)] = out_ref[rows_at(1 - core, half)]

    queries_low = low(own_ref[...])
    grad_low = low(grad_ref[...])
    w_out = w_ref[span(3, width)]
    keep(3, nn(ctxt_ref[...], grad_low))
    out_ref[...] = low(nt(grad_low, w_out))
    split_heads(out_ref, masked_g, 1.0)
    split_heads(q_ref, masked_q, HD**-0.5)
    grad_t = low(nt(w_out, grad_low)).astype(F32) * ctxt_ref[...].astype(F32)
    for head in range(heads):
        delta_ref[head : head + 1] = jnp.sum(grad_t[span(head, HD)], axis=0, keepdims=True)
    for part in range(k_ref.shape[0] // chunk):
        rows = span(part, chunk)
        v_ref[rows] = low(nt(x_ref[rows], w_ref[span(2, width)]))
        kt_ref[:, rows] = low(nt(w_ref[span(1, width)], x_ref[rows]))
    dqt_ref[...] = jnp.zeros(dqt_ref.shape, F32)
    dk_ref[...] = jnp.zeros(dk_ref.shape, F32)
    dv_ref[...] = jnp.zeros(dv_ref.shape, F32)
    for part in range(2):
        cols = span(part, chunk)

        def body(number, carry):
            keys = rows_at(number, chunk)
            bias = bias_ref[keys, cols]

            def early(head):
                pair = span(head // 2, 2 * HD)
                return (
                    nt(k_ref[keys, pair], masked_q[head, cols]) + bias,
                    nt(v_ref[keys, pair], masked_g[head, cols]),
                )

            def middle(head, both):
                row = slice(head, head + 1)
                chances = jnp.exp(both[0] - lse_ref[row, cols])
                return low(chances), low(chances * (both[1] - delta_ref[row, cols]))

            def late(head, both):
                pair, rows = span(head // 2, 2 * HD), span(head, HD)
                dv_ref[keys, pair] += nn(both[0], masked_g[head, cols])
                dk_ref[keys, pair] += nn(both[1], masked_q[head, cols])
                dqt_ref[rows, cols] += nn(kt_ref[rows, keys], both[1])

            staged(heads, early, middle, late)
            return carry

        lax.fori_loop(scalars_ref[2 * part], scalars_ref[2 * part + 1], body, 0)
    dqt = low(dqt_ref[...] * HD**-0.5)
    keep(0, nn(dqt, queries_low))
    dk, dv = low(dk_ref[...]), low(dv_ref[...])
    keep(1, tn(dk, x_ref[...]))
    keep(2, tn(dv, x_ref[...]))
    dq_ref[...] = grad_ref[...] + tn(dqt, w_ref[span(0, width)])
    if first is not None:
        part_ref[...] = low(nn(dk, w_ref[span(1, width)]) + nn(dv, w_ref[span(2, width)]))
        sums = norm_backward(dq_ref, hat_ref, inverse_ref, vec_ref[first : first + 1], next_ref)
        norms_ref[0:1] = sums[0]
        norms_ref[1:2] = sums[1]
    else:
        dk_ref[...] = nn(dk, w_ref[span(1, width)]) + nn(dv, w_ref[span(2, width)])
        for part, place in enumerate((core, 3 - core)):
            dk_ref[rows_at(place, chunk)] += dq_ref[span(part, chunk)]
        part_ref[...] = low(dk_ref[...])


def call_backward(scalars, x, own, weights, bias, vec, grad, saved, norm, first, name):
    keys, queries = bias.shape
    width = weights.shape[1]
    heads = width // HD
    outs = [
        shape(2 * width, width, dtype=BF16),
        shape(2 * width, width, dtype=BF16),
        shape(keys, width, dtype=BF16),
    ]
    if first is not None:
        outs += [shape(queries, width), shape(2, width)]
    return pl.pallas_call(
        functools.partial(backward_kernel, first=first),
        out_shape=outs,
        in_specs=[SMEM, VMEM, VMEM, VMEM]
        + [VMEM] * (3 + len(saved) + len(norm)),
        out_specs=[VMEM] * len(outs),
        scratch_shapes=[
            pltpu.VMEM((heads, queries, 2 * HD), BF16),
            pltpu.VMEM((heads, queries, 2 * HD), BF16),
            pltpu.VMEM((keys, width), BF16),
            pltpu.VMEM((width, keys), BF16),
            pltpu.VMEM((heads, queries), F32),
            pltpu.VMEM((width, queries), F32),
            pltpu.VMEM((keys, width), F32),
            pltpu.VMEM((keys, width), F32),
            pltpu.VMEM((queries, width), F32),
            pltpu.VMEM((width, width), BF16),
        ],
        compiler_params=limit(48),
        name=name,
    )(scalars, x, own, weights, bias, vec, grad, *saved, *norm)


def gelu_both(values):
    scale = (2.0 / jnp.pi) ** 0.5
    square = values * values
    bend = jnp.tanh(values * (scale + scale * 0.044715 * square))
    half = 0.5 + 0.5 * bend
    slope = half + (0.5 * values) * (1.0 - bend * bend) * (scale + 3.0 * scale * 0.044715 * square)
    return values * half, slope


def feed_kernel(core_ref, y_ref, w_ref, vec_ref, cot_ref, hat_two, inverse_two,
                block_ref, next_ref, mine_ref, sent_ref, norms_ref,
                low_ref, hid_ref, slope_ref, total_ref, hat_ref, inverse_ref, grad_low,
                *, step):
    core = core_ref[4]
    hidden = w_ref.shape[0] // 2
    half = hidden // 2
    chunks = hidden // step
    low_ref[...] = low(y_ref[...])
    total_ref[...] = y_ref[...]

    def early(number):
        return nt(w_ref[span(number, step)], low_ref[...])

    def middle(number, up):
        hid, slope = gelu_both(up)
        hid_ref[span(number, step)] = low(hid)
        slope_ref[span(number, step)] = slope

    def late(number, _):
        lower = w_ref[hidden + number * step : hidden + (number + 1) * step]
        total_ref[...] += tn(hid_ref[span(number, step)], lower)

    staged(chunks, early, middle, late, 1, 1)
    norm_forward(total_ref, vec_ref, 4, hat_ref, inverse_ref, block_ref)
    sums = norm_backward(cot_ref, hat_ref, inverse_ref, vec_ref[4:5], total_ref)
    norms_ref[2:3] = sums[0]
    norms_ref[3:4] = sums[1]
    grad_low[...] = low(total_ref[...])

    def place(number):
        inner = number % (chunks // 2)
        row = (core if number < chunks // 2 else 1 - core) * half + inner * step
        return inner, pl.multiple_of(row, step)

    def down(number):
        row = place(number)[1]
        return nt(w_ref[pl.ds(pl.multiple_of(hidden + row, step), step)], grad_low[...])

    def turn(number, grad_hidden):
        return low(slope_ref[pl.ds(place(number)[1], step)] * grad_hidden)

    def sums_of(number, grad_up):
        inner, row = place(number)
        rows = pl.ds(row, step)
        kept = mine_ref if number < chunks // 2 else sent_ref
        kept[span(inner, step)] = low(nn(grad_up, low_ref[...]))
        kept[half + inner * step : half + (inner + 1) * step] = low(nn(hid_ref[rows], grad_low[...]))
        total_ref[...] += tn(grad_up, w_ref[rows])

    staged(chunks, down, turn, sums_of, 1, 1)
    sums = norm_backward(total_ref, hat_two, inverse_two, vec_ref[2:3], next_ref)
    norms_ref[0:1] = sums[0]
    norms_ref[1:2] = sums[1]


def call_feed(scalars, y, weights, vec, cotangent, hat, inverse):
    queries, width = y.shape
    hidden = FF
    return pl.pallas_call(
        functools.partial(feed_kernel, step=256),
        out_shape=(
            shape(queries, width, dtype=BF16),
            shape(queries, width),
            shape(hidden, width, dtype=BF16),
            shape(hidden, width, dtype=BF16),
            shape(4, width),
        ),
        in_specs=[SMEM, VMEM, VMEM] + [VMEM] * 4,
        out_specs=[VMEM] * 5,
        scratch_shapes=[
            pltpu.VMEM((queries, width), BF16),
            pltpu.VMEM((hidden, queries), BF16),
            pltpu.VMEM((hidden, queries), F32),
            pltpu.VMEM((queries, width), F32),
            pltpu.VMEM((queries, width), F32),
            pltpu.VMEM((queries, 1), F32),
            pltpu.VMEM((queries, width), BF16),
        ],
        compiler_params=limit(48),
        name="feed",
    )(scalars, y, weights, vec, cotangent, hat, inverse)


def halves(values):
    high = low(values)
    return high, low(values - high.astype(F32))


def fine(dot, left, right):
    left_high, left_low = halves(left)
    right_high, right_low = halves(right)
    return dot(left_high, right_high) + (dot(left_high, right_low) + dot(left_low, right_high))


def newton_turn(x_ref, s_ref, z_ref):
    count, size = x_ref.shape[0], x_ref.shape[1]
    for number in range(count):
        high, rest = halves(x_ref[number])
        z_ref[number] = jnp.concatenate([high, rest], axis=1)
        right = jnp.concatenate(
            [jnp.concatenate([high, high], axis=1), jnp.concatenate([rest, rest], axis=1)], axis=0
        )
        product = nt(z_ref[number], right)
        high, rest = halves(product[:, :size] + product[:, size:])
        s_ref[number] = jnp.concatenate([high, rest], axis=1)
    for number in range(count):
        terms = z_ref[number]
        product = nn(s_ref[number], jnp.concatenate([terms, terms], axis=0))
        x_ref[number] = 1.5 * x_ref[number] - 0.5 * (product[:, :size] + product[:, size:])


def adam_terms(gradient, first, second):
    first_new = MOMENT_DECAY * first + (1.0 - MOMENT_DECAY) * gradient
    second_new = MOMENT_DECAY * second + (1.0 - MOMENT_DECAY) * gradient * gradient
    correction = 1.0 - MOMENT_DECAY**STEP
    direction = first_new / correction / (jnp.sqrt(second_new / correction) + ADAM_EPS)
    return first_new, second_new, direction


def optimizer_kernel(shift_ref, grad_ref, master_ref, first_ref, second_ref, left_ref, right_ref,
                     left_basis, right_basis, vec_ref, vec_first, vec_second,
                     new_master, new_first, new_second, new_left, new_right, new_left_basis,
                     new_right_basis, new_vec, new_vec_first, new_vec_second,
                     x_ref, s_ref, z_ref, p_ref):
    count, height, side = master_ref.shape
    keep = MOMENT_DECAY

    def unit(matrix):
        total = jnp.sum(jnp.sum(matrix * matrix, axis=1, keepdims=True), axis=0, keepdims=True)
        return matrix * lax.rsqrt(total + 1e-06)

    for pair in range(count // 2):
        x_ref[count + pair] = jnp.zeros((height, height), F32)
    for block in range(count):
        gradient = grad_ref[span(block, side)]
        new_left[block] = keep * left_ref[block] + (1.0 - keep) * tn(gradient, gradient)
        new_right[block] = keep * right_ref[block] + (1.0 - keep) * nt(gradient, gradient)
    for block in range(count):
        x_ref[block] = unit(fine(nn, new_left[block], left_basis[block]))
        corner = span(block % 2, side)
        x_ref[count + block // 2, corner, corner] = unit(
            fine(nn, new_right[block], right_basis[block])
        )

    def turn(number, carry):
        newton_turn(x_ref, s_ref, z_ref)
        return carry

    lax.fori_loop(0, NEWTON_TURNS, turn, 0)
    for block in range(count):
        corner = span(block % 2, side)
        new_left_basis[block] = x_ref[block]
        new_right_basis[block] = x_ref[count + block // 2, corner, corner]
    for block in range(count):
        high, rest = halves(new_left_basis[block])
        gradient = grad_ref[span(block, side)]
        partway = nn(gradient, high) + nn(gradient, rest)
        turned = fine(tn, partway, new_right_basis[block])
        new_first[block], new_second[block], p_ref[block] = adam_terms(
            turned, first_ref[block], second_ref[block]
        )
    for block in range(count):
        partback = fine(nn, new_left_basis[block], p_ref[block])
        step = fine(nt, partback, new_right_basis[block])
        new_master[block] = (
            master_ref[block] * (1.0 - LEARN_RATE * WEIGHT_DECAY) - LEARN_RATE * step
        )
    rows, columns = vec_ref.shape
    tail = grad_ref[count * side :].astype(F32)
    tail = pltpu.roll(tail, shift_ref[0], 1)
    new_vec_first[...], new_vec_second[...], direction = adam_terms(
        tail[:rows, :columns], vec_first[...], vec_second[...]
    )
    new_vec[...] = vec_ref[...] - VECTOR_RATE * direction


def optimize(shift, summed, arrays):
    count, height, side = arrays[0].shape
    matrices = count + count // 2
    return pl.pallas_call(
        optimizer_kernel,
        out_shape=[shape(*one.shape) for one in arrays],
        in_specs=[SMEM] + [VMEM] * (1 + len(arrays)),
        out_specs=[VMEM] * len(arrays),
        scratch_shapes=[
            pltpu.VMEM((matrices, height, height), F32),
            pltpu.VMEM((matrices, height, 2 * height), BF16),
            pltpu.VMEM((matrices, height, 2 * height), BF16),
            pltpu.VMEM((count, height, side), F32),
        ],
        compiler_params=limit(40),
        name="optimizer",
    )(shift, summed, *arrays)


def own_rows(values, index, chunk):
    early = lax.dynamic_slice_in_dim(values, index * chunk, chunk, 0)
    late = lax.dynamic_slice_in_dim(values, (3 - index) * chunk, chunk, 0)
    return jnp.concatenate([early, late], axis=0)


def in_order(mine, other, index, chunk):
    inner = jnp.where(index == 0, other, mine)
    outer = jnp.where(index == 0, mine, other)
    return jnp.concatenate([outer[:chunk], inner, outer[chunk:]], axis=0)


def key_bounds(key_ids, query_ids, chunk):
    edges = []
    for part in range(2):
        rows = query_ids[part * chunk : (part + 1) * chunk]
        lowest = jnp.sum((key_ids < rows[0]).astype(jnp.int32))
        highest = jnp.sum((key_ids <= rows[-1]).astype(jnp.int32))
        edges += [lowest // chunk, (highest + chunk - 1) // chunk]
    return edges


def per_device(
    decoder_input,
    encoder_states,
    decoder_segments,
    encoder_segments,
    output_cotangent,
    block_slots,
    master,
    first_moment,
    second_moment,
    row_statistics,
    column_statistics,
    row_basis,
    column_basis,
    vectors,
    vector_first,
    vector_second,
):
    core = lax.axis_index("tensor")
    cores = lax.axis_size("tensor")
    ring, rings = lax.axis_index("dp"), lax.axis_size("dp")
    swap = [(0, 1), (1, 0)]
    owned_count, block_height = master.shape[1], master.shape[2]
    vector_cols = vectors.shape[1]
    length, width = decoder_input.shape[1], decoder_input.shape[2]
    row_count = width // block_height
    block_total = block_slots.shape[0]
    column_count = block_total // row_count
    chunk = length // 4
    per_ring = owned_count * HD + VECTOR_ROWS
    group = block_height // vector_cols

    payload = low(master[0]).transpose(0, 2, 1).reshape(owned_count * HD, block_height)
    lane = jnp.arange(block_height) // vector_cols
    here = lane == ring % group
    small = jnp.where(here[None], jnp.tile(low(vectors), (1, group)), jnp.zeros((), BF16))
    small = jnp.pad(small, ((0, VECTOR_ROWS - vectors.shape[0]), (0, 0)))
    gathered = lax.all_gather(
        jnp.concatenate([payload, small], axis=0), ("dp", "tensor"), axis=0, tiled=True
    )
    slot_rows = block_slots % owned_count * HD
    w_self, w_cross, w_feed, vec = assemble(
        block_slots // owned_count * (cores * per_ring) + slot_rows,
        gathered,
        cores,
        per_ring,
        width,
        group,
    )

    tokens, encoder_rows = decoder_input[0], encoder_states[0]
    ids, encoder_ids = decoder_segments[0], encoder_segments[0]
    own_tokens = own_rows(tokens, core, chunk)
    own_ids = own_rows(ids, core, chunk)
    own_cotangent = own_rows(output_cotangent[0], core, chunk)
    places = jnp.arange(length, dtype=jnp.int32)
    own_places = own_rows(places, core, chunk)
    self_allowed = (ids[:, None] == own_ids[None, :]) & (places[:, None] <= own_places[None, :])
    self_bias = jnp.where(self_allowed, 0.0, NEGATIVE).astype(F32)
    cross_bias = jnp.where(encoder_ids[:, None] == own_ids[None, :], 0.0, NEGATIVE).astype(F32)
    self_edges = key_bounds(ids, own_ids, chunk)
    self_scalars = jnp.stack([self_edges[0], core + 1, self_edges[2], 4 - core, core])
    cross_scalars = jnp.stack(key_bounds(encoder_ids, own_ids, chunk) + [core])

    *self_saved, hat_one, inverse_one, y_one = call_forward(
        self_scalars, tokens, own_tokens, w_self, self_bias, vec, 0, "self_forward"
    )
    *cross_saved, hat_two, inverse_two, y_two = call_forward(
        cross_scalars, encoder_rows, y_one, w_cross, cross_bias, vec, 2, "cross_forward"
    )
    own_output, grad_two, ff_mine, ff_sent, norms_late = call_feed(
        self_scalars, y_two, w_feed, vec, own_cotangent, hat_two, inverse_two
    )
    cross_mine, cross_sent, part_encoder, grad_one, norms_early = call_backward(
        cross_scalars,
        encoder_rows,
        y_one,
        w_cross,
        cross_bias,
        vec,
        grad_two,
        cross_saved,
        [hat_one, inverse_one],
        0,
        "cross_backward",
    )
    self_mine, self_sent, part_input = call_backward(
        self_scalars,
        tokens,
        own_tokens,
        w_self,
        self_bias,
        vec,
        grad_one,
        self_saved,
        [],
        None,
        "self_backward",
    )
    norms = jnp.concatenate(
        [norms_early, norms_late, jnp.zeros((VECTOR_ROWS - 6, width), F32)], axis=0
    )

    ff_in, half_output = lax.ppermute((ff_sent, own_output), "tensor", swap)
    cross_in, half_encoder, norms_in = lax.ppermute(
        (cross_sent, part_encoder, norms), "tensor", swap
    )
    self_in, half_input = lax.ppermute((self_sent, part_input), "tensor", swap)
    block_output = in_order(own_output, half_output, core, chunk)
    input_gradient = part_input.astype(F32) + half_input.astype(F32)
    encoder_gradient = part_encoder.astype(F32) + half_encoder.astype(F32)

    terms = scatter(
        block_slots // owned_count * per_ring + slot_rows,
        (ff_mine, ff_in, cross_mine, cross_in, self_mine, self_in, norms, norms_in),
        cores,
        rings,
        per_ring,
        block_height,
        group,
    )
    summed = lax.psum_scatter(terms, "dp", scatter_dimension=0, tiled=True)
    shift = (block_height - ring % group * vector_cols) % block_height
    states = (first_moment, second_moment, row_statistics, column_statistics)
    arrays = [one[0] for one in (master, *states, row_basis, column_basis)]
    arrays += [vectors, vector_first, vector_second]
    updated = optimize(shift[None], summed, arrays)
    return (
        block_output[None],
        input_gradient[None],
        encoder_gradient[None],
        *[one[None] for one in updated[:7]],
        *updated[7:],
    )


def solution(mesh):
    blocks = P("tensor", "dp", None, None)
    rows = P("dp", None, None)
    return jax.shard_map(
        per_device,
        mesh=mesh,
        in_specs=(rows, rows, P("dp", None), P("dp", None), rows, P())
        + (blocks,) * 7
        + (P(None, "dp"),) * 3,
        out_specs=(rows,) * 3 + (blocks,) * 7 + (P(None, "dp"),) * 3,
        check_vma=False,
    )
```

```python
import functools

import jax
import jax.numpy as jnp
from jax import lax
from jax.experimental import pallas as pl
from jax.experimental.pallas import tpu as pltpu
from jax.sharding import PartitionSpec as P

HD = 64
FF = 2048
STEP = 10

NEGATIVE = -1e30
EPS_NORM = 1e-05
MOMENT_DECAY = 0.5
LEARN_RATE = 0.04
WEIGHT_DECAY = 0.01
VECTOR_RATE = 0.25
ADAM_EPS = 1e-08
NEWTON_TURNS = 8
VECTOR_ROWS = 16
DEPTH, SIDE = 4, 2
MIB = 2**20
F32 = jnp.float32
BF16 = jnp.bfloat16
VMEM = pl.BlockSpec(memory_space=pltpu.VMEM)
SMEM = pl.BlockSpec(memory_space=pltpu.SMEM)


def nn(left, right):
    return lax.dot_general(left, right, (((1,), (0,)), ((), ())), preferred_element_type=F32)


def nt(left, right):
    return lax.dot_general(left, right, (((1,), (1,)), ((), ())), preferred_element_type=F32)


def tn(left, right):
    return lax.dot_general(left, right, (((0,), (0,)), ((), ())), preferred_element_type=F32)


def low(values):
    return values.astype(BF16)


def span(number, size):
    return slice(number * size, (number + 1) * size)


def rows_at(number, size):
    return pl.ds(pl.multiple_of(number * size, size), size)


def shape(*dims, dtype=F32):
    return jax.ShapeDtypeStruct(dims, dtype)


def limit(mib):
    return pltpu.CompilerParams(vmem_limit_bytes=mib * MIB)


def block_places(columns, cores):
    hidden = FF // cores // HD
    heads = (columns - 2 * hidden) // 8
    places = []
    for column in range(columns):
        if column < 8 * heads:
            places.append((column // heads, column % heads * HD))
        else:
            column -= 8 * heads
            places.append((8 + column // hidden, column % hidden * HD))
    return places, heads * HD, hidden * HD


def fetch(pieces, target_ref, semaphores):
    copies, start = [], 0
    for number, piece in enumerate(pieces):
        rows = piece.shape[0]
        copies.append(
            pltpu.make_async_copy(piece, target_ref.at[pl.ds(start, rows)], semaphores.at[number])
        )
        start += rows
    for copy in copies:
        copy.start()
    for copy in copies:
        copy.wait()


def assemble_kernel(rows_ref, ends_ref, *refs, cores, group, pieces):
    self_ref, cross_ref, feed_ref, vec_ref, gathered_ref, semaphores = refs[pieces:]
    fetch(refs[:pieces], gathered_ref, semaphores)
    height = gathered_ref.shape[1]
    row_count = self_ref.shape[1] // height
    total = rows_ref.shape[0] // cores
    columns = total // row_count
    places, head_rows, hidden_rows = block_places(columns, cores)
    for core in range(cores):
        for row in range(row_count):
            for column in range(columns):
                kind, inner = places[column]
                size = head_rows if kind < 8 else hidden_rows
                w_ref = self_ref if kind < 4 else cross_ref if kind < 8 else feed_ref
                target = (kind % 4 * cores + core) * size + inner
                source = pl.multiple_of(rows_ref[core * total + row * columns + column], 16)
                w_ref[target : target + HD, span(row, height)] = gathered_ref[pl.ds(source, HD), :]
    rings = ends_ref.shape[0]
    for part in range(row_count):
        values = jnp.zeros((VECTOR_ROWS, height), F32)
        for ring in range(part * group, min((part + 1) * group, rings)):
            start = pl.multiple_of(ends_ref[ring], 16)
            values = values + gathered_ref[pl.ds(start, VECTOR_ROWS), :].astype(F32)
        vec_ref[:, span(part, height)] = values


def assemble(rows, ends, pieces, cores, width, group):
    total = sum(piece.shape[0] for piece in pieces)
    return pl.pallas_call(
        functools.partial(assemble_kernel, cores=cores, group=group, pieces=len(pieces)),
        out_shape=(
            shape(4 * width, width, dtype=BF16),
            shape(4 * width, width, dtype=BF16),
            shape(2 * FF, width, dtype=BF16),
            shape(VECTOR_ROWS, width),
        ),
        in_specs=[SMEM, SMEM] + [pl.BlockSpec(memory_space=pl.ANY)] * len(pieces),
        out_specs=[VMEM] * 4,
        scratch_shapes=[
            pltpu.VMEM((total, pieces[0].shape[1]), BF16),
            pltpu.SemaphoreType.DMA((len(pieces),)),
        ],
        compiler_params=limit(40),
        name="assemble",
    )(rows, ends, *pieces)


def scatter_kernel(rows_ref, ends_ref, ff_ref, ff_in_ref, cross_ref, cross_in_ref, self_ref,
                   self_in_ref, vec_ref, vec_in_ref, *refs, cores, group):
    *outs, all_ref, semaphores = refs
    height = all_ref.shape[1]
    row_count = self_ref.shape[1] // height
    columns = rows_ref.shape[0] // row_count
    places, head_rows, hidden_rows = block_places(columns, cores)
    for row in range(row_count):
        lanes = span(row, height)
        for column in range(columns):
            kind, inner = places[column]
            if kind < 4:
                one, two, start = self_ref, self_in_ref, kind * head_rows
            elif kind < 8:
                one, two, start = cross_ref, cross_in_ref, (kind - 4) * head_rows
            else:
                one, two, start = ff_ref, ff_in_ref, (kind - 8) * hidden_rows
            source = slice(start + inner, start + inner + HD)
            target = pl.multiple_of(rows_ref[row * columns + column], 16)
            total = one[source, lanes].astype(F32) + two[source, lanes].astype(F32)
            all_ref[pl.ds(target, HD), :] = low(total)
    total = low(vec_ref[...] + vec_in_ref[...])
    for ring in range(ends_ref.shape[0]):
        start = pl.multiple_of(ends_ref[ring], 16)
        all_ref[pl.ds(start, VECTOR_ROWS), :] = total[:, span(ring // group, height)]
    copies, start = [], 0
    for number, out in enumerate(outs):
        rows = out.shape[0]
        copies.append(
            pltpu.make_async_copy(all_ref.at[pl.ds(start, rows)], out, semaphores.at[number])
        )
        start += rows
    for copy in copies:
        copy.start()
    for copy in copies:
        copy.wait()


def scatter(rows, ends, terms, cuts, cores, height, group):
    return pl.pallas_call(
        functools.partial(scatter_kernel, cores=cores, group=group),
        out_shape=[shape(cut, height, dtype=BF16) for cut in cuts],
        in_specs=[SMEM, SMEM] + [VMEM] * 8,
        out_specs=[pl.BlockSpec(memory_space=pl.ANY)] * len(cuts),
        scratch_shapes=[
            pltpu.VMEM((sum(cuts), height), BF16),
            pltpu.SemaphoreType.DMA((len(cuts),)),
        ],
        compiler_params=limit(32),
        name="scatter",
    )(rows, ends, *terms)


def hop(values, axis, step):
    sizes = (DEPTH, SIDE, SIDE)
    pairs = []
    for source in range(DEPTH * SIDE * SIDE):
        place = [source // (SIDE * SIDE), source // SIDE % SIDE, source % SIDE]
        place[axis] = (place[axis] + step) % sizes[axis]
        pairs.append((source, (place[0] * SIDE + place[1]) * SIDE + place[2]))
    return lax.ppermute(values, "dp", pairs)


def swapped(values):
    return lax.ppermute(values, "tensor", [(0, 1), (1, 0)])


def apart(ring, other, sign):
    side = SIDE * SIDE
    deep = (sign * (ring // side - other // side)) % DEPTH
    across = (ring // SIDE % SIDE) ^ (other // SIDE % SIDE)
    return (across * SIDE + ((ring % SIDE) ^ (other % SIDE))) * DEPTH + deep


def gather_chips(own):
    deep = [hop(own, 0, step) for step in range(1, DEPTH)]
    near_x, near_y = hop(own, 2, 1), hop(own, 1, 1)
    near = [near_x, near_y, hop(near_y, 2, 1)]
    deep, near = lax.optimization_barrier((jnp.concatenate(deep, axis=0), near))
    by_x, by_y = hop(deep, 2, 1), hop(deep, 1, 1)
    cut = deep.shape[0] // 32 * 16
    return [own, deep, near[0], by_x, near[1], by_y, near[2]] + [
        hop(by_y[:cut], 2, 1),
        hop(by_x[cut:], 1, 1),
    ]


PLACES = (12, 13, 14, 15, 2, 3, 10, 11, 8, 9, 6, 7, 0, 1, 4, 5)


def fold(*terms):
    return low(functools.reduce(lambda one, two: one + two, [term.astype(F32) for term in terms]))


def reduce_plane(along_x, along_y, late_y, late_x, here):
    half = late_x.shape[0]
    from_x, from_y = hop(along_x, 2, 1), hop(along_y, 1, 1)
    more_y = hop(fold(late_y, from_x[:half]), 1, 1)
    more_x = hop(fold(late_x, from_y[:half]), 2, 1)
    return jnp.concatenate(
        [fold(here[:half], from_x[half:], more_y), fold(here[half:], from_y[half:], more_x)],
        axis=0,
    )


def reduce_column(column):
    rows = column.shape[0] // DEPTH
    return [column[:rows]] + [
        hop(column[step * rows : (step + 1) * rows], 0, step) for step in range(1, DEPTH)
    ]


def norm_forward(total_ref, vec_ref, first, hat_ref, inverse_ref, out_ref, step=64):
    gain, shift = vec_ref[first : first + 1], vec_ref[first + 1 : first + 2]

    def body(number, carry):
        rows = rows_at(number, step)
        values = total_ref[rows]
        center = values - jnp.mean(values, axis=1, keepdims=True)
        inverse = lax.rsqrt(jnp.mean(center * center, axis=1, keepdims=True) + EPS_NORM)
        hat = center * inverse
        hat_ref[rows] = hat
        inverse_ref[rows] = inverse
        out_ref[rows] = (hat * gain + shift).astype(out_ref.dtype)
        return carry

    lax.fori_loop(0, total_ref.shape[0] // step, body, 0)


def norm_backward(grad_ref, hat_ref, inverse_ref, gain, out_ref, step=64):
    width = grad_ref.shape[1]

    def body(number, carry):
        rows = rows_at(number, step)
        grad, hat = grad_ref[rows].astype(F32), hat_ref[rows]
        scaled = grad * gain
        middle = jnp.mean(scaled, axis=1, keepdims=True)
        slope = jnp.mean(scaled * hat, axis=1, keepdims=True)
        out_ref[rows] = (scaled - middle - hat * slope) * inverse_ref[rows]
        return (
            carry[0] + jnp.sum((grad * hat).reshape(step // 8, 8, width), axis=0),
            carry[1] + jnp.sum(grad.reshape(step // 8, 8, width), axis=0),
        )

    zeros = jnp.zeros((8, width), F32)
    sums = lax.fori_loop(0, grad_ref.shape[0] // step, body, (zeros, zeros))
    return [jnp.sum(one, axis=0, keepdims=True) for one in sums]


def split_heads(source_ref, masked_ref, factor):
    for head in range(masked_ref.shape[0]):
        pair = source_ref[:, span(head // 2, 2 * HD)]
        lane = lax.broadcasted_iota(jnp.int32, pair.shape, 1)
        here = (lane >= HD) if head % 2 else (lane < HD)
        masked_ref[head] = jnp.where(here, pair, jnp.zeros_like(pair)) * jnp.asarray(factor, BF16)


def staged(count, early, middle, late, ahead=2, lag=2):
    ready = [early(number) for number in range(min(ahead, count))]
    held = []
    for number in range(count):
        now = ready.pop(0)
        if number + ahead < count:
            ready.append(early(number + ahead))
        held.append((number, middle(number, now)))
        if len(held) > lag:
            late(*held.pop(0))
    while held:
        late(*held.pop(0))


def attend_forward(bounds_ref, bias_ref, masked_q, k_ref, vt_ref, m_ref, l_ref, acc_ref, lse_ref,
                   ctxt_ref):
    heads, chunk = m_ref.shape
    for part in range(lse_ref.shape[1] // chunk):
        cols = span(part, chunk)
        m_ref[...] = jnp.full(m_ref.shape, NEGATIVE, F32)
        l_ref[...] = jnp.zeros(l_ref.shape, F32)
        acc_ref[...] = jnp.zeros(acc_ref.shape, F32)

        def body(number, carry):
            keys = rows_at(number, chunk)
            bias = bias_ref[keys, cols]

            def early(head):
                return nt(k_ref[keys, span(head // 2, 2 * HD)], masked_q[head, cols]) + bias

            def middle(head, scores):
                row = slice(head, head + 1)
                before = m_ref[row]
                highest = jnp.maximum(before, jnp.max(scores, axis=0, keepdims=True))
                shrink = jnp.exp(before - highest)
                expons = jnp.exp(scores - highest)
                l_ref[row] = l_ref[row] * shrink + jnp.sum(expons, axis=0, keepdims=True)
                m_ref[row] = highest
                return shrink, low(expons)

            def late(head, pair):
                rows = span(head, HD)
                acc_ref[rows] = acc_ref[rows] * pair[0] + nn(vt_ref[rows, keys], pair[1])

            staged(heads, early, middle, late)
            return carry

        lax.fori_loop(bounds_ref[2 * part], bounds_ref[2 * part + 1], body, 0)
        for head in range(heads):
            rows = span(head, HD)
            ctxt_ref[rows, cols] = low(acc_ref[rows] / l_ref[head : head + 1])
        lse_ref[:, cols] = m_ref[...] + jnp.log(l_ref[...])


def forward_kernel(bounds_ref, x_ref, own_ref, w_ref, bias_ref, vec_ref,
                   q_ref, k_ref, lse_ref, ctxt_ref, hat_ref, inverse_ref, y_ref,
                   masked_q, vt_ref, m_ref, l_ref, acc_ref, *, first):
    width = w_ref.shape[1]
    chunk = m_ref.shape[1]
    q_ref[...] = low(nt(low(own_ref[...]), w_ref[span(0, width)]))
    split_heads(q_ref, masked_q, HD**-0.5)
    for part in range(k_ref.shape[0] // chunk):
        rows = span(part, chunk)
        k_ref[rows] = low(nt(x_ref[rows], w_ref[span(1, width)]))
        vt_ref[:, rows] = low(nt(w_ref[span(2, width)], x_ref[rows]))
    attend_forward(
        bounds_ref, bias_ref, masked_q, k_ref, vt_ref, m_ref, l_ref, acc_ref, lse_ref, ctxt_ref
    )
    y_ref[...] = own_ref[...].astype(F32) + tn(ctxt_ref[...], w_ref[span(3, width)])
    norm_forward(y_ref, vec_ref, first, hat_ref, inverse_ref, y_ref)


def call_forward(bounds, x, own, weights, bias, vec, first, name):
    keys, queries = bias.shape
    width = weights.shape[1]
    heads, chunk = width // HD, keys // 4
    return pl.pallas_call(
        functools.partial(forward_kernel, first=first),
        out_shape=(
            shape(queries, width, dtype=BF16),
            shape(keys, width, dtype=BF16),
            shape(heads, queries),
            shape(width, queries, dtype=BF16),
            shape(queries, width),
            shape(queries, 1),
            shape(queries, width),
        ),
        in_specs=[SMEM, VMEM, VMEM, VMEM, VMEM, VMEM],
        out_specs=[VMEM] * 7,
        scratch_shapes=[
            pltpu.VMEM((heads, queries, 2 * HD), BF16),
            pltpu.VMEM((width, keys), BF16),
            pltpu.VMEM((heads, chunk), F32),
            pltpu.VMEM((heads, chunk), F32),
            pltpu.VMEM((width, chunk), F32),
        ],
        compiler_params=limit(48),
        name=name,
    )(bounds, x, own, weights, bias, vec)


def backward_kernel(scalars_ref, x_ref, own_ref, w_ref, bias_ref, vec_ref, grad_ref, q_ref, k_ref,
                    lse_ref, ctxt_ref, *rest, first):
    if first is not None:
        hat_ref, inverse_ref, *rest = rest
        mine_ref, sent_ref, part_ref, next_ref, norms_ref, *rest = rest
    else:
        mine_ref, sent_ref, part_ref, *rest = rest
        next_ref = None
    masked_q, masked_g, v_ref, kt_ref, delta_ref, dqt_ref, dk_ref, dv_ref, dq_ref, out_ref = rest
    heads, queries = lse_ref.shape
    width = w_ref.shape[1]
    chunk = queries // 2
    core = scalars_ref[4]
    half = width // 2

    def keep(kind, gradient):
        out_ref[...] = low(gradient)
        mine_ref[span(kind, half)] = out_ref[rows_at(core, half)]
        sent_ref[span(kind, half)] = out_ref[rows_at(1 - core, half)]

    queries_low = low(own_ref[...])
    grad_low = low(grad_ref[...])
    w_out = w_ref[span(3, width)]
    keep(3, nn(ctxt_ref[...], grad_low))
    out_ref[...] = low(nt(grad_low, w_out))
    split_heads(out_ref, masked_g, 1.0)
    split_heads(q_ref, masked_q, HD**-0.5)
    grad_t = low(nt(w_out, grad_low)).astype(F32) * ctxt_ref[...].astype(F32)
    for head in range(heads):
        delta_ref[head : head + 1] = jnp.sum(grad_t[span(head, HD)], axis=0, keepdims=True)
    for part in range(k_ref.shape[0] // chunk):
        rows = span(part, chunk)
        v_ref[rows] = low(nt(x_ref[rows], w_ref[span(2, width)]))
        kt_ref[:, rows] = low(nt(w_ref[span(1, width)], x_ref[rows]))
    dqt_ref[...] = jnp.zeros(dqt_ref.shape, F32)
    dk_ref[...] = jnp.zeros(dk_ref.shape, F32)
    dv_ref[...] = jnp.zeros(dv_ref.shape, F32)
    for part in range(2):
        cols = span(part, chunk)

        def body(number, carry):
            keys = rows_at(number, chunk)
            bias = bias_ref[keys, cols]

            def early(head):
                pair = span(head // 2, 2 * HD)
                return (
                    nt(k_ref[keys, pair], masked_q[head, cols]) + bias,
                    nt(v_ref[keys, pair], masked_g[head, cols]),
                )

            def middle(head, both):
                row = slice(head, head + 1)
                chances = jnp.exp(both[0] - lse_ref[row, cols])
                return low(chances), low(chances * (both[1] - delta_ref[row, cols]))

            def late(head, both):
                pair, rows = span(head // 2, 2 * HD), span(head, HD)
                dv_ref[keys, pair] += nn(both[0], masked_g[head, cols])
                dk_ref[keys, pair] += nn(both[1], masked_q[head, cols])
                dqt_ref[rows, cols] += nn(kt_ref[rows, keys], both[1])

            staged(heads, early, middle, late)
            return carry

        lax.fori_loop(scalars_ref[2 * part], scalars_ref[2 * part + 1], body, 0)
    dqt = low(dqt_ref[...] * HD**-0.5)
    keep(0, nn(dqt, queries_low))
    dk, dv = low(dk_ref[...]), low(dv_ref[...])
    keep(1, tn(dk, x_ref[...]))
    keep(2, tn(dv, x_ref[...]))
    dq_ref[...] = grad_ref[...] + tn(dqt, w_ref[span(0, width)])
    if first is not None:
        part_ref[...] = low(nn(dk, w_ref[span(1, width)]) + nn(dv, w_ref[span(2, width)]))
        sums = norm_backward(dq_ref, hat_ref, inverse_ref, vec_ref[first : first + 1], next_ref)
        norms_ref[0:1] = sums[0]
        norms_ref[1:2] = sums[1]
    else:
        dk_ref[...] = nn(dk, w_ref[span(1, width)]) + nn(dv, w_ref[span(2, width)])
        for part, place in enumerate((core, 3 - core)):
            dk_ref[rows_at(place, chunk)] += dq_ref[span(part, chunk)]
        part_ref[...] = low(dk_ref[...])


def call_backward(scalars, x, own, weights, bias, vec, grad, saved, norm, first, name):
    keys, queries = bias.shape
    width = weights.shape[1]
    heads = width // HD
    outs = [
        shape(2 * width, width, dtype=BF16),
        shape(2 * width, width, dtype=BF16),
        shape(keys, width, dtype=BF16),
    ]
    if first is not None:
        outs += [shape(queries, width), shape(2, width)]
    return pl.pallas_call(
        functools.partial(backward_kernel, first=first),
        out_shape=outs,
        in_specs=[SMEM, VMEM, VMEM, VMEM]
        + [VMEM] * (3 + len(saved) + len(norm)),
        out_specs=[VMEM] * len(outs),
        scratch_shapes=[
            pltpu.VMEM((heads, queries, 2 * HD), BF16),
            pltpu.VMEM((heads, queries, 2 * HD), BF16),
            pltpu.VMEM((keys, width), BF16),
            pltpu.VMEM((width, keys), BF16),
            pltpu.VMEM((heads, queries), F32),
            pltpu.VMEM((width, queries), F32),
            pltpu.VMEM((keys, width), F32),
            pltpu.VMEM((keys, width), F32),
            pltpu.VMEM((queries, width), F32),
            pltpu.VMEM((width, width), BF16),
        ],
        compiler_params=limit(48),
        name=name,
    )(scalars, x, own, weights, bias, vec, grad, *saved, *norm)


def gelu_both(values):
    scale = (2.0 / jnp.pi) ** 0.5
    square = values * values
    bend = jnp.tanh(values * (scale + scale * 0.044715 * square))
    half = 0.5 + 0.5 * bend
    slope = half + (0.5 * values) * (1.0 - bend * bend) * (scale + 3.0 * scale * 0.044715 * square)
    return values * half, slope


def feed_kernel(core_ref, y_ref, w_ref, vec_ref, cot_ref, hat_two, inverse_two,
                block_ref, next_ref, mine_ref, sent_ref, norms_ref,
                low_ref, hid_ref, slope_ref, total_ref, hat_ref, inverse_ref, grad_low,
                *, step):
    core = core_ref[4]
    hidden = w_ref.shape[0] // 2
    half = hidden // 2
    chunks = hidden // step
    low_ref[...] = low(y_ref[...])
    total_ref[...] = y_ref[...]

    def early(number):
        return nt(w_ref[span(number, step)], low_ref[...])

    def middle(number, up):
        hid, slope = gelu_both(up)
        hid_ref[span(number, step)] = low(hid)
        slope_ref[span(number, step)] = slope

    def late(number, _):
        lower = w_ref[hidden + number * step : hidden + (number + 1) * step]
        total_ref[...] += tn(hid_ref[span(number, step)], lower)

    staged(chunks, early, middle, late, 1, 1)
    norm_forward(total_ref, vec_ref, 4, hat_ref, inverse_ref, block_ref)
    sums = norm_backward(cot_ref, hat_ref, inverse_ref, vec_ref[4:5], total_ref)
    norms_ref[2:3] = sums[0]
    norms_ref[3:4] = sums[1]
    grad_low[...] = low(total_ref[...])

    def place(number):
        inner = number % (chunks // 2)
        row = (core if number < chunks // 2 else 1 - core) * half + inner * step
        return inner, pl.multiple_of(row, step)

    def down(number):
        row = place(number)[1]
        return nt(w_ref[pl.ds(pl.multiple_of(hidden + row, step), step)], grad_low[...])

    def turn(number, grad_hidden):
        return low(slope_ref[pl.ds(place(number)[1], step)] * grad_hidden)

    def sums_of(number, grad_up):
        inner, row = place(number)
        rows = pl.ds(row, step)
        kept = mine_ref if number < chunks // 2 else sent_ref
        kept[span(inner, step)] = low(nn(grad_up, low_ref[...]))
        kept[half + inner * step : half + (inner + 1) * step] = low(nn(hid_ref[rows], grad_low[...]))
        total_ref[...] += tn(grad_up, w_ref[rows])

    staged(chunks, down, turn, sums_of, 1, 1)
    sums = norm_backward(total_ref, hat_two, inverse_two, vec_ref[2:3], next_ref)
    norms_ref[0:1] = sums[0]
    norms_ref[1:2] = sums[1]


def call_feed(scalars, y, weights, vec, cotangent, hat, inverse):
    queries, width = y.shape
    hidden = FF
    return pl.pallas_call(
        functools.partial(feed_kernel, step=256),
        out_shape=(
            shape(queries, width, dtype=BF16),
            shape(queries, width),
            shape(hidden, width, dtype=BF16),
            shape(hidden, width, dtype=BF16),
            shape(4, width),
        ),
        in_specs=[SMEM, VMEM, VMEM] + [VMEM] * 4,
        out_specs=[VMEM] * 5,
        scratch_shapes=[
            pltpu.VMEM((queries, width), BF16),
            pltpu.VMEM((hidden, queries), BF16),
            pltpu.VMEM((hidden, queries), F32),
            pltpu.VMEM((queries, width), F32),
            pltpu.VMEM((queries, width), F32),
            pltpu.VMEM((queries, 1), F32),
            pltpu.VMEM((queries, width), BF16),
        ],
        compiler_params=limit(48),
        name="feed",
    )(scalars, y, weights, vec, cotangent, hat, inverse)


def halves(values):
    high = low(values)
    return high, low(values - high.astype(F32))


def fine(dot, left, right):
    left_high, left_low = halves(left)
    right_high, right_low = halves(right)
    return dot(left_high, right_high) + (dot(left_high, right_low) + dot(left_low, right_high))


def newton_turn(x_ref, s_ref, z_ref):
    count, size = x_ref.shape[0], x_ref.shape[1]
    for number in range(count):
        high, rest = halves(x_ref[number])
        z_ref[number] = jnp.concatenate([high, rest], axis=1)
        right = jnp.concatenate(
            [jnp.concatenate([high, high], axis=1), jnp.concatenate([rest, rest], axis=1)], axis=0
        )
        product = nt(z_ref[number], right)
        high, rest = halves(product[:, :size] + product[:, size:])
        s_ref[number] = jnp.concatenate([high, rest], axis=1)
    for number in range(count):
        terms = z_ref[number]
        product = nn(s_ref[number], jnp.concatenate([terms, terms], axis=0))
        x_ref[number] = 1.5 * x_ref[number] - 0.5 * (product[:, :size] + product[:, size:])


def adam_terms(gradient, first, second):
    first_new = MOMENT_DECAY * first + (1.0 - MOMENT_DECAY) * gradient
    second_new = MOMENT_DECAY * second + (1.0 - MOMENT_DECAY) * gradient * gradient
    correction = 1.0 - MOMENT_DECAY**STEP
    direction = first_new / correction / (jnp.sqrt(second_new / correction) + ADAM_EPS)
    return first_new, second_new, direction


def optimizer_kernel(shift_ref, *refs, terms, vectors, held):
    grads, refs = refs[:terms], refs[terms:]
    master_ref, first_ref, second_ref, left_ref, right_ref, left_basis, right_basis = refs[:7]
    vec_in, refs = refs[7 : 7 + vectors], refs[7 + vectors + held :]
    new_master, new_first, new_second, new_left, new_right = refs[:5]
    new_left_basis, new_right_basis = refs[5:7]
    vec_out, (g_ref, x_ref, s_ref, z_ref, p_ref) = refs[7 : 7 + vectors], refs[7 + vectors :]
    count, side, height = master_ref.shape
    keep = MOMENT_DECAY

    def unit(matrix):
        total = jnp.sum(jnp.sum(matrix * matrix, axis=1, keepdims=True), axis=0, keepdims=True)
        return matrix * lax.rsqrt(total + 1e-06)

    g_ref[...] = fold(*[one[...] for one in grads])
    for pair in range((count + 1) // 2):
        x_ref[count + pair] = jnp.zeros((height, height), F32)
    for block in range(count):
        gradient = g_ref[span(block, side)]
        new_left[block] = keep * left_ref[block] + (1.0 - keep) * tn(gradient, gradient)
        new_right[block] = keep * right_ref[block] + (1.0 - keep) * nt(gradient, gradient)
    for block in range(count):
        x_ref[block] = unit(fine(nn, new_left[block], left_basis[block]))
        corner = span(block % 2, side)
        x_ref[count + block // 2, corner, corner] = unit(
            fine(nn, new_right[block], right_basis[block])
        )

    def turn(number, carry):
        newton_turn(x_ref, s_ref, z_ref)
        return carry

    lax.fori_loop(0, NEWTON_TURNS, turn, 0)
    for block in range(count):
        corner = span(block % 2, side)
        new_left_basis[block] = x_ref[block]
        new_right_basis[block] = x_ref[count + block // 2, corner, corner]
    for block in range(count):
        high, rest = halves(new_left_basis[block])
        gradient = g_ref[span(block, side)]
        partway = nn(gradient, high) + nn(gradient, rest)
        turned = fine(tn, new_right_basis[block], partway)
        new_first[block], new_second[block], p_ref[block] = adam_terms(
            turned, first_ref[block], second_ref[block]
        )
    for block in range(count):
        partback = fine(nn, new_right_basis[block], p_ref[block])
        step = fine(nt, partback, new_left_basis[block])
        new_master[block] = (
            master_ref[block] * (1.0 - LEARN_RATE * WEIGHT_DECAY) - LEARN_RATE * step
        )
    if vectors:
        vec_ref, vec_first, vec_second = vec_in
        rows, columns = vec_ref.shape
        tail = pltpu.roll(g_ref[count * side :].astype(F32), shift_ref[0], 1)
        vec_out[1][...], vec_out[2][...], direction = adam_terms(
            tail[:rows, :columns], vec_first[...], vec_second[...]
        )
        vec_out[0][...] = vec_ref[...] - VECTOR_RATE * direction


def optimize(shift, grads, arrays, number, count, vectors, before):
    def part(one):
        return pl.BlockSpec((count,) + one.shape[1:], lambda step: (number, 0, 0))

    side, height = arrays[0].shape[1:]
    matrices = count + (count + 1) // 2
    inputs = [shift, *grads, *arrays, *vectors]
    whole = [pl.BlockSpec(one.shape, lambda step: (0, 0)) for one in vectors]
    return pl.pallas_call(
        functools.partial(
            optimizer_kernel, terms=len(grads), vectors=len(vectors), held=len(before)
        ),
        grid=(1,),
        out_shape=[shape(*one.shape) for one in [*arrays, *vectors]],
        in_specs=[SMEM]
        + [pl.BlockSpec(one.shape, lambda step: (0, 0)) for one in grads]
        + [part(one) for one in arrays]
        + whole
        + [pl.BlockSpec(memory_space=pl.ANY)] * len(before),
        out_specs=[part(one) for one in arrays] + whole,
        input_output_aliases={len(inputs) + place: place for place in range(len(before))},
        scratch_shapes=[
            pltpu.VMEM(grads[0].shape, BF16),
            pltpu.VMEM((matrices, height, height), F32),
            pltpu.VMEM((matrices, height, 2 * height), BF16),
            pltpu.VMEM((matrices, height, 2 * height), BF16),
            pltpu.VMEM((count, side, height), F32),
        ],
        compiler_params=limit(48),
        name="optimizer",
    )(*inputs, *before)


def own_rows(values, index, chunk):
    early = lax.dynamic_slice_in_dim(values, index * chunk, chunk, 0)
    late = lax.dynamic_slice_in_dim(values, (3 - index) * chunk, chunk, 0)
    return jnp.concatenate([early, late], axis=0)


def in_order(mine, other, index, chunk):
    inner = jnp.where(index == 0, other, mine)
    outer = jnp.where(index == 0, mine, other)
    return jnp.concatenate([outer[:chunk], inner, outer[chunk:]], axis=0)


def key_bounds(key_ids, query_ids, chunk):
    edges = []
    for part in range(2):
        rows = query_ids[part * chunk : (part + 1) * chunk]
        lowest = jnp.sum((key_ids < rows[0]).astype(jnp.int32))
        highest = jnp.sum((key_ids <= rows[-1]).astype(jnp.int32))
        edges += [lowest // chunk, (highest + chunk - 1) // chunk]
    return edges


def per_device(
    decoder_input,
    encoder_states,
    decoder_segments,
    encoder_segments,
    output_cotangent,
    block_slots,
    master,
    first_moment,
    second_moment,
    row_statistics,
    column_statistics,
    row_basis,
    column_basis,
    vectors,
    vector_first,
    vector_second,
):
    core = lax.axis_index("tensor")
    cores = lax.axis_size("tensor")
    ring, rings = lax.axis_index("dp"), lax.axis_size("dp")
    owned_count, block_height = master.shape[1], master.shape[2]
    vector_cols = vectors.shape[1]
    length, width = decoder_input.shape[1], decoder_input.shape[2]
    row_count = width // block_height
    block_total = block_slots.shape[0]
    column_count = block_total // row_count
    chunk = length // 4
    per_ring = owned_count * HD + VECTOR_ROWS
    group = block_height // vector_cols

    payload = low(master[0]).transpose(0, 2, 1).reshape(owned_count * HD, block_height)
    lane = jnp.arange(block_height) // vector_cols
    here = lane == ring % group
    small = jnp.where(here[None], jnp.tile(low(vectors), (1, group)), jnp.zeros((), BF16))
    small = jnp.pad(small, ((0, VECTOR_ROWS - vectors.shape[0]), (0, 0)))
    payload = jnp.concatenate([payload, small], axis=0)
    owner, local = block_slots // owned_count, block_slots % owned_count
    chips = jnp.arange(rings, dtype=jnp.int32)
    grid_of_chips = rings == DEPTH * SIDE * SIDE
    if grid_of_chips:
        pieces = gather_chips(payload)
        pieces += [swapped(piece) for piece in pieces]
        starts = apart(ring, owner, 1) * per_ring + local * HD
        slices = [(index ^ core) * rings * per_ring for index in range(cores)]
        ends = (apart(ring, chips, 1) + 1) * per_ring - VECTOR_ROWS
    else:
        pieces = [lax.all_gather(payload, ("dp", "tensor"), axis=0, tiled=True)]
        starts = owner * cores * per_ring + local * HD
        slices = [index * per_ring for index in range(cores)]
        ends = (chips * cores + 1) * per_ring - VECTOR_ROWS
    w_self, w_cross, w_feed, vec = assemble(
        jnp.concatenate([starts + start for start in slices]), ends, pieces, cores, width, group
    )

    tokens, encoder_rows = decoder_input[0], encoder_states[0]
    ids, encoder_ids = decoder_segments[0], encoder_segments[0]
    own_tokens = own_rows(tokens, core, chunk)
    own_ids = own_rows(ids, core, chunk)
    own_cotangent = own_rows(output_cotangent[0], core, chunk)
    places = jnp.arange(length, dtype=jnp.int32)
    own_places = own_rows(places, core, chunk)
    self_allowed = (ids[:, None] == own_ids[None, :]) & (places[:, None] <= own_places[None, :])
    self_bias = jnp.where(self_allowed, 0.0, NEGATIVE).astype(F32)
    cross_bias = jnp.where(encoder_ids[:, None] == own_ids[None, :], 0.0, NEGATIVE).astype(F32)
    self_edges = key_bounds(ids, own_ids, chunk)
    self_scalars = jnp.stack([self_edges[0], core + 1, self_edges[2], 4 - core, core])
    cross_scalars = jnp.stack(key_bounds(encoder_ids, own_ids, chunk) + [core])

    *self_saved, hat_one, inverse_one, y_one = call_forward(
        self_scalars, tokens, own_tokens, w_self, self_bias, vec, 0, "self_forward"
    )
    *cross_saved, hat_two, inverse_two, y_two = call_forward(
        cross_scalars, encoder_rows, y_one, w_cross, cross_bias, vec, 2, "cross_forward"
    )
    own_output, grad_two, ff_mine, ff_sent, norms_late = call_feed(
        self_scalars, y_two, w_feed, vec, own_cotangent, hat_two, inverse_two
    )
    cross_mine, cross_sent, part_encoder, grad_one, norms_early = call_backward(
        cross_scalars,
        encoder_rows,
        y_one,
        w_cross,
        cross_bias,
        vec,
        grad_two,
        cross_saved,
        [hat_one, inverse_one],
        0,
        "cross_backward",
    )
    self_mine, self_sent, part_input = call_backward(
        self_scalars,
        tokens,
        own_tokens,
        w_self,
        self_bias,
        vec,
        grad_one,
        self_saved,
        [],
        None,
        "self_backward",
    )
    norms = jnp.concatenate(
        [norms_early, norms_late, jnp.zeros((VECTOR_ROWS - 6, width), F32)], axis=0
    )

    terms = [ff_mine, ff_sent, cross_mine, cross_sent, self_mine, self_sent]
    terms = [one if number % 2 == 0 else swapped(one) for number, one in enumerate(terms)]
    terms += [norms, swapped(norms)]
    shift = ((block_height - ring % group * vector_cols) % block_height)[None]
    arrays = [one[0].transpose(0, 2, 1) for one in (master, first_moment, second_moment)]
    arrays += [
        one[0] for one in (row_statistics, column_statistics, row_basis, column_basis)
    ]
    vector_states = [vectors, vector_first, vector_second]
    if grid_of_chips:
        early_count = owned_count // 2
        sizes = (early_count * HD, per_ring - early_count * HD)
        order = jnp.array(PLACES, jnp.int32)
        late = local // early_count
        rows = jnp.where(
            late == 1,
            rings * sizes[0] + order[apart(ring, owner, -1)] * sizes[1],
            order[apart(ring, owner, -1)] * sizes[0],
        )
        ends = rings * sizes[0] + (order[apart(ring, chips, -1)] + 1) * sizes[1] - VECTOR_ROWS
        cuts = [size * places for size in sizes for places in (4, 4, 2, 2, 4)]
        parts = scatter(
            rows + local % early_count * HD, ends, terms, cuts, cores, block_height, group
        )
        column = reduce_plane(*parts[:5])
        column, parts = lax.optimization_barrier((column, parts[5:]))
        early = reduce_column(column)
        column = reduce_plane(*parts)
        updated = optimize(shift, early, arrays, 0, early_count, [], [])
        updated = optimize(
            shift, reduce_column(column), arrays, 1, early_count, vector_states, updated
        )
    else:
        ends = (chips + 1) * per_ring - VECTOR_ROWS
        (whole,) = scatter(
            owner * per_ring + local * HD,
            ends,
            terms,
            [rings * per_ring],
            cores,
            block_height,
            group,
        )
        summed = lax.psum_scatter(whole, "dp", scatter_dimension=0, tiled=True)
        updated = optimize(shift, [summed], arrays, 0, owned_count, vector_states, [])

    block_output = in_order(own_output, swapped(own_output), core, chunk)
    input_gradient = part_input.astype(F32) + swapped(part_input).astype(F32)
    encoder_gradient = part_encoder.astype(F32) + swapped(part_encoder).astype(F32)
    return (
        block_output[None],
        input_gradient[None],
        encoder_gradient[None],
        *[one.transpose(0, 2, 1)[None] for one in updated[:3]],
        *[one[None] for one in updated[3:7]],
        *updated[7:],
    )


def solution(mesh):
    blocks = P("tensor", "dp", None, None)
    rows = P("dp", None, None)
    return jax.shard_map(
        per_device,
        mesh=mesh,
        in_specs=(rows, rows, P("dp", None), P("dp", None), rows, P())
        + (blocks,) * 7
        + (P(None, "dp"),) * 3,
        out_specs=(rows,) * 3 + (blocks,) * 7 + (P(None, "dp"),) * 3,
        check_vma=False,
    )
```

```python
import functools

import jax
import jax.numpy as jnp
from jax import lax
from jax.experimental import pallas as pl
from jax.experimental.pallas import tpu as pltpu
from jax.sharding import PartitionSpec as P

HD = 64
FF = 2048
STEP = 10

NEGATIVE = -1e30
EPS_NORM = 1e-05
MOMENT_DECAY = 0.5
LEARN_RATE = 0.04
WEIGHT_DECAY = 0.01
VECTOR_RATE = 0.25
ADAM_EPS = 1e-08
NEWTON_TURNS = 8
EARLY_TURNS = 5
VECTOR_ROWS = 16
DEPTH, SIDE = 4, 2
MIB = 2**20
F32 = jnp.float32
BF16 = jnp.bfloat16
VMEM = pl.BlockSpec(memory_space=pltpu.VMEM)
SMEM = pl.BlockSpec(memory_space=pltpu.SMEM)
ANY = pl.BlockSpec(memory_space=pl.ANY)


def nn(left, right):
    return lax.dot_general(left, right, (((1,), (0,)), ((), ())), preferred_element_type=F32)


def nt(left, right):
    return lax.dot_general(left, right, (((1,), (1,)), ((), ())), preferred_element_type=F32)


def tn(left, right):
    return lax.dot_general(left, right, (((0,), (0,)), ((), ())), preferred_element_type=F32)


def low(values):
    return values.astype(BF16)


def span(number, size):
    return slice(number * size, (number + 1) * size)


def rows_at(number, size):
    return pl.ds(pl.multiple_of(number * size, size), size)


def shape(*dims, dtype=F32):
    return jax.ShapeDtypeStruct(dims, dtype)


def scratch(shapes):
    return [pltpu.VMEM(one.shape, one.dtype) for one in shapes]


def limit(mib):
    return pltpu.CompilerParams(vmem_limit_bytes=mib * MIB)


def block_places(columns, cores):
    hidden = FF // cores // HD
    heads = (columns - 2 * hidden) // 8
    places = []
    for column in range(columns):
        if column < 8 * heads:
            places.append((column // heads, column % heads * HD))
        else:
            column -= 8 * heads
            places.append((8 + column // hidden, column % hidden * HD))
    return places, heads * HD, hidden * HD


def start_copies(pairs, semaphores, first=0):
    copies = [
        pltpu.make_async_copy(source, target, semaphores.at[first + number])
        for number, (source, target) in enumerate(pairs)
    ]
    for copy in copies:
        copy.start()
    return copies


def wait_for(copies):
    for copy in copies:
        copy.wait()


def in_a_row(pieces, target_ref):
    pairs, start = [], 0
    for piece in pieces:
        pairs.append((piece, target_ref.at[pl.ds(start, piece.shape[0])]))
        start += piece.shape[0]
    return pairs


def assemble(rows_ref, ends_ref, gathered_ref, w_refs, vec_ref, cores, group):
    height = gathered_ref.shape[1]
    row_count = vec_ref.shape[1] // height
    total = rows_ref.shape[0] // cores
    columns = total // row_count
    places, head_rows, hidden_rows = block_places(columns, cores)
    for core in range(cores):
        for row in range(row_count):
            for column in range(columns):
                kind, inner = places[column]
                size = head_rows if kind < 8 else hidden_rows
                target = (kind % 4 * cores + core) * size + inner
                source = pl.multiple_of(rows_ref[core * total + row * columns + column], 16)
                block = gathered_ref[pl.ds(source, HD), :]
                w_refs[kind // 4][target : target + HD, span(row, height)] = block
    rings = ends_ref.shape[0]
    for part in range(row_count):
        values = jnp.zeros((VECTOR_ROWS, height), F32)
        for ring in range(part * group, min((part + 1) * group, rings)):
            start = pl.multiple_of(ends_ref[ring], 16)
            values = values + gathered_ref[pl.ds(start, VECTOR_ROWS), :].astype(F32)
        vec_ref[:, span(part, height)] = values


def scatter_kernel(rows_ref, ends_ref, *refs, cores, group, cuts):
    ins, (vec_ref, vec_in_ref), refs = refs[:6], refs[6:8], refs[8:]
    outs, refs = refs[:cuts], refs[cuts:]
    terms, (all_ref, in_sems, out_sems) = refs[:6], refs[6:]
    copies = start_copies(zip(ins, terms), in_sems)
    height = all_ref.shape[1]
    row_count = vec_ref.shape[1] // height
    columns = rows_ref.shape[0] // row_count
    places, head_rows, hidden_rows = block_places(columns, cores)
    for part, (first, last, size) in enumerate(
        ((8, 10, hidden_rows), (4, 8, head_rows), (0, 4, head_rows))
    ):
        one, two = terms[2 * part : 2 * part + 2]
        wait_for(copies[2 * part : 2 * part + 2])
        for column in range(columns):
            kind, inner = places[column]
            if first <= kind < last:
                start = (kind - first) * size + inner
                for row in range(row_count):
                    here = slice(start, start + HD), span(row, height)
                    target = pl.multiple_of(rows_ref[row * columns + column], 16)
                    total = one[here].astype(F32) + two[here].astype(F32)
                    all_ref[pl.ds(target, HD), :] = low(total)
    total = low(vec_ref[...] + vec_in_ref[...])
    for ring in range(ends_ref.shape[0]):
        start = pl.multiple_of(ends_ref[ring], 16)
        all_ref[pl.ds(start, VECTOR_ROWS), :] = total[:, span(ring // group, height)]
    pairs = [(part, out) for out, part in in_a_row(outs, all_ref)]
    wait_for(start_copies(pairs, out_sems))


def scatter(rows, ends, terms, cuts, cores, height, group):
    return pl.pallas_call(
        functools.partial(scatter_kernel, cores=cores, group=group, cuts=len(cuts)),
        out_shape=[shape(cut, height, dtype=BF16) for cut in cuts],
        in_specs=[SMEM, SMEM] + [ANY] * 6 + [VMEM] * 2,
        out_specs=[ANY] * len(cuts),
        scratch_shapes=scratch(terms[:6])
        + [
            pltpu.VMEM((sum(cuts), height), BF16),
            pltpu.SemaphoreType.DMA((6,)),
            pltpu.SemaphoreType.DMA((len(cuts),)),
        ],
        compiler_params=limit(60),
        name="scatter",
    )(rows, ends, *terms)


def hop(values, *steps):
    sizes = (DEPTH, SIDE, SIDE)
    pairs = []
    for source in range(DEPTH * SIDE * SIDE):
        place = (source // (SIDE * SIDE), source // SIDE % SIDE, source % SIDE)
        z, y, x = ((one + step) % size for one, step, size in zip(place, steps, sizes))
        pairs.append((source, (z * SIDE + y) * SIDE + x))
    return lax.ppermute(values, "dp", pairs)


def swapped(values):
    return lax.ppermute(values, "tensor", [(0, 1), (1, 0)])


def apart(ring, other, sign):
    side = SIDE * SIDE
    deep = (sign * (ring // side - other // side)) % DEPTH
    across = (ring // SIDE % SIDE) ^ (other // SIDE % SIDE)
    return (across * SIDE + ((ring % SIDE) ^ (other % SIDE))) * DEPTH + deep


def gather_chips(own, beside):
    deep = [hop(own, step, 0, 0) for step in range(1, DEPTH)]
    near = [hop(own, 0, 0, 1), hop(own, 0, 1, 0), hop(own, 0, 1, 1)]
    deep, near, beside = lax.optimization_barrier((jnp.concatenate(deep, axis=0), near, beside))
    by_x, by_y = hop(deep, 0, 0, 1), hop(deep, 0, 1, 0)
    cut = deep.shape[0] // 32 * 16
    pieces = [own, deep, near[0], by_x, near[1], by_y, near[2]]
    return pieces + [hop(by_y[:cut], 0, 0, 1), hop(by_x[cut:], 0, 1, 0)], beside


PLACES = (12, 13, 14, 15, 2, 3, 10, 11, 8, 9, 6, 7, 0, 1, 4, 5)


def fold(*terms):
    return low(functools.reduce(lambda one, two: one + two, [term.astype(F32) for term in terms]))


def reduce_plane(along_x, along_y, late_y, late_x, here, beside):
    half = late_x.shape[0]
    from_x, from_y = hop(along_x, 0, 0, 1), hop(along_y, 0, 1, 0)
    from_x, from_y, beside = lax.optimization_barrier((from_x, from_y, beside))
    more_y = hop(fold(late_y, from_x[:half]), 0, 1, 0)
    more_x = hop(fold(late_x, from_y[:half]), 0, 0, 1)
    column = jnp.concatenate(
        [fold(here[:half], from_x[half:], more_y), fold(here[half:], from_y[half:], more_x)],
        axis=0,
    )
    return column, beside


def reduce_column(column):
    rows = column.shape[0] // DEPTH
    return [column[:rows]] + [
        hop(column[step * rows : (step + 1) * rows], step, 0, 0) for step in range(1, DEPTH)
    ]


def norm_forward(total_ref, vec_ref, first, hat_ref, inverse_ref, out_ref, step=64):
    gain, shift = vec_ref[first : first + 1], vec_ref[first + 1 : first + 2]

    def body(number, carry):
        rows = rows_at(number, step)
        values = total_ref[rows]
        center = values - jnp.mean(values, axis=1, keepdims=True)
        inverse = lax.rsqrt(jnp.mean(center * center, axis=1, keepdims=True) + EPS_NORM)
        hat = center * inverse
        hat_ref[rows] = hat
        inverse_ref[rows] = inverse
        out_ref[rows] = (hat * gain + shift).astype(out_ref.dtype)
        return carry

    lax.fori_loop(0, total_ref.shape[0] // step, body, 0)


def norm_backward(grad_ref, hat_ref, inverse_ref, gain, out_ref, step=64):
    width = grad_ref.shape[1]

    def body(number, carry):
        rows = rows_at(number, step)
        grad, hat = grad_ref[rows].astype(F32), hat_ref[rows]
        scaled = grad * gain
        middle = jnp.mean(scaled, axis=1, keepdims=True)
        slope = jnp.mean(scaled * hat, axis=1, keepdims=True)
        out_ref[rows] = (scaled - middle - hat * slope) * inverse_ref[rows]
        return (
            carry[0] + jnp.sum((grad * hat).reshape(step // 8, 8, width), axis=0),
            carry[1] + jnp.sum(grad.reshape(step // 8, 8, width), axis=0),
        )

    zeros = jnp.zeros((8, width), F32)
    sums = lax.fori_loop(0, grad_ref.shape[0] // step, body, (zeros, zeros))
    return [jnp.sum(one, axis=0, keepdims=True) for one in sums]


def split_heads(source_ref, masked_ref, factor):
    for head in range(masked_ref.shape[0]):
        pair = source_ref[:, span(head // 2, 2 * HD)]
        lane = lax.broadcasted_iota(jnp.int32, pair.shape, 1)
        here = (lane >= HD) if head % 2 else (lane < HD)
        masked_ref[head] = jnp.where(here, pair, jnp.zeros_like(pair)) * jnp.asarray(factor, BF16)


def staged(count, early, middle, late, ahead=2, lag=2):
    ready = [early(number) for number in range(min(ahead, count))]
    held = []
    for number in range(count):
        now = ready.pop(0)
        if number + ahead < count:
            ready.append(early(number + ahead))
        held.append((number, middle(number, now)))
        if len(held) > lag:
            late(*held.pop(0))
    while held:
        late(*held.pop(0))


def attend_forward(bounds_ref, bias_ref, masked_q, k_ref, vt_ref, m_ref, l_ref, acc_ref, lse_ref,
                   ctxt_ref):
    heads, chunk = m_ref.shape
    for part in range(lse_ref.shape[1] // chunk):
        cols = span(part, chunk)
        m_ref[...] = jnp.full(m_ref.shape, NEGATIVE, F32)
        l_ref[...] = jnp.zeros(l_ref.shape, F32)
        acc_ref[...] = jnp.zeros(acc_ref.shape, F32)

        def body(number, carry):
            keys = rows_at(number, chunk)
            bias = bias_ref[keys, cols]

            def early(head):
                return nt(k_ref[keys, span(head // 2, 2 * HD)], masked_q[head, cols]) + bias

            def middle(head, scores):
                row = slice(head, head + 1)
                before = m_ref[row]
                highest = jnp.maximum(before, jnp.max(scores, axis=0, keepdims=True))
                shrink = jnp.exp(before - highest)
                expons = jnp.exp(scores - highest)
                l_ref[row] = l_ref[row] * shrink + jnp.sum(expons, axis=0, keepdims=True)
                m_ref[row] = highest
                return shrink, low(expons)

            def late(head, pair):
                rows = span(head, HD)
                acc_ref[rows] = acc_ref[rows] * pair[0] + nn(vt_ref[rows, keys], pair[1])

            staged(heads, early, middle, late)
            return carry

        lax.fori_loop(bounds_ref[2 * part], bounds_ref[2 * part + 1], body, 0)
        for head in range(heads):
            rows = span(head, HD)
            ctxt_ref[rows, cols] = low(acc_ref[rows] / l_ref[head : head + 1])
        lse_ref[:, cols] = m_ref[...] + jnp.log(l_ref[...])


def branch_forward(bounds_ref, x_ref, own_ref, w_ref, bias_ref, vec_ref,
                   q_ref, k_ref, lse_ref, ctxt_ref, hat_ref, inverse_ref, y_ref, first):
    keys, width = k_ref.shape
    heads, queries = lse_ref.shape
    chunk = keys // 4

    def body(masked_q, vt_ref, m_ref, l_ref, acc_ref):
        q_ref[...] = low(nt(low(own_ref[...]), w_ref[span(0, width)]))
        split_heads(q_ref, masked_q, HD**-0.5)
        for part in range(keys // chunk):
            rows = span(part, chunk)
            k_ref[rows] = low(nt(x_ref[rows], w_ref[span(1, width)]))
            vt_ref[:, rows] = low(nt(w_ref[span(2, width)], x_ref[rows]))
        attend_forward(
            bounds_ref, bias_ref, masked_q, k_ref, vt_ref, m_ref, l_ref, acc_ref, lse_ref, ctxt_ref
        )
        y_ref[...] = own_ref[...].astype(F32) + tn(ctxt_ref[...], w_ref[span(3, width)])
        norm_forward(y_ref, vec_ref, first, hat_ref, inverse_ref, y_ref)

    pl.run_scoped(
        body,
        pltpu.VMEM((heads, queries, 2 * HD), BF16),
        pltpu.VMEM((width, keys), BF16),
        pltpu.VMEM((heads, chunk), F32),
        pltpu.VMEM((heads, chunk), F32),
        pltpu.VMEM((width, chunk), F32),
    )


def branch_backward(scalars_ref, x_ref, own_ref, w_ref, bias_ref, grad_ref, q_ref, k_ref, lse_ref,
                    ctxt_ref, mine_ref, sent_ref, part_ref, norm, arrive):
    heads, queries = lse_ref.shape
    keys, width = k_ref.shape
    chunk = queries // 2

    def body(masked_q, masked_g, v_ref, kt_ref, delta_ref, dqt_ref, dk_ref, dv_ref, dq_ref, out_ref):
        core = scalars_ref[4]
        half = width // 2
        arrive(0)

        def keep(kind, gradient):
            out_ref[...] = low(gradient)
            mine_ref[span(kind, half)] = out_ref[rows_at(core, half)]
            sent_ref[span(kind, half)] = out_ref[rows_at(1 - core, half)]

        grad_low = low(grad_ref[...])
        w_out = w_ref[span(3, width)]
        keep(3, nn(ctxt_ref[...], grad_low))
        out_ref[...] = low(nt(grad_low, w_out))
        split_heads(out_ref, masked_g, 1.0)
        arrive(1)
        split_heads(q_ref, masked_q, HD**-0.5)
        grad_t = low(nt(w_out, grad_low)).astype(F32) * ctxt_ref[...].astype(F32)
        for head in range(heads):
            delta_ref[head : head + 1] = jnp.sum(grad_t[span(head, HD)], axis=0, keepdims=True)
        for part in range(k_ref.shape[0] // chunk):
            rows = span(part, chunk)
            v_ref[rows] = low(nt(x_ref[rows], w_ref[span(2, width)]))
            kt_ref[:, rows] = low(nt(w_ref[span(1, width)], x_ref[rows]))
        dqt_ref[...] = jnp.zeros(dqt_ref.shape, F32)
        dk_ref[...] = jnp.zeros(dk_ref.shape, F32)
        dv_ref[...] = jnp.zeros(dv_ref.shape, F32)
        for part in range(2):
            cols = span(part, chunk)

            def pair(number, carry):
                keys = rows_at(number, chunk)
                bias = bias_ref[keys, cols]

                def early(head):
                    pair = span(head // 2, 2 * HD)
                    return (
                        nt(k_ref[keys, pair], masked_q[head, cols]) + bias,
                        nt(v_ref[keys, pair], masked_g[head, cols]),
                    )

                def middle(head, both):
                    row = slice(head, head + 1)
                    chances = jnp.exp(both[0] - lse_ref[row, cols])
                    return low(chances), low(chances * (both[1] - delta_ref[row, cols]))

                def late(head, both):
                    pair, rows = span(head // 2, 2 * HD), span(head, HD)
                    dv_ref[keys, pair] += nn(both[0], masked_g[head, cols])
                    dk_ref[keys, pair] += nn(both[1], masked_q[head, cols])
                    dqt_ref[rows, cols] += nn(kt_ref[rows, keys], both[1])

                staged(heads, early, middle, late)
                return carry

            lax.fori_loop(scalars_ref[2 * part], scalars_ref[2 * part + 1], pair, 0)
        dqt = low(dqt_ref[...] * HD**-0.5)
        keep(0, nn(dqt, low(own_ref[...])))
        dk, dv = low(dk_ref[...]), low(dv_ref[...])
        keep(1, tn(dk, x_ref[...]))
        keep(2, tn(dv, x_ref[...]))
        dq_ref[...] = grad_ref[...] + tn(dqt, w_ref[span(0, width)])
        if norm is not None:
            part_ref[...] = low(nn(dk, w_ref[span(1, width)]) + nn(dv, w_ref[span(2, width)]))
            hat_ref, inverse_ref, gain, next_ref, norms_ref, place = norm
            sums = norm_backward(dq_ref, hat_ref, inverse_ref, gain, next_ref)
            norms_ref[place : place + 1] = sums[0]
            norms_ref[place + 1 : place + 2] = sums[1]
        else:
            dk_ref[...] = nn(dk, w_ref[span(1, width)]) + nn(dv, w_ref[span(2, width)])
            for part, place in enumerate((core, 3 - core)):
                dk_ref[rows_at(place, chunk)] += dq_ref[span(part, chunk)]
            part_ref[...] = low(dk_ref[...])

    pl.run_scoped(
        body,
        pltpu.VMEM((heads, queries, 2 * HD), BF16),
        pltpu.VMEM((heads, queries, 2 * HD), BF16),
        pltpu.VMEM((keys, width), BF16),
        pltpu.VMEM((width, keys), BF16),
        pltpu.VMEM((heads, queries), F32),
        pltpu.VMEM((width, queries), F32),
        pltpu.VMEM((keys, width), F32),
        pltpu.VMEM((keys, width), F32),
        pltpu.VMEM((queries, width), F32),
        pltpu.VMEM((width, width), BF16),
    )


def gelu_both(values):
    scale = (2.0 / jnp.pi) ** 0.5
    square = values * values
    bend = jnp.tanh(values * (scale + scale * 0.044715 * square))
    half = 0.5 + 0.5 * bend
    slope = half + (0.5 * values) * (1.0 - bend * bend) * (scale + 3.0 * scale * 0.044715 * square)
    return values * half, slope


def feed_both(core, y_ref, w_ref, vec_ref, cot_ref, hat_two, inverse_two,
              block_ref, next_ref, mine_ref, sent_ref, norms_ref, arrive, step=256):
    queries, width = y_ref.shape
    hidden = w_ref.shape[0] // 2
    half = hidden // 2
    chunks = hidden // step

    def body(low_ref, hid_ref, slope_ref, total_ref, hat_ref, inverse_ref, grad_low):
        low_ref[...] = low(y_ref[...])
        total_ref[...] = y_ref[...]

        def early(number):
            return nt(w_ref[span(number, step)], low_ref[...])

        def middle(number, up):
            hid, slope = gelu_both(up)
            hid_ref[span(number, step)] = low(hid)
            slope_ref[span(number, step)] = slope

        def late(number, _):
            lower = w_ref[hidden + number * step : hidden + (number + 1) * step]
            total_ref[...] += tn(hid_ref[span(number, step)], lower)

        staged(chunks, early, middle, late, 1, 1)
        norm_forward(total_ref, vec_ref, 4, hat_ref, inverse_ref, block_ref)
        sums = norm_backward(cot_ref, hat_ref, inverse_ref, vec_ref[4:5], total_ref)
        norms_ref[4:5] = sums[0]
        norms_ref[5:6] = sums[1]
        grad_low[...] = low(total_ref[...])

        def place(number):
            inner = number % (chunks // 2)
            row = (core if number < chunks // 2 else 1 - core) * half + inner * step
            return inner, pl.multiple_of(row, step)

        def down(number):
            row = place(number)[1]
            return nt(w_ref[pl.ds(pl.multiple_of(hidden + row, step), step)], grad_low[...])

        def turn(number, grad_hidden):
            return low(slope_ref[pl.ds(place(number)[1], step)] * grad_hidden)

        def sums_of(number, grad_up):
            inner, row = place(number)
            rows = pl.ds(row, step)
            kept = mine_ref if number < chunks // 2 else sent_ref
            kept[span(inner, step)] = low(nn(grad_up, low_ref[...]))
            kept[half + inner * step : half + (inner + 1) * step] = low(nn(hid_ref[rows], grad_low[...]))
            total_ref[...] += tn(grad_up, w_ref[rows])

        staged(chunks, down, turn, sums_of, 1, 1)
        sums = norm_backward(total_ref, hat_two, inverse_two, vec_ref[2:3], next_ref)
        norms_ref[2:3] = sums[0]
        norms_ref[3:4] = sums[1]

    pl.run_scoped(
        body,
        pltpu.VMEM((queries, width), BF16),
        pltpu.VMEM((hidden, queries), BF16),
        pltpu.VMEM((hidden, queries), F32),
        pltpu.VMEM((queries, width), F32),
        pltpu.VMEM((queries, width), F32),
        pltpu.VMEM((queries, 1), F32),
        pltpu.VMEM((queries, width), BF16),
    )


def layer_kernel(self_ref, cross_ref, rows_ref, ends_ref, *refs, cores, group, pieces):
    gathered, refs = refs[:pieces], refs[pieces:]
    ins, refs = refs[:6], refs[6:]
    block_out, ff_mine_out, ff_sent_out, mine_out, sent_out, part_out, next_out = refs[:7]
    norms_ref, w_out, q_out, k_out, lse_out, ctxt_out = refs[7:13]
    w_self, w_cross, w_feed, vec_ref, x_ref, own_ref, bias_ref, enc_ref, bias_cross, cot_ref = refs[13:23]
    self_saved, refs = refs[23:27], refs[27:]
    cross_saved, refs = refs[:4], refs[4:]
    hat_one, inverse_one, y_one, hat_two, inverse_two, y_two, refs = *refs[:6], refs[6:]
    block_ref, ff_mine, ff_sent, mine_ref, sent_ref, part_ref, grad_ref, next_ref = refs[:8]
    piece_sems, in_sems, out_sems = refs[8:]
    norms_ref[...] = jnp.zeros(norms_ref.shape, F32)

    targets = (x_ref, own_ref, bias_ref, enc_ref, bias_cross, cot_ref)

    def fetch(gathered_ref):
        arriving = start_copies(in_a_row(gathered, gathered_ref), piece_sems)
        start_copies(zip(ins, targets), in_sems)
        wait_for(arriving)
        assemble(
            rows_ref, ends_ref, gathered_ref, (w_self, w_cross, w_feed), vec_ref, cores, group
        )

    total = sum(piece.shape[0] for piece in gathered)
    pl.run_scoped(fetch, pltpu.VMEM((total, gathered[0].shape[1]), BF16))
    arriving = [
        pltpu.make_async_copy(source, target, in_sems.at[number])
        for number, (source, target) in enumerate(zip(ins, targets))
    ]
    wait_for(arriving[:3])
    leaving = start_copies([(w_self, w_out)], out_sems)
    branch_forward(
        self_ref, x_ref, own_ref, w_self, bias_ref, vec_ref, *self_saved, hat_one, inverse_one,
        y_one, 0,
    )
    leaving += start_copies(zip(self_saved, (q_out, k_out, lse_out, ctxt_out)), out_sems, 1)
    wait_for(arriving[3:5])
    branch_forward(
        cross_ref, enc_ref, y_one, w_cross, bias_cross, vec_ref, *cross_saved, hat_two, inverse_two,
        y_two, 2,
    )
    wait_for(arriving[5:])
    feed_both(
        self_ref[4], y_two, w_feed, vec_ref, cot_ref, hat_two, inverse_two, block_ref, grad_ref,
        ff_mine, ff_sent, norms_ref, None,
    )
    pairs = [(block_ref, block_out), (ff_mine, ff_mine_out), (ff_sent, ff_sent_out)]
    leaving += start_copies(pairs, out_sems, 5)
    branch_backward(
        cross_ref, enc_ref, y_one, w_cross, bias_cross, grad_ref, *cross_saved, mine_ref, sent_ref,
        part_ref, (hat_one, inverse_one, vec_ref[0:1], next_ref, norms_ref, 0), lambda number: None,
    )
    pairs = [(mine_ref, mine_out), (sent_ref, sent_out), (part_ref, part_out), (next_ref, next_out)]
    leaving += start_copies(pairs, out_sems, 8)
    wait_for(leaving)


def saved_shapes(keys, queries, width):
    heads = width // HD
    return [
        shape(queries, width, dtype=BF16),
        shape(keys, width, dtype=BF16),
        shape(heads, queries),
        shape(width, queries, dtype=BF16),
    ]


def call_layer(scalars, pieces, inputs, cores, group):
    keys, queries = inputs[2].shape
    width = inputs[0].shape[1]
    saved = saved_shapes(keys, queries, width)
    weights = shape(4 * width, width, dtype=BF16)
    tokens = shape(queries, width)
    norm = [tokens, shape(queries, 1), tokens]
    outs = [
        shape(queries, width, dtype=BF16),
        shape(FF, width, dtype=BF16),
        shape(FF, width, dtype=BF16),
        shape(2 * width, width, dtype=BF16),
        shape(2 * width, width, dtype=BF16),
        shape(keys, width, dtype=BF16),
        tokens,
    ]
    kept = [weights, weights, shape(2 * FF, width, dtype=BF16), shape(VECTOR_ROWS, width)]
    kept += [*inputs, *saved, *saved, *norm, *norm, *outs[:6], tokens, tokens]
    norms = shape(VECTOR_ROWS, width)
    return pl.pallas_call(
        functools.partial(layer_kernel, cores=cores, group=group, pieces=len(pieces)),
        out_shape=[*outs, norms, weights, *saved],
        in_specs=[SMEM] * 4 + [ANY] * (len(pieces) + len(inputs)),
        out_specs=[ANY] * 7 + [VMEM] + [ANY] * 5,
        scratch_shapes=scratch(kept)
        + [
            pltpu.SemaphoreType.DMA((len(pieces),)),
            pltpu.SemaphoreType.DMA((6,)),
            pltpu.SemaphoreType.DMA((12,)),
        ],
        compiler_params=limit(56),
        name="layer",
    )(*scalars, *pieces, *inputs)


def self_backward_kernel(scalars_ref, *refs):
    ins, (mine_out, sent_out, part_out), refs = refs[:9], refs[9:12], refs[12:]
    grad_ref, ctxt_ref, w_ref, q_ref, x_ref, own_ref, k_ref, lse_ref, bias_ref = refs[:9]
    mine_ref, sent_ref, part_ref, in_sems, out_sems = refs[9:]
    copies = start_copies(zip(ins, refs[:9]), in_sems)
    branch_backward(
        scalars_ref, x_ref, own_ref, w_ref, bias_ref, grad_ref, q_ref, k_ref, lse_ref, ctxt_ref,
        mine_ref, sent_ref, part_ref, None,
        lambda number: wait_for(copies[3:] if number else copies[:3]),
    )
    pairs = [(mine_ref, mine_out), (sent_ref, sent_out), (part_ref, part_out)]
    wait_for(start_copies(pairs, out_sems))


def call_self_backward(scalars, inputs):
    keys, width = inputs[4].shape
    outs = [
        shape(2 * width, width, dtype=BF16),
        shape(2 * width, width, dtype=BF16),
        shape(keys, width, dtype=BF16),
    ]
    return pl.pallas_call(
        self_backward_kernel,
        out_shape=outs,
        in_specs=[SMEM] + [ANY] * 9,
        out_specs=[ANY] * 3,
        scratch_shapes=scratch([*inputs, *outs])
        + [pltpu.SemaphoreType.DMA((9,)), pltpu.SemaphoreType.DMA((3,))],
        compiler_params=limit(62),
        cost_estimate=pl.CostEstimate(
            flops=12 * 10**9, bytes_accessed=12 * MIB, transcendentals=0
        ),
        name="self_backward",
    )(scalars, *inputs)


def halves(values):
    high = low(values)
    return high, low(values - high.astype(F32))


def fine(dot, left, right):
    left_high, left_low = halves(left)
    right_high, right_low = halves(right)
    return dot(left_high, right_high) + (dot(left_high, right_low) + dot(left_low, right_high))


def newton_turn(x_ref, s_ref, z_ref):
    count, size = x_ref.shape[0], x_ref.shape[1]
    for number in range(count):
        high, rest = halves(x_ref[number])
        z_ref[number] = jnp.concatenate([high, rest], axis=1)
        right = jnp.concatenate(
            [jnp.concatenate([high, high], axis=1), jnp.concatenate([rest, rest], axis=1)], axis=0
        )
        product = nt(z_ref[number], right)
        high, rest = halves(product[:, :size] + product[:, size:])
        s_ref[number] = jnp.concatenate([high, rest], axis=1)
    for number in range(count):
        terms = z_ref[number]
        product = nn(s_ref[number], jnp.concatenate([terms, terms], axis=0))
        x_ref[number] = 1.5 * x_ref[number] - 0.5 * (product[:, :size] + product[:, size:])


def early_turn(x_ref, s_ref, z_ref):
    count, size = x_ref.shape[0], x_ref.shape[1]
    for number in range(count):
        high = low(x_ref[number])
        z_ref[number, :, :size] = high
        s_ref[number, :, :size] = low(nt(high, high))
    for number in range(count):
        product = nn(s_ref[number, :, :size], z_ref[number, :, :size])
        x_ref[number] = 1.5 * x_ref[number] - 0.5 * product


def adam_terms(gradient, first, second):
    first_new = MOMENT_DECAY * first + (1.0 - MOMENT_DECAY) * gradient
    second_new = MOMENT_DECAY * second + (1.0 - MOMENT_DECAY) * gradient * gradient
    correction = 1.0 - MOMENT_DECAY**STEP
    direction = first_new / correction / (jnp.sqrt(second_new / correction) + ADAM_EPS)
    return first_new, second_new, direction


def optimizer_kernel(shift_ref, *refs, terms, vectors, held):
    grads, refs = refs[:terms], refs[terms:]
    master_ref, first_ref, second_ref, left_ref, right_ref, left_basis, right_basis = refs[:7]
    vec_in, refs = refs[7 : 7 + vectors], refs[7 + vectors + held :]
    new_master, new_first, new_second, new_left, new_right = refs[:5]
    new_left_basis, new_right_basis = refs[5:7]
    vec_out, (g_ref, x_ref, s_ref, z_ref, p_ref) = refs[7 : 7 + vectors], refs[7 + vectors :]
    count, side, height = master_ref.shape
    keep = MOMENT_DECAY

    def unit(matrix):
        total = jnp.sum(jnp.sum(matrix * matrix, axis=1, keepdims=True), axis=0, keepdims=True)
        return matrix * lax.rsqrt(total + 1e-06)

    g_ref[...] = fold(*[one[...] for one in grads])
    for pair in range((count + 1) // 2):
        x_ref[count + pair] = jnp.zeros((height, height), F32)
    for block in range(count):
        gradient = g_ref[span(block, side)]
        new_left[block] = keep * left_ref[block] + (1.0 - keep) * tn(gradient, gradient)
        new_right[block] = keep * right_ref[block] + (1.0 - keep) * nt(gradient, gradient)
    for block in range(count):
        x_ref[block] = unit(fine(nn, new_left[block], left_basis[block]))
        corner = span(block % 2, side)
        x_ref[count + block // 2, corner, corner] = unit(
            fine(nn, new_right[block], right_basis[block])
        )

    def rough(number, carry):
        early_turn(x_ref, s_ref, z_ref)
        return carry

    def turn(number, carry):
        newton_turn(x_ref, s_ref, z_ref)
        return carry

    lax.fori_loop(0, EARLY_TURNS, rough, 0)
    lax.fori_loop(EARLY_TURNS, NEWTON_TURNS, turn, 0)
    for block in range(count):
        corner = span(block % 2, side)
        new_left_basis[block] = x_ref[block]
        new_right_basis[block] = x_ref[count + block // 2, corner, corner]
    for block in range(count):
        high, rest = halves(new_left_basis[block])
        gradient = g_ref[span(block, side)]
        partway = nn(gradient, high) + nn(gradient, rest)
        turned = fine(tn, new_right_basis[block], partway)
        new_first[block], new_second[block], p_ref[block] = adam_terms(
            turned, first_ref[block], second_ref[block]
        )
    for block in range(count):
        partback = fine(nn, new_right_basis[block], p_ref[block])
        step = fine(nt, partback, new_left_basis[block])
        new_master[block] = (
            master_ref[block] * (1.0 - LEARN_RATE * WEIGHT_DECAY) - LEARN_RATE * step
        )
    if vectors:
        vec_ref, vec_first, vec_second = vec_in
        rows, columns = vec_ref.shape
        tail = pltpu.roll(g_ref[count * side :].astype(F32), shift_ref[0], 1)
        vec_out[1][...], vec_out[2][...], direction = adam_terms(
            tail[:rows, :columns], vec_first[...], vec_second[...]
        )
        vec_out[0][...] = vec_ref[...] - VECTOR_RATE * direction


def optimize(shift, grads, arrays, number, count, vectors, before):
    def part(one):
        return pl.BlockSpec((count,) + one.shape[1:], lambda step: (number, 0, 0))

    side, height = arrays[0].shape[1:]
    matrices = count + (count + 1) // 2
    inputs = [shift, *grads, *arrays, *vectors]
    whole = [pl.BlockSpec(one.shape, lambda step: (0, 0)) for one in vectors]
    return pl.pallas_call(
        functools.partial(
            optimizer_kernel, terms=len(grads), vectors=len(vectors), held=len(before)
        ),
        grid=(1,),
        out_shape=[shape(*one.shape) for one in [*arrays, *vectors]],
        in_specs=[SMEM]
        + [pl.BlockSpec(one.shape, lambda step: (0, 0)) for one in grads]
        + [part(one) for one in arrays]
        + whole
        + [pl.BlockSpec(memory_space=pl.ANY)] * len(before),
        out_specs=[part(one) for one in arrays] + whole,
        input_output_aliases={len(inputs) + place: place for place in range(len(before))},
        scratch_shapes=[
            pltpu.VMEM(grads[0].shape, BF16),
            pltpu.VMEM((matrices, height, height), F32),
            pltpu.VMEM((matrices, height, 2 * height), BF16),
            pltpu.VMEM((matrices, height, 2 * height), BF16),
            pltpu.VMEM((count, side, height), F32),
        ],
        compiler_params=limit(24),
        cost_estimate=pl.CostEstimate(
            flops=matrices * NEWTON_TURNS * 8 * height**3, bytes_accessed=16 * MIB, transcendentals=0
        ),
        name="optimizer",
    )(*inputs, *before)


def own_rows(values, index, chunk):
    early = lax.dynamic_slice_in_dim(values, index * chunk, chunk, 0)
    late = lax.dynamic_slice_in_dim(values, (3 - index) * chunk, chunk, 0)
    return jnp.concatenate([early, late], axis=0)


def in_order(mine, other, index, chunk):
    inner = jnp.where(index == 0, other, mine)
    outer = jnp.where(index == 0, mine, other)
    return jnp.concatenate([outer[:chunk], inner, outer[chunk:]], axis=0)


def token_outputs(own_output, part_input, part_encoder, core, chunk):
    return (
        in_order(own_output, swapped(own_output), core, chunk),
        part_input.astype(F32) + swapped(part_input).astype(F32),
        part_encoder.astype(F32) + swapped(part_encoder).astype(F32),
    )


def key_bounds(key_ids, query_ids, chunk):
    rows = query_ids.reshape(-1, chunk)
    lowest = jnp.sum((key_ids[None] < rows[:, :1]).astype(jnp.int32), axis=1, keepdims=True)
    highest = jnp.sum((key_ids[None] <= rows[:, -1:]).astype(jnp.int32), axis=1, keepdims=True)
    return jnp.concatenate([lowest, highest + (chunk - 1)], axis=1) // chunk


def per_device(
    decoder_input,
    encoder_states,
    decoder_segments,
    encoder_segments,
    output_cotangent,
    block_slots,
    master,
    first_moment,
    second_moment,
    row_statistics,
    column_statistics,
    row_basis,
    column_basis,
    vectors,
    vector_first,
    vector_second,
):
    core = lax.axis_index("tensor")
    cores = lax.axis_size("tensor")
    ring, rings = lax.axis_index("dp"), lax.axis_size("dp")
    owned_count, block_height = master.shape[1], master.shape[2]
    vector_cols = vectors.shape[1]
    length, width = decoder_input.shape[1], decoder_input.shape[2]
    row_count = width // block_height
    block_total = block_slots.shape[0]
    column_count = block_total // row_count
    chunk = length // 4
    per_ring = owned_count * HD + VECTOR_ROWS
    group = block_height // vector_cols

    payload = low(master[0]).transpose(0, 2, 1).reshape(owned_count * HD, block_height)
    lane = jnp.arange(block_height) // vector_cols
    here = lane == ring % group
    small = jnp.where(here[None], jnp.tile(low(vectors), (1, group)), jnp.zeros((), BF16))
    small = jnp.pad(small, ((0, VECTOR_ROWS - vectors.shape[0]), (0, 0)))
    tokens, encoder_rows = decoder_input[0], encoder_states[0]
    ids, encoder_ids = decoder_segments[0], encoder_segments[0]
    own_tokens = own_rows(tokens, core, chunk)
    own_ids = own_rows(ids, core, chunk)
    own_cotangent = own_rows(output_cotangent[0], core, chunk)
    places = jnp.arange(length, dtype=jnp.int32)
    own_places = own_rows(places, core, chunk)
    self_allowed = (ids[:, None] == own_ids[None, :]) & (places[:, None] <= own_places[None, :])
    self_bias = jnp.where(self_allowed, 0.0, NEGATIVE).astype(F32)
    cross_bias = jnp.where(encoder_ids[:, None] == own_ids[None, :], 0.0, NEGATIVE).astype(F32)
    here_and_core = jnp.full((1,), core, jnp.int32)
    ends = jnp.stack([here_and_core + 1, 4 - here_and_core])
    self_edges = jnp.concatenate([key_bounds(ids, own_ids, chunk)[:, :1], ends], axis=1)
    self_scalars = jnp.concatenate([self_edges.reshape(-1), here_and_core])
    cross_edges = key_bounds(encoder_ids, own_ids, chunk)
    cross_scalars = jnp.concatenate([cross_edges.reshape(-1), here_and_core])

    payload = jnp.concatenate([payload, small], axis=0)
    owner, local = block_slots // owned_count, block_slots % owned_count
    chips = jnp.arange(rings, dtype=jnp.int32)
    grid_of_chips = rings == DEPTH * SIDE * SIDE
    if grid_of_chips:
        starts = apart(ring, owner, 1) * per_ring + local * HD
        slices = [(index ^ core) * rings * per_ring for index in range(cores)]
        ends = (apart(ring, chips, 1) + 1) * per_ring - VECTOR_ROWS
        early_count = owned_count // 2
        sizes = (early_count * HD, per_ring - early_count * HD)
        order = jnp.array(PLACES, jnp.int32)
        late = local // early_count
        sum_rows = local % early_count * HD + jnp.where(
            late == 1,
            rings * sizes[0] + order[apart(ring, owner, -1)] * sizes[1],
            order[apart(ring, owner, -1)] * sizes[0],
        )
        sum_ends = rings * sizes[0] + (order[apart(ring, chips, -1)] + 1) * sizes[1] - VECTOR_ROWS
    else:
        starts = owner * cores * per_ring + local * HD
        slices = [index * per_ring for index in range(cores)]
        ends = (chips * cores + 1) * per_ring - VECTOR_ROWS
        sum_rows = owner * per_ring + local * HD
        sum_ends = (chips + 1) * per_ring - VECTOR_ROWS
    starts = jnp.concatenate([starts + start for start in slices])
    beside = (starts, ends, own_tokens, own_cotangent, self_bias, cross_bias)
    beside += (self_scalars, cross_scalars, sum_rows, sum_ends)
    if grid_of_chips:
        pieces, beside = gather_chips(payload, beside)
        pieces += [swapped(piece) for piece in pieces]
    else:
        pieces = [lax.all_gather(payload, ("dp", "tensor"), axis=0, tiled=True)]
    starts, ends, own_tokens, own_cotangent, self_bias, cross_bias, *scalars = beside
    self_scalars, cross_scalars, sum_rows, sum_ends = scalars
    layer = call_layer(
        (self_scalars, cross_scalars, starts, ends),
        pieces,
        (tokens, own_tokens, self_bias, encoder_rows, cross_bias, own_cotangent),
        cores,
        group,
    )
    own_output, ff_mine, ff_sent, cross_mine, cross_sent, part_encoder, grad_one, norms = layer[:8]
    w_self, q_self, k_self, lse_self, ctxt_self = layer[8:]
    self_mine, self_sent, part_input = call_self_backward(
        self_scalars,
        (grad_one, ctxt_self, w_self, q_self, tokens, own_tokens, k_self, lse_self, self_bias),
    )

    terms = [ff_mine, ff_sent, cross_mine, cross_sent, self_mine, self_sent]
    terms = [one if number % 2 == 0 else swapped(one) for number, one in enumerate(terms)]
    terms += [norms, swapped(norms)]
    shift = ((block_height - ring % group * vector_cols) % block_height)[None]
    arrays = [one[0].transpose(0, 2, 1) for one in (master, first_moment, second_moment)]
    arrays += [
        one[0] for one in (row_statistics, column_statistics, row_basis, column_basis)
    ]
    vector_states = [vectors, vector_first, vector_second]
    if grid_of_chips:
        cuts = [size * places for size in sizes for places in (4, 4, 2, 2, 4)]
        parts = scatter(sum_rows, sum_ends, terms, cuts, cores, block_height, group)
        own_output, part_encoder, part_input, parts = lax.optimization_barrier(
            (own_output, part_encoder, part_input, parts)
        )
        tokens_out = token_outputs(own_output, part_input, part_encoder, core, chunk)
        column, tokens_out = reduce_plane(*parts[:5], tokens_out)
        block_output, input_gradient, encoder_gradient = tokens_out
        column, parts = lax.optimization_barrier((column, parts[5:]))
        column, early = reduce_plane(*parts, reduce_column(column))
        updated = optimize(shift, early, arrays, 0, early_count, [], [])
        updated = optimize(
            shift, reduce_column(column), arrays, 1, early_count, vector_states, updated
        )
    else:
        (whole,) = scatter(
            sum_rows,
            sum_ends,
            terms,
            [rings * per_ring],
            cores,
            block_height,
            group,
        )
        summed = lax.psum_scatter(whole, "dp", scatter_dimension=0, tiled=True)
        updated = optimize(shift, [summed], arrays, 0, owned_count, vector_states, [])
        tokens_out = token_outputs(own_output, part_input, part_encoder, core, chunk)
        block_output, input_gradient, encoder_gradient = tokens_out

    return (
        block_output[None],
        input_gradient[None],
        encoder_gradient[None],
        *[one.transpose(0, 2, 1)[None] for one in updated[:3]],
        *[one[None] for one in updated[3:7]],
        *updated[7:],
    )


def solution(mesh):
    blocks = P("tensor", "dp", None, None)
    rows = P("dp", None, None)
    return jax.shard_map(
        per_device,
        mesh=mesh,
        in_specs=(rows, rows, P("dp", None), P("dp", None), rows, P())
        + (blocks,) * 7
        + (P(None, "dp"),) * 3,
        out_specs=(rows,) * 3 + (blocks,) * 7 + (P(None, "dp"),) * 3,
        check_vma=False,
    )
```

```python
import functools

import jax
import jax.numpy as jnp
from jax import lax
from jax.experimental import pallas as pl
from jax.experimental.pallas import tpu as pltpu
from jax.sharding import PartitionSpec as P

HD = 64
FF = 2048
STEP = 10

NEGATIVE = -1e30
EPS_NORM = 1e-05
MOMENT_DECAY = 0.5
LEARN_RATE = 0.04
WEIGHT_DECAY = 0.01
VECTOR_RATE = 0.25
ADAM_EPS = 1e-08
NEWTON_TURNS = 8
EARLY_TURNS = 5
VECTOR_ROWS = 16
DEPTH, SIDE = 4, 2
MIB = 2**20
F32 = jnp.float32
BF16 = jnp.bfloat16
VMEM = pl.BlockSpec(memory_space=pltpu.VMEM)
SMEM = pl.BlockSpec(memory_space=pltpu.SMEM)
ANY = pl.BlockSpec(memory_space=pl.ANY)


def nn(left, right):
    return lax.dot_general(left, right, (((1,), (0,)), ((), ())), preferred_element_type=F32)


def nt(left, right):
    return lax.dot_general(left, right, (((1,), (1,)), ((), ())), preferred_element_type=F32)


def tn(left, right):
    return lax.dot_general(left, right, (((0,), (0,)), ((), ())), preferred_element_type=F32)


def low(values):
    return values.astype(BF16)


def span(number, size):
    return slice(number * size, (number + 1) * size)


def rows_at(number, size):
    return pl.ds(pl.multiple_of(number * size, size), size)


def shape(*dims, dtype=F32):
    return jax.ShapeDtypeStruct(dims, dtype)


def scratch(shapes):
    return [pltpu.VMEM(one.shape, one.dtype) for one in shapes]


def limit(mib):
    return pltpu.CompilerParams(vmem_limit_bytes=mib * MIB)


def block_places(columns, cores):
    hidden = FF // cores // HD
    heads = (columns - 2 * hidden) // 8
    places = []
    for column in range(columns):
        if column < 8 * heads:
            places.append((column // heads, column % heads * HD))
        else:
            column -= 8 * heads
            places.append((8 + column // hidden, column % hidden * HD))
    return places, heads * HD, hidden * HD


def start_copies(pairs, semaphores, first=0):
    copies = [
        pltpu.make_async_copy(source, target, semaphores.at[first + number])
        for number, (source, target) in enumerate(pairs)
    ]
    for copy in copies:
        copy.start()
    return copies


def wait_for(copies):
    for copy in copies:
        copy.wait()


def in_a_row(pieces, target_ref):
    pairs, start = [], 0
    for piece in pieces:
        pairs.append((piece, target_ref.at[pl.ds(start, piece.shape[0])]))
        start += piece.shape[0]
    return pairs


def assemble(rows_ref, ends_ref, gathered_ref, w_refs, vec_ref, cores, group):
    height = gathered_ref.shape[1]
    row_count = vec_ref.shape[1] // height
    total = rows_ref.shape[0] // cores
    columns = total // row_count
    places, head_rows, hidden_rows = block_places(columns, cores)
    for core in range(cores):
        for row in range(row_count):
            for column in range(columns):
                kind, inner = places[column]
                size = head_rows if kind < 8 else hidden_rows
                target = (kind % 4 * cores + core) * size + inner
                source = pl.multiple_of(rows_ref[core * total + row * columns + column], 16)
                block = gathered_ref[pl.ds(source, HD), :]
                w_refs[kind // 4][target : target + HD, span(row, height)] = block
    rings = ends_ref.shape[0]
    for part in range(row_count):
        values = jnp.zeros((VECTOR_ROWS, height), F32)
        for ring in range(part * group, min((part + 1) * group, rings)):
            start = pl.multiple_of(ends_ref[ring], 16)
            values = values + gathered_ref[pl.ds(start, VECTOR_ROWS), :].astype(F32)
        vec_ref[:, span(part, height)] = values


def scatter_kernel(rows_ref, ends_ref, *refs, cores, group, cuts):
    ins, (vec_ref, vec_in_ref), refs = refs[:6], refs[6:8], refs[8:]
    outs, refs = refs[:cuts], refs[cuts:]
    terms, (all_ref, in_sems, out_sems) = refs[:6], refs[6:]
    copies = start_copies(zip(ins, terms), in_sems)
    height = all_ref.shape[1]
    row_count = vec_ref.shape[1] // height
    columns = rows_ref.shape[0] // row_count
    places, head_rows, hidden_rows = block_places(columns, cores)
    for part, (first, last, size) in enumerate(
        ((8, 10, hidden_rows), (4, 8, head_rows), (0, 4, head_rows))
    ):
        one, two = terms[2 * part : 2 * part + 2]
        wait_for(copies[2 * part : 2 * part + 2])
        for column in range(columns):
            kind, inner = places[column]
            if first <= kind < last:
                start = (kind - first) * size + inner
                for row in range(row_count):
                    here = slice(start, start + HD), span(row, height)
                    target = pl.multiple_of(rows_ref[row * columns + column], 16)
                    total = one[here].astype(F32) + two[here].astype(F32)
                    all_ref[pl.ds(target, HD), :] = low(total)
    total = low(vec_ref[...] + vec_in_ref[...])
    for ring in range(ends_ref.shape[0]):
        start = pl.multiple_of(ends_ref[ring], 16)
        all_ref[pl.ds(start, VECTOR_ROWS), :] = total[:, span(ring // group, height)]
    pairs = [(part, out) for out, part in in_a_row(outs, all_ref)]
    wait_for(start_copies(pairs, out_sems))


def scatter(rows, ends, terms, cuts, cores, height, group):
    return pl.pallas_call(
        functools.partial(scatter_kernel, cores=cores, group=group, cuts=len(cuts)),
        out_shape=[shape(cut, height, dtype=BF16) for cut in cuts],
        in_specs=[SMEM, SMEM] + [ANY] * 6 + [VMEM] * 2,
        out_specs=[ANY] * len(cuts),
        scratch_shapes=scratch(terms[:6])
        + [
            pltpu.VMEM((sum(cuts), height), BF16),
            pltpu.SemaphoreType.DMA((6,)),
            pltpu.SemaphoreType.DMA((len(cuts),)),
        ],
        compiler_params=limit(60),
        name="scatter",
    )(rows, ends, *terms)


def hop(values, *steps):
    sizes = (DEPTH, SIDE, SIDE)
    pairs = []
    for source in range(DEPTH * SIDE * SIDE):
        place = (source // (SIDE * SIDE), source // SIDE % SIDE, source % SIDE)
        z, y, x = ((one + step) % size for one, step, size in zip(place, steps, sizes))
        pairs.append((source, (z * SIDE + y) * SIDE + x))
    return lax.ppermute(values, "dp", pairs)


def swapped(values):
    return lax.ppermute(values, "tensor", [(0, 1), (1, 0)])


def apart(ring, other, sign):
    side = SIDE * SIDE
    deep = (sign * (ring // side - other // side)) % DEPTH
    across = (ring // SIDE % SIDE) ^ (other // SIDE % SIDE)
    return (across * SIDE + ((ring % SIDE) ^ (other % SIDE))) * DEPTH + deep


def gather_chips(own, beside):
    deep = [hop(own, step, 0, 0) for step in range(1, DEPTH)]
    near = [hop(own, 0, 0, 1), hop(own, 0, 1, 0), hop(own, 0, 1, 1)]
    deep, near, beside = lax.optimization_barrier((jnp.concatenate(deep, axis=0), near, beside))
    by_x, by_y = hop(deep, 0, 0, 1), hop(deep, 0, 1, 0)
    cut = deep.shape[0] // 32 * 16
    pieces = [own, deep, near[0], by_x, near[1], by_y, near[2]]
    return pieces + [hop(by_y[:cut], 0, 0, 1), hop(by_x[cut:], 0, 1, 0)], beside


PLACES = (12, 13, 14, 15, 2, 3, 10, 11, 8, 9, 6, 7, 0, 1, 4, 5)


def fold(*terms):
    return low(functools.reduce(lambda one, two: one + two, [term.astype(F32) for term in terms]))


def reduce_plane(along_x, along_y, late_y, late_x, here, beside):
    half = late_x.shape[0]
    from_x, from_y = hop(along_x, 0, 0, 1), hop(along_y, 0, 1, 0)
    from_x, from_y, beside = lax.optimization_barrier((from_x, from_y, beside))
    more_y = hop(fold(late_y, from_x[:half]), 0, 1, 0)
    more_x = hop(fold(late_x, from_y[:half]), 0, 0, 1)
    column = jnp.concatenate(
        [fold(here[:half], from_x[half:], more_y), fold(here[half:], from_y[half:], more_x)],
        axis=0,
    )
    return column, beside


def reduce_column(column):
    rows = column.shape[0] // DEPTH
    return [column[:rows]] + [
        hop(column[step * rows : (step + 1) * rows], step, 0, 0) for step in range(1, DEPTH)
    ]


def norm_forward(total_ref, vec_ref, first, hat_ref, inverse_ref, out_ref, step=64):
    gain, shift = vec_ref[first : first + 1], vec_ref[first + 1 : first + 2]

    def body(number, carry):
        rows = rows_at(number, step)
        values = total_ref[rows]
        center = values - jnp.mean(values, axis=1, keepdims=True)
        inverse = lax.rsqrt(jnp.mean(center * center, axis=1, keepdims=True) + EPS_NORM)
        hat = center * inverse
        hat_ref[rows] = hat
        inverse_ref[rows] = inverse
        out_ref[rows] = (hat * gain + shift).astype(out_ref.dtype)
        return carry

    lax.fori_loop(0, total_ref.shape[0] // step, body, 0, unroll=8)


def norm_backward(grad_ref, hat_ref, inverse_ref, gain, out_ref, step=64):
    width = grad_ref.shape[1]

    def body(number, carry):
        rows = rows_at(number, step)
        grad, hat = grad_ref[rows].astype(F32), hat_ref[rows]
        scaled = grad * gain
        middle = jnp.mean(scaled, axis=1, keepdims=True)
        slope = jnp.mean(scaled * hat, axis=1, keepdims=True)
        out_ref[rows] = (scaled - middle - hat * slope) * inverse_ref[rows]
        return (
            carry[0] + jnp.sum((grad * hat).reshape(step // 8, 8, width), axis=0),
            carry[1] + jnp.sum(grad.reshape(step // 8, 8, width), axis=0),
        )

    zeros = jnp.zeros((8, width), F32)
    sums = lax.fori_loop(0, grad_ref.shape[0] // step, body, (zeros, zeros), unroll=8)
    return [jnp.sum(one, axis=0, keepdims=True) for one in sums]


def split_heads(source_ref, masked_ref, factor):
    for head in range(masked_ref.shape[0]):
        pair = source_ref[:, span(head // 2, 2 * HD)]
        lane = lax.broadcasted_iota(jnp.int32, pair.shape, 1)
        here = (lane >= HD) if head % 2 else (lane < HD)
        masked_ref[head] = jnp.where(here, pair, jnp.zeros_like(pair)) * jnp.asarray(factor, BF16)


def staged(count, early, middle, late, ahead=2, lag=2):
    ready = [early(number) for number in range(min(ahead, count))]
    held = []
    for number in range(count):
        now = ready.pop(0)
        if number + ahead < count:
            ready.append(early(number + ahead))
        held.append((number, middle(number, now)))
        if len(held) > lag:
            late(*held.pop(0))
    while held:
        late(*held.pop(0))


def attend_forward(bounds_ref, bias_ref, masked_q, k_ref, vt_ref, m_ref, l_ref, acc_ref, lse_ref,
                   ctxt_ref):
    heads, chunk = m_ref.shape
    for part in range(lse_ref.shape[1] // chunk):
        cols = span(part, chunk)
        m_ref[...] = jnp.full(m_ref.shape, NEGATIVE, F32)
        l_ref[...] = jnp.zeros(l_ref.shape, F32)
        acc_ref[...] = jnp.zeros(acc_ref.shape, F32)

        def body(number, carry):
            keys = rows_at(number, chunk)
            bias = bias_ref[keys, cols]

            def early(head):
                return nt(k_ref[keys, span(head // 2, 2 * HD)], masked_q[head, cols]) + bias

            def middle(head, scores):
                row = slice(head, head + 1)
                before = m_ref[row]
                highest = jnp.maximum(before, jnp.max(scores, axis=0, keepdims=True))
                shrink = jnp.exp(before - highest)
                expons = jnp.exp(scores - highest)
                l_ref[row] = l_ref[row] * shrink + jnp.sum(expons, axis=0, keepdims=True)
                m_ref[row] = highest
                return shrink, low(expons)

            def late(head, pair):
                rows = span(head, HD)
                acc_ref[rows] = acc_ref[rows] * pair[0] + nn(vt_ref[rows, keys], pair[1])

            staged(heads, early, middle, late)
            return carry

        lax.fori_loop(bounds_ref[2 * part], bounds_ref[2 * part + 1], body, 0)
        for head in range(heads):
            rows = span(head, HD)
            ctxt_ref[rows, cols] = low(acc_ref[rows] / l_ref[head : head + 1])
        lse_ref[:, cols] = m_ref[...] + jnp.log(l_ref[...])


def branch_forward(bounds_ref, x_ref, own_ref, w_ref, bias_ref, vec_ref,
                   q_ref, k_ref, lse_ref, ctxt_ref, hat_ref, inverse_ref, y_ref, first):
    keys, width = k_ref.shape
    heads, queries = lse_ref.shape
    chunk = keys // 4

    def body(masked_q, vt_ref, m_ref, l_ref, acc_ref):
        q_ref[...] = low(nt(low(own_ref[...]), w_ref[span(0, width)]))
        split_heads(q_ref, masked_q, HD**-0.5)
        k_ref[...] = low(nt(x_ref[...], w_ref[span(1, width)]))
        vt_ref[...] = low(nt(w_ref[span(2, width)], x_ref[...]))
        attend_forward(
            bounds_ref, bias_ref, masked_q, k_ref, vt_ref, m_ref, l_ref, acc_ref, lse_ref, ctxt_ref
        )
        y_ref[...] = own_ref[...].astype(F32) + tn(ctxt_ref[...], w_ref[span(3, width)])
        norm_forward(y_ref, vec_ref, first, hat_ref, inverse_ref, y_ref)

    pl.run_scoped(
        body,
        pltpu.VMEM((heads, queries, 2 * HD), BF16),
        pltpu.VMEM((width, keys), BF16),
        pltpu.VMEM((heads, chunk), F32),
        pltpu.VMEM((heads, chunk), F32),
        pltpu.VMEM((width, chunk), F32),
    )


def branch_backward(scalars_ref, x_ref, own_ref, w_ref, bias_ref, grad_ref, q_ref, k_ref, lse_ref,
                    ctxt_ref, mine_ref, sent_ref, part_ref, norm, arrive):
    heads, queries = lse_ref.shape
    keys, width = k_ref.shape
    chunk = queries // 2

    def body(masked_q, masked_g, v_ref, kt_ref, delta_ref, dqt_ref, dk_ref, dv_ref, dq_ref, out_ref):
        core = scalars_ref[4]
        half = width // 2
        arrive(0)

        def keep(kind, gradient):
            out_ref[...] = low(gradient)
            mine_ref[span(kind, half)] = out_ref[rows_at(core, half)]
            sent_ref[span(kind, half)] = out_ref[rows_at(1 - core, half)]

        grad_low = low(grad_ref[...])
        w_out = w_ref[span(3, width)]
        keep(3, nn(ctxt_ref[...], grad_low))
        out_ref[...] = low(nt(grad_low, w_out))
        split_heads(out_ref, masked_g, 1.0)
        arrive(1)
        split_heads(q_ref, masked_q, HD**-0.5)
        grad_t = low(nt(w_out, grad_low)).astype(F32) * ctxt_ref[...].astype(F32)
        for head in range(heads):
            delta_ref[head : head + 1] = jnp.sum(grad_t[span(head, HD)], axis=0, keepdims=True)
        v_ref[...] = low(nt(x_ref[...], w_ref[span(2, width)]))
        kt_ref[...] = low(nt(w_ref[span(1, width)], x_ref[...]))
        dqt_ref[...] = jnp.zeros(dqt_ref.shape, F32)
        dk_ref[...] = jnp.zeros(dk_ref.shape, F32)
        dv_ref[...] = jnp.zeros(dv_ref.shape, F32)
        for part in range(2):
            cols = span(part, chunk)

            def pair(number, carry):
                keys = rows_at(number, chunk)
                bias = bias_ref[keys, cols]

                def early(head):
                    pair = span(head // 2, 2 * HD)
                    return (
                        nt(k_ref[keys, pair], masked_q[head, cols]) + bias,
                        nt(v_ref[keys, pair], masked_g[head, cols]),
                    )

                def middle(head, both):
                    row = slice(head, head + 1)
                    chances = jnp.exp(both[0] - lse_ref[row, cols])
                    return low(chances), low(chances * (both[1] - delta_ref[row, cols]))

                def late(head, both):
                    pair, rows = span(head // 2, 2 * HD), span(head, HD)
                    dv_ref[keys, pair] += nn(both[0], masked_g[head, cols])
                    dk_ref[keys, pair] += nn(both[1], masked_q[head, cols])
                    dqt_ref[rows, cols] += nn(kt_ref[rows, keys], both[1])

                staged(heads, early, middle, late)
                return carry

            lax.fori_loop(scalars_ref[2 * part], scalars_ref[2 * part + 1], pair, 0)
        dqt = low(dqt_ref[...] * HD**-0.5)
        keep(0, nn(dqt, low(own_ref[...])))
        dk, dv = low(dk_ref[...]), low(dv_ref[...])
        keep(1, tn(dk, x_ref[...]))
        keep(2, tn(dv, x_ref[...]))
        dq_ref[...] = grad_ref[...] + tn(dqt, w_ref[span(0, width)])
        if norm is not None:
            part_ref[...] = low(nn(dk, w_ref[span(1, width)]) + nn(dv, w_ref[span(2, width)]))
            hat_ref, inverse_ref, gain, next_ref, norms_ref, place = norm
            sums = norm_backward(dq_ref, hat_ref, inverse_ref, gain, next_ref)
            norms_ref[place : place + 1] = sums[0]
            norms_ref[place + 1 : place + 2] = sums[1]
        else:
            dk_ref[...] = nn(dk, w_ref[span(1, width)]) + nn(dv, w_ref[span(2, width)])
            for part, place in enumerate((core, 3 - core)):
                dk_ref[rows_at(place, chunk)] += dq_ref[span(part, chunk)]
            part_ref[...] = low(dk_ref[...])

    pl.run_scoped(
        body,
        pltpu.VMEM((heads, queries, 2 * HD), BF16),
        pltpu.VMEM((heads, queries, 2 * HD), BF16),
        pltpu.VMEM((keys, width), BF16),
        pltpu.VMEM((width, keys), BF16),
        pltpu.VMEM((heads, queries), F32),
        pltpu.VMEM((width, queries), F32),
        pltpu.VMEM((keys, width), F32),
        pltpu.VMEM((keys, width), F32),
        pltpu.VMEM((queries, width), F32),
        pltpu.VMEM((width, width), BF16),
    )


def gelu_both(values):
    scale = (2.0 / jnp.pi) ** 0.5
    square = values * values
    bend = jnp.tanh(values * (scale + scale * 0.044715 * square))
    half = 0.5 + 0.5 * bend
    slope = half + (0.5 * values) * (1.0 - bend * bend) * (scale + 3.0 * scale * 0.044715 * square)
    return values * half, slope


def feed_both(core, y_ref, w_ref, vec_ref, cot_ref, hat_two, inverse_two,
              block_ref, next_ref, mine_ref, sent_ref, norms_ref, arrive, step=256):
    queries, width = y_ref.shape
    hidden = w_ref.shape[0] // 2
    half = hidden // 2
    chunks = hidden // step

    def body(low_ref, hid_ref, slope_ref, total_ref, hat_ref, inverse_ref, grad_low):
        low_ref[...] = low(y_ref[...])
        total_ref[...] = y_ref[...]

        def early(number):
            return nt(w_ref[span(number, step)], low_ref[...])

        def middle(number, up):
            hid, slope = gelu_both(up)
            hid_ref[span(number, step)] = low(hid)
            slope_ref[span(number, step)] = slope

        def late(number, _):
            lower = w_ref[hidden + number * step : hidden + (number + 1) * step]
            total_ref[...] += tn(hid_ref[span(number, step)], lower)

        staged(chunks, early, middle, late, 1, 1)
        norm_forward(total_ref, vec_ref, 4, hat_ref, inverse_ref, block_ref)
        sums = norm_backward(cot_ref, hat_ref, inverse_ref, vec_ref[4:5], total_ref)
        norms_ref[4:5] = sums[0]
        norms_ref[5:6] = sums[1]
        grad_low[...] = low(total_ref[...])

        def place(number):
            inner = number % (chunks // 2)
            row = (core if number < chunks // 2 else 1 - core) * half + inner * step
            return inner, pl.multiple_of(row, step)

        def down(number):
            row = place(number)[1]
            return nt(w_ref[pl.ds(pl.multiple_of(hidden + row, step), step)], grad_low[...])

        def turn(number, grad_hidden):
            return low(slope_ref[pl.ds(place(number)[1], step)] * grad_hidden)

        def sums_of(number, grad_up):
            inner, row = place(number)
            rows = pl.ds(row, step)
            kept = mine_ref if number < chunks // 2 else sent_ref
            kept[span(inner, step)] = low(nn(grad_up, low_ref[...]))
            kept[half + inner * step : half + (inner + 1) * step] = low(nn(hid_ref[rows], grad_low[...]))
            total_ref[...] += tn(grad_up, w_ref[rows])

        staged(chunks, down, turn, sums_of, 1, 1)
        sums = norm_backward(total_ref, hat_two, inverse_two, vec_ref[2:3], next_ref)
        norms_ref[2:3] = sums[0]
        norms_ref[3:4] = sums[1]

    pl.run_scoped(
        body,
        pltpu.VMEM((queries, width), BF16),
        pltpu.VMEM((hidden, queries), BF16),
        pltpu.VMEM((hidden, queries), F32),
        pltpu.VMEM((queries, width), F32),
        pltpu.VMEM((queries, width), F32),
        pltpu.VMEM((queries, 1), F32),
        pltpu.VMEM((queries, width), BF16),
    )


def layer_kernel(self_ref, cross_ref, rows_ref, ends_ref, *refs, cores, group, pieces):
    gathered, refs = refs[:pieces], refs[pieces:]
    ins, refs = refs[:6], refs[6:]
    block_out, ff_mine_out, ff_sent_out, mine_out, sent_out, part_out, next_out = refs[:7]
    norms_ref, w_out, q_out, k_out, lse_out, ctxt_out = refs[7:13]
    w_self, w_cross, w_feed, vec_ref, x_ref, own_ref, bias_ref, enc_ref, bias_cross, cot_ref = refs[13:23]
    self_saved, refs = refs[23:27], refs[27:]
    cross_saved, refs = refs[:4], refs[4:]
    hat_one, inverse_one, y_one, hat_two, inverse_two, y_two, refs = *refs[:6], refs[6:]
    block_ref, ff_mine, ff_sent, mine_ref, sent_ref, part_ref, grad_ref, next_ref = refs[:8]
    piece_sems, in_sems, out_sems = refs[8:]
    norms_ref[...] = jnp.zeros(norms_ref.shape, F32)

    targets = (x_ref, own_ref, bias_ref, enc_ref, bias_cross, cot_ref)

    def fetch(gathered_ref):
        arriving = start_copies(in_a_row(gathered, gathered_ref), piece_sems)
        start_copies(zip(ins, targets), in_sems)
        wait_for(arriving)
        assemble(
            rows_ref, ends_ref, gathered_ref, (w_self, w_cross, w_feed), vec_ref, cores, group
        )

    total = sum(piece.shape[0] for piece in gathered)
    pl.run_scoped(fetch, pltpu.VMEM((total, gathered[0].shape[1]), BF16))
    arriving = [
        pltpu.make_async_copy(source, target, in_sems.at[number])
        for number, (source, target) in enumerate(zip(ins, targets))
    ]
    wait_for(arriving[:3])
    leaving = start_copies([(w_self, w_out)], out_sems)
    branch_forward(
        self_ref, x_ref, own_ref, w_self, bias_ref, vec_ref, *self_saved, hat_one, inverse_one,
        y_one, 0,
    )
    leaving += start_copies(zip(self_saved, (q_out, k_out, lse_out, ctxt_out)), out_sems, 1)
    wait_for(arriving[3:5])
    branch_forward(
        cross_ref, enc_ref, y_one, w_cross, bias_cross, vec_ref, *cross_saved, hat_two, inverse_two,
        y_two, 2,
    )
    wait_for(arriving[5:])
    feed_both(
        self_ref[4], y_two, w_feed, vec_ref, cot_ref, hat_two, inverse_two, block_ref, grad_ref,
        ff_mine, ff_sent, norms_ref, None,
    )
    pairs = [(block_ref, block_out), (ff_mine, ff_mine_out), (ff_sent, ff_sent_out)]
    leaving += start_copies(pairs, out_sems, 5)
    branch_backward(
        cross_ref, enc_ref, y_one, w_cross, bias_cross, grad_ref, *cross_saved, mine_ref, sent_ref,
        part_ref, (hat_one, inverse_one, vec_ref[0:1], next_ref, norms_ref, 0), lambda number: None,
    )
    pairs = [(mine_ref, mine_out), (sent_ref, sent_out), (part_ref, part_out), (next_ref, next_out)]
    leaving += start_copies(pairs, out_sems, 8)
    wait_for(leaving)


def saved_shapes(keys, queries, width):
    heads = width // HD
    return [
        shape(queries, width, dtype=BF16),
        shape(keys, width, dtype=BF16),
        shape(heads, queries),
        shape(width, queries, dtype=BF16),
    ]


def call_layer(scalars, pieces, inputs, cores, group):
    keys, queries = inputs[2].shape
    width = inputs[0].shape[1]
    saved = saved_shapes(keys, queries, width)
    weights = shape(4 * width, width, dtype=BF16)
    tokens = shape(queries, width)
    norm = [tokens, shape(queries, 1), tokens]
    outs = [
        shape(queries, width, dtype=BF16),
        shape(FF, width, dtype=BF16),
        shape(FF, width, dtype=BF16),
        shape(2 * width, width, dtype=BF16),
        shape(2 * width, width, dtype=BF16),
        shape(keys, width, dtype=BF16),
        tokens,
    ]
    kept = [weights, weights, shape(2 * FF, width, dtype=BF16), shape(VECTOR_ROWS, width)]
    kept += [*inputs, *saved, *saved, *norm, *norm, *outs[:6], tokens, tokens]
    norms = shape(VECTOR_ROWS, width)
    return pl.pallas_call(
        functools.partial(layer_kernel, cores=cores, group=group, pieces=len(pieces)),
        out_shape=[*outs, norms, weights, *saved],
        in_specs=[SMEM] * 4 + [ANY] * (len(pieces) + len(inputs)),
        out_specs=[ANY] * 7 + [VMEM] + [ANY] * 5,
        scratch_shapes=scratch(kept)
        + [
            pltpu.SemaphoreType.DMA((len(pieces),)),
            pltpu.SemaphoreType.DMA((6,)),
            pltpu.SemaphoreType.DMA((12,)),
        ],
        compiler_params=limit(56),
        name="layer",
    )(*scalars, *pieces, *inputs)


def self_backward_kernel(scalars_ref, *refs):
    ins, (mine_out, sent_out, part_out), refs = refs[:9], refs[9:12], refs[12:]
    grad_ref, ctxt_ref, w_ref, q_ref, x_ref, own_ref, k_ref, lse_ref, bias_ref = refs[:9]
    mine_ref, sent_ref, part_ref, in_sems, out_sems = refs[9:]
    copies = start_copies(zip(ins, refs[:9]), in_sems)
    branch_backward(
        scalars_ref, x_ref, own_ref, w_ref, bias_ref, grad_ref, q_ref, k_ref, lse_ref, ctxt_ref,
        mine_ref, sent_ref, part_ref, None,
        lambda number: wait_for(copies[3:] if number else copies[:3]),
    )
    pairs = [(mine_ref, mine_out), (sent_ref, sent_out), (part_ref, part_out)]
    wait_for(start_copies(pairs, out_sems))


def call_self_backward(scalars, inputs):
    keys, width = inputs[4].shape
    outs = [
        shape(2 * width, width, dtype=BF16),
        shape(2 * width, width, dtype=BF16),
        shape(keys, width, dtype=BF16),
    ]
    return pl.pallas_call(
        self_backward_kernel,
        out_shape=outs,
        in_specs=[SMEM] + [ANY] * 9,
        out_specs=[ANY] * 3,
        scratch_shapes=scratch([*inputs, *outs])
        + [pltpu.SemaphoreType.DMA((9,)), pltpu.SemaphoreType.DMA((3,))],
        compiler_params=limit(62),
        cost_estimate=pl.CostEstimate(
            flops=12 * 10**9, bytes_accessed=12 * MIB, transcendentals=0
        ),
        name="self_backward",
    )(scalars, *inputs)


def halves(values):
    high = low(values)
    return high, low(values - high.astype(F32))


def fine(dot, left, right):
    left_high, left_low = halves(left)
    right_high, right_low = halves(right)
    return dot(left_high, right_high) + (dot(left_high, right_low) + dot(left_low, right_high))


def newton_turn(x_ref, s_ref, z_ref):
    count, size = x_ref.shape[0], x_ref.shape[1]
    for number in range(count):
        high, rest = halves(x_ref[number])
        z_ref[number] = jnp.concatenate([high, rest], axis=1)
        right = jnp.concatenate(
            [jnp.concatenate([high, high], axis=1), jnp.concatenate([rest, rest], axis=1)], axis=0
        )
        product = nt(z_ref[number], right)
        high, rest = halves(product[:, :size] + product[:, size:])
        s_ref[number] = jnp.concatenate([high, rest], axis=1)
    for number in range(count):
        terms = z_ref[number]
        product = nn(s_ref[number], jnp.concatenate([terms, terms], axis=0))
        x_ref[number] = 1.5 * x_ref[number] - 0.5 * (product[:, :size] + product[:, size:])


def early_turn(x_ref, s_ref, z_ref):
    count, size = x_ref.shape[0], x_ref.shape[1]
    for number in range(count):
        high = low(x_ref[number])
        z_ref[number, :, :size] = high
        s_ref[number, :, :size] = low(nt(high, high))
    for number in range(count):
        product = nn(s_ref[number, :, :size], z_ref[number, :, :size])
        x_ref[number] = 1.5 * x_ref[number] - 0.5 * product


def adam_terms(gradient, first, second):
    first_new = MOMENT_DECAY * first + (1.0 - MOMENT_DECAY) * gradient
    second_new = MOMENT_DECAY * second + (1.0 - MOMENT_DECAY) * gradient * gradient
    correction = 1.0 - MOMENT_DECAY**STEP
    direction = first_new / correction / (jnp.sqrt(second_new / correction) + ADAM_EPS)
    return first_new, second_new, direction


def optimizer_kernel(shift_ref, *refs, terms, vectors, held):
    grads, refs = refs[:terms], refs[terms:]
    master_ref, first_ref, second_ref, left_ref, right_ref, left_basis, right_basis = refs[:7]
    vec_in, refs = refs[7 : 7 + vectors], refs[7 + vectors + held :]
    new_master, new_first, new_second, new_left, new_right = refs[:5]
    new_left_basis, new_right_basis = refs[5:7]
    vec_out, (g_ref, x_ref, s_ref, z_ref, p_ref) = refs[7 : 7 + vectors], refs[7 + vectors :]
    count, side, height = master_ref.shape
    keep = MOMENT_DECAY

    def unit(matrix):
        total = jnp.sum(jnp.sum(matrix * matrix, axis=1, keepdims=True), axis=0, keepdims=True)
        return matrix * lax.rsqrt(total + 1e-06)

    g_ref[...] = fold(*[one[...] for one in grads])
    for pair in range((count + 1) // 2):
        x_ref[count + pair] = jnp.zeros((height, height), F32)
    for block in range(count):
        gradient = g_ref[span(block, side)]
        new_left[block] = keep * left_ref[block] + (1.0 - keep) * tn(gradient, gradient)
        new_right[block] = keep * right_ref[block] + (1.0 - keep) * nt(gradient, gradient)
    for block in range(count):
        x_ref[block] = unit(fine(nn, new_left[block], left_basis[block]))
        corner = span(block % 2, side)
        x_ref[count + block // 2, corner, corner] = unit(
            fine(nn, new_right[block], right_basis[block])
        )

    def rough(number, carry):
        early_turn(x_ref, s_ref, z_ref)
        return carry

    def turn(number, carry):
        newton_turn(x_ref, s_ref, z_ref)
        return carry

    lax.fori_loop(0, EARLY_TURNS, rough, 0, unroll=True)
    lax.fori_loop(EARLY_TURNS, NEWTON_TURNS, turn, 0, unroll=True)
    for block in range(count):
        corner = span(block % 2, side)
        new_left_basis[block] = x_ref[block]
        new_right_basis[block] = x_ref[count + block // 2, corner, corner]
    for block in range(count):
        high, rest = halves(new_left_basis[block])
        gradient = g_ref[span(block, side)]
        partway = nn(gradient, high) + nn(gradient, rest)
        turned = fine(tn, new_right_basis[block], partway)
        new_first[block], new_second[block], p_ref[block] = adam_terms(
            turned, first_ref[block], second_ref[block]
        )
    for block in range(count):
        partback = fine(nn, new_right_basis[block], p_ref[block])
        step = fine(nt, partback, new_left_basis[block])
        new_master[block] = (
            master_ref[block] * (1.0 - LEARN_RATE * WEIGHT_DECAY) - LEARN_RATE * step
        )
    if vectors:
        vec_ref, vec_first, vec_second = vec_in
        rows, columns = vec_ref.shape
        tail = pltpu.roll(g_ref[count * side :].astype(F32), shift_ref[0], 1)
        vec_out[1][...], vec_out[2][...], direction = adam_terms(
            tail[:rows, :columns], vec_first[...], vec_second[...]
        )
        vec_out[0][...] = vec_ref[...] - VECTOR_RATE * direction


def optimize(shift, grads, arrays, number, count, vectors, before):
    def part(one):
        return pl.BlockSpec((count,) + one.shape[1:], lambda step: (number, 0, 0))

    side, height = arrays[0].shape[1:]
    matrices = count + (count + 1) // 2
    inputs = [shift, *grads, *arrays, *vectors]
    whole = [pl.BlockSpec(one.shape, lambda step: (0, 0)) for one in vectors]
    return pl.pallas_call(
        functools.partial(
            optimizer_kernel, terms=len(grads), vectors=len(vectors), held=len(before)
        ),
        grid=(1,),
        out_shape=[shape(*one.shape) for one in [*arrays, *vectors]],
        in_specs=[SMEM]
        + [pl.BlockSpec(one.shape, lambda step: (0, 0)) for one in grads]
        + [part(one) for one in arrays]
        + whole
        + [pl.BlockSpec(memory_space=pl.ANY)] * len(before),
        out_specs=[part(one) for one in arrays] + whole,
        input_output_aliases={len(inputs) + place: place for place in range(len(before))},
        scratch_shapes=[
            pltpu.VMEM(grads[0].shape, BF16),
            pltpu.VMEM((matrices, height, height), F32),
            pltpu.VMEM((matrices, height, 2 * height), BF16),
            pltpu.VMEM((matrices, height, 2 * height), BF16),
            pltpu.VMEM((count, side, height), F32),
        ],
        compiler_params=limit(24),
        cost_estimate=pl.CostEstimate(
            flops=matrices * NEWTON_TURNS * 8 * height**3, bytes_accessed=16 * MIB, transcendentals=0
        ),
        name="optimizer",
    )(*inputs, *before)


def own_rows(values, index, chunk):
    early = lax.dynamic_slice_in_dim(values, index * chunk, chunk, 0)
    late = lax.dynamic_slice_in_dim(values, (3 - index) * chunk, chunk, 0)
    return jnp.concatenate([early, late], axis=0)


def in_order(mine, other, index, chunk):
    inner = jnp.where(index == 0, other, mine)
    outer = jnp.where(index == 0, mine, other)
    return jnp.concatenate([outer[:chunk], inner, outer[chunk:]], axis=0)


def token_outputs(own_output, part_input, part_encoder, core, chunk):
    return (
        in_order(own_output, swapped(own_output), core, chunk),
        part_input.astype(F32) + swapped(part_input).astype(F32),
        part_encoder.astype(F32) + swapped(part_encoder).astype(F32),
    )


def key_bounds(key_ids, query_ids, chunk):
    rows = query_ids.reshape(-1, chunk)
    lowest = jnp.sum((key_ids[None] < rows[:, :1]).astype(jnp.int32), axis=1, keepdims=True)
    highest = jnp.sum((key_ids[None] <= rows[:, -1:]).astype(jnp.int32), axis=1, keepdims=True)
    return jnp.concatenate([lowest, highest + (chunk - 1)], axis=1) // chunk


def per_device(
    decoder_input,
    encoder_states,
    decoder_segments,
    encoder_segments,
    output_cotangent,
    block_slots,
    master,
    first_moment,
    second_moment,
    row_statistics,
    column_statistics,
    row_basis,
    column_basis,
    vectors,
    vector_first,
    vector_second,
):
    core = lax.axis_index("tensor")
    cores = lax.axis_size("tensor")
    ring, rings = lax.axis_index("dp"), lax.axis_size("dp")
    owned_count, block_height = master.shape[1], master.shape[2]
    vector_cols = vectors.shape[1]
    length, width = decoder_input.shape[1], decoder_input.shape[2]
    row_count = width // block_height
    block_total = block_slots.shape[0]
    column_count = block_total // row_count
    chunk = length // 4
    per_ring = owned_count * HD + VECTOR_ROWS
    group = block_height // vector_cols

    payload = low(master[0]).transpose(0, 2, 1).reshape(owned_count * HD, block_height)
    lane = jnp.arange(block_height) // vector_cols
    here = lane == ring % group
    small = jnp.where(here[None], jnp.tile(low(vectors), (1, group)), jnp.zeros((), BF16))
    small = jnp.pad(small, ((0, VECTOR_ROWS - vectors.shape[0]), (0, 0)))
    tokens, encoder_rows = decoder_input[0], encoder_states[0]
    ids, encoder_ids = decoder_segments[0], encoder_segments[0]
    own_tokens = own_rows(tokens, core, chunk)
    own_ids = own_rows(ids, core, chunk)
    own_cotangent = own_rows(output_cotangent[0], core, chunk)
    places = jnp.arange(length, dtype=jnp.int32)
    own_places = own_rows(places, core, chunk)
    self_allowed = (ids[:, None] == own_ids[None, :]) & (places[:, None] <= own_places[None, :])
    self_bias = jnp.where(self_allowed, 0.0, NEGATIVE).astype(F32)
    cross_bias = jnp.where(encoder_ids[:, None] == own_ids[None, :], 0.0, NEGATIVE).astype(F32)
    here_and_core = jnp.full((1,), core, jnp.int32)
    ends = jnp.stack([here_and_core + 1, 4 - here_and_core])
    self_edges = jnp.concatenate([key_bounds(ids, own_ids, chunk)[:, :1], ends], axis=1)
    self_scalars = jnp.concatenate([self_edges.reshape(-1), here_and_core])
    cross_edges = key_bounds(encoder_ids, own_ids, chunk)
    cross_scalars = jnp.concatenate([cross_edges.reshape(-1), here_and_core])

    payload = jnp.concatenate([payload, small], axis=0)
    owner, local = block_slots // owned_count, block_slots % owned_count
    chips = jnp.arange(rings, dtype=jnp.int32)
    grid_of_chips = rings == DEPTH * SIDE * SIDE
    if grid_of_chips:
        starts = apart(ring, owner, 1) * per_ring + local * HD
        slices = [(index ^ core) * rings * per_ring for index in range(cores)]
        ends = (apart(ring, chips, 1) + 1) * per_ring - VECTOR_ROWS
        early_count = owned_count // 2
        sizes = (early_count * HD, per_ring - early_count * HD)
        order = jnp.array(PLACES, jnp.int32)
        late = local // early_count
        sum_rows = local % early_count * HD + jnp.where(
            late == 1,
            rings * sizes[0] + order[apart(ring, owner, -1)] * sizes[1],
            order[apart(ring, owner, -1)] * sizes[0],
        )
        sum_ends = rings * sizes[0] + (order[apart(ring, chips, -1)] + 1) * sizes[1] - VECTOR_ROWS
    else:
        starts = owner * cores * per_ring + local * HD
        slices = [index * per_ring for index in range(cores)]
        ends = (chips * cores + 1) * per_ring - VECTOR_ROWS
        sum_rows = owner * per_ring + local * HD
        sum_ends = (chips + 1) * per_ring - VECTOR_ROWS
    starts = jnp.concatenate([starts + start for start in slices])
    beside = (starts, ends, own_tokens, own_cotangent, self_bias, cross_bias)
    beside += (self_scalars, cross_scalars, sum_rows, sum_ends)
    if grid_of_chips:
        pieces, beside = gather_chips(payload, beside)
        pieces += [swapped(piece) for piece in pieces]
    else:
        pieces = [lax.all_gather(payload, ("dp", "tensor"), axis=0, tiled=True)]
    starts, ends, own_tokens, own_cotangent, self_bias, cross_bias, *scalars = beside
    self_scalars, cross_scalars, sum_rows, sum_ends = scalars
    layer = call_layer(
        (self_scalars, cross_scalars, starts, ends),
        pieces,
        (tokens, own_tokens, self_bias, encoder_rows, cross_bias, own_cotangent),
        cores,
        group,
    )
    own_output, ff_mine, ff_sent, cross_mine, cross_sent, part_encoder, grad_one, norms = layer[:8]
    w_self, q_self, k_self, lse_self, ctxt_self = layer[8:]
    self_mine, self_sent, part_input = call_self_backward(
        self_scalars,
        (grad_one, ctxt_self, w_self, q_self, tokens, own_tokens, k_self, lse_self, self_bias),
    )

    terms = [ff_mine, ff_sent, cross_mine, cross_sent, self_mine, self_sent]
    terms = [one if number % 2 == 0 else swapped(one) for number, one in enumerate(terms)]
    terms += [norms, swapped(norms)]
    shift = ((block_height - ring % group * vector_cols) % block_height)[None]
    arrays = [one[0].transpose(0, 2, 1) for one in (master, first_moment, second_moment)]
    arrays += [
        one[0] for one in (row_statistics, column_statistics, row_basis, column_basis)
    ]
    vector_states = [vectors, vector_first, vector_second]
    if grid_of_chips:
        cuts = [size * places for size in sizes for places in (4, 4, 2, 2, 4)]
        parts = scatter(sum_rows, sum_ends, terms, cuts, cores, block_height, group)
        own_output, part_encoder, part_input, parts = lax.optimization_barrier(
            (own_output, part_encoder, part_input, parts)
        )
        tokens_out = token_outputs(own_output, part_input, part_encoder, core, chunk)
        column, tokens_out = reduce_plane(*parts[:5], tokens_out)
        block_output, input_gradient, encoder_gradient = tokens_out
        column, parts = lax.optimization_barrier((column, parts[5:]))
        column, early = reduce_plane(*parts, reduce_column(column))
        updated = optimize(shift, early, arrays, 0, early_count, [], [])
        updated = optimize(
            shift, reduce_column(column), arrays, 1, early_count, vector_states, updated
        )
    else:
        (whole,) = scatter(
            sum_rows,
            sum_ends,
            terms,
            [rings * per_ring],
            cores,
            block_height,
            group,
        )
        summed = lax.psum_scatter(whole, "dp", scatter_dimension=0, tiled=True)
        updated = optimize(shift, [summed], arrays, 0, owned_count, vector_states, [])
        tokens_out = token_outputs(own_output, part_input, part_encoder, core, chunk)
        block_output, input_gradient, encoder_gradient = tokens_out

    return (
        block_output[None],
        input_gradient[None],
        encoder_gradient[None],
        *[one.transpose(0, 2, 1)[None] for one in updated[:3]],
        *[one[None] for one in updated[3:7]],
        *updated[7:],
    )


def solution(mesh):
    blocks = P("tensor", "dp", None, None)
    rows = P("dp", None, None)
    return jax.shard_map(
        per_device,
        mesh=mesh,
        in_specs=(rows, rows, P("dp", None), P("dp", None), rows, P())
        + (blocks,) * 7
        + (P(None, "dp"),) * 3,
        out_specs=(rows,) * 3 + (blocks,) * 7 + (P(None, "dp"),) * 3,
        check_vma=False,
    )
```

```python
import functools

import jax
import jax.numpy as jnp
from jax import lax
from jax.experimental import pallas as pl
from jax.experimental.pallas import tpu as pltpu
from jax.sharding import PartitionSpec as P

HD = 64
FF = 2048
STEP = 10

NEGATIVE = -1e30
EPS_NORM = 1e-05
MOMENT_DECAY = 0.5
LEARN_RATE = 0.04
WEIGHT_DECAY = 0.01
VECTOR_RATE = 0.25
ADAM_EPS = 1e-08
NEWTON_TURNS = 8
EARLY_TURNS = 5
VECTOR_ROWS = 16
DEPTH, SIDE = 4, 2
MIB = 2**20
F32 = jnp.float32
BF16 = jnp.bfloat16
VMEM = pl.BlockSpec(memory_space=pltpu.VMEM)
SMEM = pl.BlockSpec(memory_space=pltpu.SMEM)
ANY = pl.BlockSpec(memory_space=pl.ANY)


def nn(left, right):
    return lax.dot_general(left, right, (((1,), (0,)), ((), ())), preferred_element_type=F32)


def nt(left, right):
    return lax.dot_general(left, right, (((1,), (1,)), ((), ())), preferred_element_type=F32)


def tn(left, right):
    return lax.dot_general(left, right, (((0,), (0,)), ((), ())), preferred_element_type=F32)


def low(values):
    return values.astype(BF16)


def span(number, size):
    return slice(number * size, (number + 1) * size)


def rows_at(number, size):
    return pl.ds(pl.multiple_of(number * size, size), size)


def shape(*dims, dtype=F32):
    return jax.ShapeDtypeStruct(dims, dtype)


def scratch(shapes):
    return [pltpu.VMEM(one.shape, one.dtype) for one in shapes]


def limit(mib):
    return pltpu.CompilerParams(vmem_limit_bytes=mib * MIB)


def block_places(columns, cores):
    hidden = FF // cores // HD
    heads = (columns - 2 * hidden) // 8
    places = []
    for column in range(columns):
        if column < 8 * heads:
            places.append((column // heads, column % heads * HD))
        else:
            column -= 8 * heads
            places.append((8 + column // hidden, column % hidden * HD))
    return places, heads * HD, hidden * HD


def start_copies(pairs, semaphores, first=0):
    copies = [
        pltpu.make_async_copy(source, target, semaphores.at[first + number])
        for number, (source, target) in enumerate(pairs)
    ]
    for copy in copies:
        copy.start()
    return copies


def wait_for(copies):
    for copy in copies:
        copy.wait()


def in_a_row(pieces, target_ref):
    pairs, start = [], 0
    for piece in pieces:
        pairs.append((piece, target_ref.at[pl.ds(start, piece.shape[0])]))
        start += piece.shape[0]
    return pairs


def assemble(rows_ref, ends_ref, gathered_ref, w_refs, vec_ref, cores, group):
    height = gathered_ref.shape[1]
    row_count = vec_ref.shape[1] // height
    total = rows_ref.shape[0] // cores
    columns = total // row_count
    places, head_rows, hidden_rows = block_places(columns, cores)
    for core in range(cores):
        for row in range(row_count):
            for column in range(columns):
                kind, inner = places[column]
                size = head_rows if kind < 8 else hidden_rows
                target = (kind % 4 * cores + core) * size + inner
                source = pl.multiple_of(rows_ref[core * total + row * columns + column], 16)
                block = gathered_ref[pl.ds(source, HD), :]
                w_refs[kind // 4][target : target + HD, span(row, height)] = block
    rings = ends_ref.shape[0]
    for part in range(row_count):
        values = jnp.zeros((VECTOR_ROWS, height), F32)
        for ring in range(part * group, min((part + 1) * group, rings)):
            start = pl.multiple_of(ends_ref[ring], 16)
            values = values + gathered_ref[pl.ds(start, VECTOR_ROWS), :].astype(F32)
        vec_ref[:, span(part, height)] = values


def scatter_kernel(rows_ref, ends_ref, *refs, cores, group, cuts):
    ff_mine, cross_mine, arrived, self_mine, self_in, vec_ref = refs[:6]
    outs, refs = refs[6 : 6 + cuts], refs[6 + cuts :]
    terms, (all_ref, in_sems, out_sems) = refs[:7], refs[7:]
    ff_in, cross_in, vec_in = in_a_row((terms[1], terms[3], terms[6]), arrived)
    pairs = [(ff_mine, terms[0]), ff_in[::-1], (cross_mine, terms[2]), cross_in[::-1]]
    pairs += [(self_mine, terms[4]), (self_in, terms[5]), vec_in[::-1]]
    copies = start_copies(pairs, in_sems)
    height = all_ref.shape[1]
    row_count = vec_ref.shape[1] // height
    columns = rows_ref.shape[0] // row_count
    places, head_rows, hidden_rows = block_places(columns, cores)
    for part, (first, last, size) in enumerate(
        ((8, 10, hidden_rows), (4, 8, head_rows), (0, 4, head_rows))
    ):
        one, two = terms[2 * part : 2 * part + 2]
        wait_for(copies[2 * part : 2 * part + 2])
        for column in range(columns):
            kind, inner = places[column]
            if first <= kind < last:
                start = (kind - first) * size + inner
                for row in range(row_count):
                    here = slice(start, start + HD), span(row, height)
                    target = pl.multiple_of(rows_ref[row * columns + column], 16)
                    total = one[here].astype(F32) + two[here].astype(F32)
                    all_ref[pl.ds(target, HD), :] = low(total)
    wait_for(copies[6:])
    total = low(vec_ref[...] + terms[6][...].astype(F32))
    for ring in range(ends_ref.shape[0]):
        start = pl.multiple_of(ends_ref[ring], 16)
        all_ref[pl.ds(start, VECTOR_ROWS), :] = total[:, span(ring // group, height)]
    pairs = [(part, out) for out, part in in_a_row(outs, all_ref)]
    wait_for(start_copies(pairs, out_sems))


def scatter(rows, ends, terms, cuts, cores, height, group):
    return pl.pallas_call(
        functools.partial(scatter_kernel, cores=cores, group=group, cuts=len(cuts)),
        out_shape=[shape(cut, height, dtype=BF16) for cut in cuts],
        in_specs=[SMEM, SMEM] + [ANY] * 5 + [VMEM],
        out_specs=[ANY] * len(cuts),
        scratch_shapes=scratch([*terms[:1] * 2, *terms[1:2] * 2, *terms[3:4] * 2])
        + [
            pltpu.VMEM(terms[5].shape, BF16),
            pltpu.VMEM((sum(cuts), height), BF16),
            pltpu.SemaphoreType.DMA((7,)),
            pltpu.SemaphoreType.DMA((len(cuts),)),
        ],
        compiler_params=limit(63),
        name="scatter",
    )(rows, ends, *terms)


def hop(values, *steps):
    sizes = (DEPTH, SIDE, SIDE)
    pairs = []
    for source in range(DEPTH * SIDE * SIDE):
        place = (source // (SIDE * SIDE), source // SIDE % SIDE, source % SIDE)
        z, y, x = ((one + step) % size for one, step, size in zip(place, steps, sizes))
        pairs.append((source, (z * SIDE + y) * SIDE + x))
    return lax.ppermute(values, "dp", pairs)


def swapped(values):
    return lax.ppermute(values, "tensor", [(0, 1), (1, 0)])


def apart(ring, other, sign):
    side = SIDE * SIDE
    deep = (sign * (ring // side - other // side)) % DEPTH
    across = (ring // SIDE % SIDE) ^ (other // SIDE % SIDE)
    return (across * SIDE + ((ring % SIDE) ^ (other % SIDE))) * DEPTH + deep


def gather_chips(own, beside):
    deep = [hop(own, step, 0, 0) for step in range(1, DEPTH)]
    near = [hop(own, 0, 0, 1), hop(own, 0, 1, 0), hop(own, 0, 1, 1)]
    deep, near, beside = lax.optimization_barrier((jnp.concatenate(deep, axis=0), near, beside))
    by_x, by_y = hop(deep, 0, 0, 1), hop(deep, 0, 1, 0)
    cut = deep.shape[0] // 32 * 16
    pieces = [own, deep, near[0], by_x, near[1], by_y, near[2]]
    return pieces + [hop(by_y[:cut], 0, 0, 1), hop(by_x[cut:], 0, 1, 0)], beside


PLACES = (12, 13, 14, 15, 2, 3, 10, 11, 8, 9, 6, 7, 0, 1, 4, 5)


def fold(*terms):
    return low(functools.reduce(lambda one, two: one + two, [term.astype(F32) for term in terms]))


def reduce_plane(along_x, along_y, late_y, late_x, here, beside):
    half = late_x.shape[0]
    from_x, from_y = hop(along_x, 0, 0, 1), hop(along_y, 0, 1, 0)
    from_x, from_y, beside = lax.optimization_barrier((from_x, from_y, beside))
    more_y = hop(fold(late_y, from_x[:half]), 0, 1, 0)
    more_x = hop(fold(late_x, from_y[:half]), 0, 0, 1)
    column = jnp.concatenate(
        [fold(here[:half], from_x[half:], more_y), fold(here[half:], from_y[half:], more_x)],
        axis=0,
    )
    return column, beside


def reduce_column(column):
    rows = column.shape[0] // DEPTH
    return [column[:rows]] + [
        hop(column[step * rows : (step + 1) * rows], step, 0, 0) for step in range(1, DEPTH)
    ]


def norm_forward(total_ref, vec_ref, first, hat_ref, inverse_ref, out_ref, step=64):
    gain, shift = vec_ref[first : first + 1], vec_ref[first + 1 : first + 2]

    def body(number, carry):
        rows = rows_at(number, step)
        values = total_ref[rows]
        center = values - jnp.mean(values, axis=1, keepdims=True)
        inverse = lax.rsqrt(jnp.mean(center * center, axis=1, keepdims=True) + EPS_NORM)
        hat = center * inverse
        hat_ref[rows] = hat
        inverse_ref[rows] = inverse
        out_ref[rows] = (hat * gain + shift).astype(out_ref.dtype)
        return carry

    lax.fori_loop(0, total_ref.shape[0] // step, body, 0, unroll=8)


def norm_backward(grad_ref, hat_ref, inverse_ref, gain, out_ref, step=64):
    width = grad_ref.shape[1]

    def body(number, carry):
        rows = rows_at(number, step)
        grad, hat = grad_ref[rows].astype(F32), hat_ref[rows]
        scaled = grad * gain
        middle = jnp.mean(scaled, axis=1, keepdims=True)
        slope = jnp.mean(scaled * hat, axis=1, keepdims=True)
        out_ref[rows] = (scaled - middle - hat * slope) * inverse_ref[rows]
        return (
            carry[0] + jnp.sum((grad * hat).reshape(step // 8, 8, width), axis=0),
            carry[1] + jnp.sum(grad.reshape(step // 8, 8, width), axis=0),
        )

    zeros = jnp.zeros((8, width), F32)
    sums = lax.fori_loop(0, grad_ref.shape[0] // step, body, (zeros, zeros), unroll=8)
    return [jnp.sum(one, axis=0, keepdims=True) for one in sums]


def split_heads(source_ref, masked_ref, factor):
    for head in range(masked_ref.shape[0]):
        pair = source_ref[:, span(head // 2, 2 * HD)]
        lane = lax.broadcasted_iota(jnp.int32, pair.shape, 1)
        here = (lane >= HD) if head % 2 else (lane < HD)
        masked_ref[head] = jnp.where(here, pair, jnp.zeros_like(pair)) * jnp.asarray(factor, BF16)


def staged(count, early, middle, late, ahead=2, lag=2):
    ready = [early(number) for number in range(min(ahead, count))]
    held = []
    for number in range(count):
        now = ready.pop(0)
        if number + ahead < count:
            ready.append(early(number + ahead))
        held.append((number, middle(number, now)))
        if len(held) > lag:
            late(*held.pop(0))
    while held:
        late(*held.pop(0))


def attend_forward(bounds_ref, bias_ref, masked_q, k_ref, vt_ref, m_ref, l_ref, acc_ref, lse_ref,
                   ctxt_ref):
    heads, chunk = m_ref.shape
    for part in range(lse_ref.shape[1] // chunk):
        cols = span(part, chunk)
        m_ref[...] = jnp.full(m_ref.shape, NEGATIVE, F32)
        l_ref[...] = jnp.zeros(l_ref.shape, F32)
        acc_ref[...] = jnp.zeros(acc_ref.shape, F32)

        def body(number, carry):
            keys = rows_at(number, chunk)
            bias = bias_ref[keys, cols]

            def early(head):
                return nt(k_ref[keys, span(head // 2, 2 * HD)], masked_q[head, cols]) + bias

            def middle(head, scores):
                row = slice(head, head + 1)
                before = m_ref[row]
                highest = jnp.maximum(before, jnp.max(scores, axis=0, keepdims=True))
                shrink = jnp.exp(before - highest)
                expons = jnp.exp(scores - highest)
                l_ref[row] = l_ref[row] * shrink + jnp.sum(expons, axis=0, keepdims=True)
                m_ref[row] = highest
                return shrink, low(expons)

            def late(head, pair):
                rows = span(head, HD)
                acc_ref[rows] = acc_ref[rows] * pair[0] + nn(vt_ref[rows, keys], pair[1])

            staged(heads, early, middle, late)
            return carry

        lax.fori_loop(bounds_ref[2 * part], bounds_ref[2 * part + 1], body, 0)
        for head in range(heads):
            rows = span(head, HD)
            ctxt_ref[rows, cols] = low(acc_ref[rows] / l_ref[head : head + 1])
        lse_ref[:, cols] = m_ref[...] + jnp.log(l_ref[...])


def branch_forward(bounds_ref, x_ref, own_ref, w_ref, bias_ref, vec_ref,
                   q_ref, k_ref, lse_ref, ctxt_ref, hat_ref, inverse_ref, y_ref, first):
    keys, width = k_ref.shape
    heads, queries = lse_ref.shape
    chunk = keys // 4

    def body(masked_q, vt_ref, m_ref, l_ref, acc_ref):
        q_ref[...] = low(nt(low(own_ref[...]), w_ref[span(0, width)]))
        split_heads(q_ref, masked_q, HD**-0.5)
        k_ref[...] = low(nt(x_ref[...], w_ref[span(1, width)]))
        vt_ref[...] = low(nt(w_ref[span(2, width)], x_ref[...]))
        attend_forward(
            bounds_ref, bias_ref, masked_q, k_ref, vt_ref, m_ref, l_ref, acc_ref, lse_ref, ctxt_ref
        )
        y_ref[...] = own_ref[...].astype(F32) + tn(ctxt_ref[...], w_ref[span(3, width)])
        norm_forward(y_ref, vec_ref, first, hat_ref, inverse_ref, y_ref)

    pl.run_scoped(
        body,
        pltpu.VMEM((heads, queries, 2 * HD), BF16),
        pltpu.VMEM((width, keys), BF16),
        pltpu.VMEM((heads, chunk), F32),
        pltpu.VMEM((heads, chunk), F32),
        pltpu.VMEM((width, chunk), F32),
    )


def branch_backward(scalars_ref, x_ref, own_ref, w_ref, bias_ref, grad_ref, q_ref, k_ref, lse_ref,
                    ctxt_ref, mine_ref, sent_ref, part_ref, norm, arrive):
    heads, queries = lse_ref.shape
    keys, width = k_ref.shape
    chunk = queries // 2

    def body(masked_q, masked_g, v_ref, kt_ref, delta_ref, dqt_ref, dk_ref, dv_ref, dq_ref, out_ref):
        core = scalars_ref[4]
        half = width // 2
        arrive(0)

        def keep(kind, gradient):
            out_ref[...] = low(gradient)
            mine_ref[span(kind, half)] = out_ref[rows_at(core, half)]
            sent_ref[span(kind, half)] = out_ref[rows_at(1 - core, half)]

        grad_low = low(grad_ref[...])
        w_out = w_ref[span(3, width)]
        keep(3, nn(ctxt_ref[...], grad_low))
        out_ref[...] = low(nt(grad_low, w_out))
        split_heads(out_ref, masked_g, 1.0)
        arrive(1)
        split_heads(q_ref, masked_q, HD**-0.5)
        grad_t = low(nt(w_out, grad_low)).astype(F32) * ctxt_ref[...].astype(F32)
        for head in range(heads):
            delta_ref[head : head + 1] = jnp.sum(grad_t[span(head, HD)], axis=0, keepdims=True)
        v_ref[...] = low(nt(x_ref[...], w_ref[span(2, width)]))
        kt_ref[...] = low(nt(w_ref[span(1, width)], x_ref[...]))
        dqt_ref[...] = jnp.zeros(dqt_ref.shape, F32)
        dk_ref[...] = jnp.zeros(dk_ref.shape, F32)
        dv_ref[...] = jnp.zeros(dv_ref.shape, F32)
        for part in range(2):
            cols = span(part, chunk)

            def pair(number, carry):
                keys = rows_at(number, chunk)
                bias = bias_ref[keys, cols]

                def early(head):
                    pair = span(head // 2, 2 * HD)
                    return (
                        nt(k_ref[keys, pair], masked_q[head, cols]) + bias,
                        nt(v_ref[keys, pair], masked_g[head, cols]),
                    )

                def middle(head, both):
                    row = slice(head, head + 1)
                    chances = jnp.exp(both[0] - lse_ref[row, cols])
                    return low(chances), low(chances * (both[1] - delta_ref[row, cols]))

                def late(head, both):
                    pair, rows = span(head // 2, 2 * HD), span(head, HD)
                    dv_ref[keys, pair] += nn(both[0], masked_g[head, cols])
                    dk_ref[keys, pair] += nn(both[1], masked_q[head, cols])
                    dqt_ref[rows, cols] += nn(kt_ref[rows, keys], both[1])

                staged(heads, early, middle, late)
                return carry

            lax.fori_loop(scalars_ref[2 * part], scalars_ref[2 * part + 1], pair, 0)
        dqt = low(dqt_ref[...] * HD**-0.5)
        keep(0, nn(dqt, low(own_ref[...])))
        dk, dv = low(dk_ref[...]), low(dv_ref[...])
        keep(1, tn(dk, x_ref[...]))
        keep(2, tn(dv, x_ref[...]))
        dq_ref[...] = grad_ref[...] + tn(dqt, w_ref[span(0, width)])
        if norm is not None:
            part_ref[...] = low(nn(dk, w_ref[span(1, width)]) + nn(dv, w_ref[span(2, width)]))
            hat_ref, inverse_ref, gain, next_ref, norms_ref, place = norm
            sums = norm_backward(dq_ref, hat_ref, inverse_ref, gain, next_ref)
            norms_ref[place : place + 1] = sums[0]
            norms_ref[place + 1 : place + 2] = sums[1]
        else:
            dk_ref[...] = nn(dk, w_ref[span(1, width)]) + nn(dv, w_ref[span(2, width)])
            for part, place in enumerate((core, 3 - core)):
                dk_ref[rows_at(place, chunk)] += dq_ref[span(part, chunk)]
            part_ref[...] = low(dk_ref[...])

    pl.run_scoped(
        body,
        pltpu.VMEM((heads, queries, 2 * HD), BF16),
        pltpu.VMEM((heads, queries, 2 * HD), BF16),
        pltpu.VMEM((keys, width), BF16),
        pltpu.VMEM((width, keys), BF16),
        pltpu.VMEM((heads, queries), F32),
        pltpu.VMEM((width, queries), F32),
        pltpu.VMEM((keys, width), F32),
        pltpu.VMEM((keys, width), F32),
        pltpu.VMEM((queries, width), F32),
        pltpu.VMEM((width, width), BF16),
    )


def gelu_both(values):
    scale = (2.0 / jnp.pi) ** 0.5
    square = values * values
    bend = jnp.tanh(values * (scale + scale * 0.044715 * square))
    half = 0.5 + 0.5 * bend
    slope = half + (0.5 * values) * (1.0 - bend * bend) * (scale + 3.0 * scale * 0.044715 * square)
    return values * half, slope


def feed_both(core, y_ref, w_ref, vec_ref, cot_ref, hat_two, inverse_two,
              block_ref, next_ref, mine_ref, sent_ref, norms_ref, arrive, step=256):
    queries, width = y_ref.shape
    hidden = w_ref.shape[0] // 2
    half = hidden // 2
    chunks = hidden // step

    def body(low_ref, hid_ref, slope_ref, total_ref, hat_ref, inverse_ref, grad_low):
        low_ref[...] = low(y_ref[...])
        total_ref[...] = y_ref[...]

        def early(number):
            return nt(w_ref[span(number, step)], low_ref[...])

        def middle(number, up):
            hid, slope = gelu_both(up)
            hid_ref[span(number, step)] = low(hid)
            slope_ref[span(number, step)] = slope

        def late(number, _):
            lower = w_ref[hidden + number * step : hidden + (number + 1) * step]
            total_ref[...] += tn(hid_ref[span(number, step)], lower)

        staged(chunks, early, middle, late, 1, 1)
        norm_forward(total_ref, vec_ref, 4, hat_ref, inverse_ref, block_ref)
        sums = norm_backward(cot_ref, hat_ref, inverse_ref, vec_ref[4:5], total_ref)
        norms_ref[4:5] = sums[0]
        norms_ref[5:6] = sums[1]
        grad_low[...] = low(total_ref[...])

        def place(number):
            inner = number % (chunks // 2)
            row = (core if number < chunks // 2 else 1 - core) * half + inner * step
            return inner, pl.multiple_of(row, step)

        def down(number):
            row = place(number)[1]
            return nt(w_ref[pl.ds(pl.multiple_of(hidden + row, step), step)], grad_low[...])

        def turn(number, grad_hidden):
            return low(slope_ref[pl.ds(place(number)[1], step)] * grad_hidden)

        def sums_of(number, grad_up):
            inner, row = place(number)
            rows = pl.ds(row, step)
            kept = mine_ref if number < chunks // 2 else sent_ref
            kept[span(inner, step)] = low(nn(grad_up, low_ref[...]))
            kept[half + inner * step : half + (inner + 1) * step] = low(nn(hid_ref[rows], grad_low[...]))
            total_ref[...] += tn(grad_up, w_ref[rows])

        staged(chunks, down, turn, sums_of, 1, 1)
        sums = norm_backward(total_ref, hat_two, inverse_two, vec_ref[2:3], next_ref)
        norms_ref[2:3] = sums[0]
        norms_ref[3:4] = sums[1]

    pl.run_scoped(
        body,
        pltpu.VMEM((queries, width), BF16),
        pltpu.VMEM((hidden, queries), BF16),
        pltpu.VMEM((hidden, queries), F32),
        pltpu.VMEM((queries, width), F32),
        pltpu.VMEM((queries, width), F32),
        pltpu.VMEM((queries, 1), F32),
        pltpu.VMEM((queries, width), BF16),
    )


def layer_kernel(self_ref, cross_ref, rows_ref, ends_ref, *refs, cores, group, pieces):
    gathered, refs = refs[:pieces], refs[pieces:]
    ins, refs = refs[:6], refs[6:]
    block_out, ff_mine_out, mine_out, sent_out, part_out, next_out = refs[:6]
    norms_ref, w_out, q_out, k_out, lse_out, ctxt_out = refs[6:12]
    refs = refs[12:]
    w_self, w_cross, w_feed, vec_ref, x_ref, own_ref, bias_ref, enc_ref, bias_cross, cot_ref = refs[:10]
    self_saved, cross_saved, refs = refs[10:14], refs[14:18], refs[18:]
    hat_one, inverse_one, y_one, hat_two, inverse_two, y_two, refs = *refs[:6], refs[6:]
    block_ref, ff_mine, ff_sent, mine_ref, sent_ref, part_ref, grad_ref, next_ref = refs[:8]
    norms_low, refs = refs[8], refs[1:]
    sent_parts = [part for _, part in in_a_row((ff_sent, sent_ref, norms_low), sent_out)]
    piece_sems, in_sems, out_sems = refs[8:]
    norms_ref[...] = jnp.zeros(norms_ref.shape, F32)

    targets = (x_ref, own_ref, bias_ref, enc_ref, bias_cross, cot_ref)

    def fetch(gathered_ref):
        arriving = start_copies(in_a_row(gathered, gathered_ref), piece_sems)
        start_copies(zip(ins, targets), in_sems)
        wait_for(arriving)
        assemble(
            rows_ref, ends_ref, gathered_ref, (w_self, w_cross, w_feed), vec_ref, cores, group
        )

    total = sum(piece.shape[0] for piece in gathered)
    pl.run_scoped(fetch, pltpu.VMEM((total, gathered[0].shape[1]), BF16))
    arriving = [
        pltpu.make_async_copy(source, target, in_sems.at[number])
        for number, (source, target) in enumerate(zip(ins, targets))
    ]
    wait_for(arriving[:3])
    leaving = start_copies([(w_self, w_out)], out_sems)
    branch_forward(
        self_ref, x_ref, own_ref, w_self, bias_ref, vec_ref, *self_saved, hat_one, inverse_one,
        y_one, 0,
    )
    leaving += start_copies(zip(self_saved, (q_out, k_out, lse_out, ctxt_out)), out_sems, 1)
    wait_for(arriving[3:5])
    branch_forward(
        cross_ref, enc_ref, y_one, w_cross, bias_cross, vec_ref, *cross_saved, hat_two, inverse_two,
        y_two, 2,
    )
    wait_for(arriving[5:])
    feed_both(
        self_ref[4], y_two, w_feed, vec_ref, cot_ref, hat_two, inverse_two, block_ref, grad_ref,
        ff_mine, ff_sent, norms_ref, None,
    )
    pairs = [(block_ref, block_out), (ff_mine, ff_mine_out), (ff_sent, sent_parts[0])]
    leaving += start_copies(pairs, out_sems, 5)
    branch_backward(
        cross_ref, enc_ref, y_one, w_cross, bias_cross, grad_ref, *cross_saved, mine_ref, sent_ref,
        part_ref, (hat_one, inverse_one, vec_ref[0:1], next_ref, norms_ref, 0), lambda number: None,
    )
    norms_low[...] = low(norms_ref[...])
    pairs = [(mine_ref, mine_out), (sent_ref, sent_parts[1]), (norms_low, sent_parts[2])]
    pairs += [(part_ref, part_out), (next_ref, next_out)]
    leaving += start_copies(pairs, out_sems, 8)
    wait_for(leaving)


def saved_shapes(keys, queries, width):
    heads = width // HD
    return [
        shape(queries, width, dtype=BF16),
        shape(keys, width, dtype=BF16),
        shape(heads, queries),
        shape(width, queries, dtype=BF16),
    ]


def call_layer(scalars, pieces, inputs, cores, group):
    keys, queries = inputs[2].shape
    width = inputs[0].shape[1]
    saved = saved_shapes(keys, queries, width)
    weights = shape(4 * width, width, dtype=BF16)
    tokens = shape(queries, width)
    norm = [tokens, shape(queries, 1), tokens]
    own, feed = shape(queries, width, dtype=BF16), shape(FF, width, dtype=BF16)
    branch, rows = shape(2 * width, width, dtype=BF16), shape(keys, width, dtype=BF16)
    sent = shape(FF + 2 * width + VECTOR_ROWS, width, dtype=BF16)
    kept = [weights, weights, shape(2 * FF, width, dtype=BF16), shape(VECTOR_ROWS, width)]
    kept += [*inputs, *saved, *saved, *norm, *norm]
    kept += [own, feed, feed, branch, branch, rows, tokens, tokens]
    kept += [shape(VECTOR_ROWS, width, dtype=BF16)]
    norms = shape(VECTOR_ROWS, width)
    return pl.pallas_call(
        functools.partial(layer_kernel, cores=cores, group=group, pieces=len(pieces)),
        out_shape=[own, feed, branch, sent, rows, tokens, norms, weights, *saved],
        in_specs=[SMEM] * 4 + [ANY] * (len(pieces) + len(inputs)),
        out_specs=[ANY] * 6 + [VMEM] + [ANY] * 5,
        scratch_shapes=scratch(kept)
        + [
            pltpu.SemaphoreType.DMA((len(pieces),)),
            pltpu.SemaphoreType.DMA((6,)),
            pltpu.SemaphoreType.DMA((13,)),
        ],
        compiler_params=limit(56),
        name="layer",
    )(*scalars, *pieces, *inputs)


def self_backward_kernel(scalars_ref, *refs):
    ins, (mine_out, sent_out, part_out), refs = refs[:9], refs[9:12], refs[12:]
    grad_ref, ctxt_ref, w_ref, q_ref, x_ref, own_ref, k_ref, lse_ref, bias_ref = refs[:9]
    mine_ref, sent_ref, part_ref, in_sems, out_sems = refs[9:]
    copies = start_copies(zip(ins, refs[:9]), in_sems)
    branch_backward(
        scalars_ref, x_ref, own_ref, w_ref, bias_ref, grad_ref, q_ref, k_ref, lse_ref, ctxt_ref,
        mine_ref, sent_ref, part_ref, None,
        lambda number: wait_for(copies[3:] if number else copies[:3]),
    )
    pairs = [(mine_ref, mine_out), (sent_ref, sent_out), (part_ref, part_out)]
    wait_for(start_copies(pairs, out_sems))


def call_self_backward(scalars, inputs):
    keys, width = inputs[4].shape
    outs = [
        shape(2 * width, width, dtype=BF16),
        shape(2 * width, width, dtype=BF16),
        shape(keys, width, dtype=BF16),
    ]
    return pl.pallas_call(
        self_backward_kernel,
        out_shape=outs,
        in_specs=[SMEM] + [ANY] * 9,
        out_specs=[ANY] * 3,
        scratch_shapes=scratch([*inputs, *outs])
        + [pltpu.SemaphoreType.DMA((9,)), pltpu.SemaphoreType.DMA((3,))],
        compiler_params=limit(63),
        cost_estimate=pl.CostEstimate(
            flops=12 * 10**9, bytes_accessed=12 * MIB, transcendentals=0
        ),
        name="self_backward",
    )(scalars, *inputs)


def halves(values):
    high = low(values)
    return high, low(values - high.astype(F32))


def fine(dot, left, right):
    left_high, left_low = halves(left)
    right_high, right_low = halves(right)
    return dot(left_high, right_high) + (dot(left_high, right_low) + dot(left_low, right_high))


def newton_turn(x_ref, s_ref, z_ref):
    count, size = x_ref.shape[0], x_ref.shape[1]
    for number in range(count):
        high, rest = halves(x_ref[number])
        z_ref[number] = jnp.concatenate([high, rest], axis=1)
        right = jnp.concatenate(
            [jnp.concatenate([high, high], axis=1), jnp.concatenate([rest, rest], axis=1)], axis=0
        )
        product = nt(z_ref[number], right)
        high, rest = halves(product[:, :size] + product[:, size:])
        s_ref[number] = jnp.concatenate([high, rest], axis=1)
    for number in range(count):
        terms = z_ref[number]
        product = nn(s_ref[number], jnp.concatenate([terms, terms], axis=0))
        x_ref[number] = 1.5 * x_ref[number] - 0.5 * (product[:, :size] + product[:, size:])


def early_turn(x_ref, s_ref, z_ref):
    count, size = x_ref.shape[0], x_ref.shape[1]
    for number in range(count):
        high = low(x_ref[number])
        z_ref[number, :, :size] = high
        s_ref[number, :, :size] = low(nt(high, high))
    for number in range(count):
        product = nn(s_ref[number, :, :size], z_ref[number, :, :size])
        x_ref[number] = 1.5 * x_ref[number] - 0.5 * product


def adam_terms(gradient, first, second):
    first_new = MOMENT_DECAY * first + (1.0 - MOMENT_DECAY) * gradient
    second_new = MOMENT_DECAY * second + (1.0 - MOMENT_DECAY) * gradient * gradient
    correction = 1.0 - MOMENT_DECAY**STEP
    direction = first_new / correction / (jnp.sqrt(second_new / correction) + ADAM_EPS)
    return first_new, second_new, direction


def optimizer_kernel(shift_ref, *refs, terms, vectors, held):
    grads, refs = refs[:terms], refs[terms:]
    master_ref, first_ref, second_ref, left_ref, right_ref, left_basis, right_basis = refs[:7]
    vec_in, refs = refs[7 : 7 + vectors], refs[7 + vectors + held :]
    new_master, new_first, new_second, new_left, new_right = refs[:5]
    new_left_basis, new_right_basis = refs[5:7]
    vec_out, (g_ref, x_ref, s_ref, z_ref, p_ref) = refs[7 : 7 + vectors], refs[7 + vectors :]
    count, side, height = master_ref.shape
    keep = MOMENT_DECAY

    def unit(matrix):
        total = jnp.sum(jnp.sum(matrix * matrix, axis=1, keepdims=True), axis=0, keepdims=True)
        return matrix * lax.rsqrt(total + 1e-06)

    g_ref[...] = fold(*[one[...] for one in grads])
    for pair in range((count + 1) // 2):
        x_ref[count + pair] = jnp.zeros((height, height), F32)
    for block in range(count):
        gradient = g_ref[span(block, side)]
        new_left[block] = keep * left_ref[block] + (1.0 - keep) * tn(gradient, gradient)
        new_right[block] = keep * right_ref[block] + (1.0 - keep) * nt(gradient, gradient)
    for block in range(count):
        x_ref[block] = unit(fine(nn, new_left[block], left_basis[block]))
        corner = span(block % 2, side)
        x_ref[count + block // 2, corner, corner] = unit(
            fine(nn, new_right[block], right_basis[block])
        )

    def rough(number, carry):
        early_turn(x_ref, s_ref, z_ref)
        return carry

    def turn(number, carry):
        newton_turn(x_ref, s_ref, z_ref)
        return carry

    lax.fori_loop(0, EARLY_TURNS, rough, 0, unroll=True)
    lax.fori_loop(EARLY_TURNS, NEWTON_TURNS, turn, 0, unroll=True)
    for block in range(count):
        corner = span(block % 2, side)
        new_left_basis[block] = x_ref[block]
        new_right_basis[block] = x_ref[count + block // 2, corner, corner]
    for block in range(count):
        high, rest = halves(new_left_basis[block])
        gradient = g_ref[span(block, side)]
        partway = nn(gradient, high) + nn(gradient, rest)
        turned = fine(tn, new_right_basis[block], partway)
        new_first[block], new_second[block], p_ref[block] = adam_terms(
            turned, first_ref[block], second_ref[block]
        )
    for block in range(count):
        partback = fine(nn, new_right_basis[block], p_ref[block])
        step = fine(nt, partback, new_left_basis[block])
        new_master[block] = (
            master_ref[block] * (1.0 - LEARN_RATE * WEIGHT_DECAY) - LEARN_RATE * step
        )
    if vectors:
        vec_ref, vec_first, vec_second = vec_in
        rows, columns = vec_ref.shape
        tail = pltpu.roll(g_ref[count * side :].astype(F32), shift_ref[0], 1)
        vec_out[1][...], vec_out[2][...], direction = adam_terms(
            tail[:rows, :columns], vec_first[...], vec_second[...]
        )
        vec_out[0][...] = vec_ref[...] - VECTOR_RATE * direction


def optimize(shift, grads, arrays, number, count, vectors, before):
    def part(one):
        return pl.BlockSpec((count,) + one.shape[1:], lambda step: (number, 0, 0))

    side, height = arrays[0].shape[1:]
    matrices = count + (count + 1) // 2
    inputs = [shift, *grads, *arrays, *vectors]
    whole = [pl.BlockSpec(one.shape, lambda step: (0, 0)) for one in vectors]
    return pl.pallas_call(
        functools.partial(
            optimizer_kernel, terms=len(grads), vectors=len(vectors), held=len(before)
        ),
        grid=(1,),
        out_shape=[shape(*one.shape) for one in [*arrays, *vectors]],
        in_specs=[SMEM]
        + [pl.BlockSpec(one.shape, lambda step: (0, 0)) for one in grads]
        + [part(one) for one in arrays]
        + whole
        + [pl.BlockSpec(memory_space=pl.ANY)] * len(before),
        out_specs=[part(one) for one in arrays] + whole,
        input_output_aliases={len(inputs) + place: place for place in range(len(before))},
        scratch_shapes=[
            pltpu.VMEM(grads[0].shape, BF16),
            pltpu.VMEM((matrices, height, height), F32),
            pltpu.VMEM((matrices, height, 2 * height), BF16),
            pltpu.VMEM((matrices, height, 2 * height), BF16),
            pltpu.VMEM((count, side, height), F32),
        ],
        compiler_params=limit(24),
        cost_estimate=pl.CostEstimate(
            flops=matrices * NEWTON_TURNS * 8 * height**3, bytes_accessed=16 * MIB, transcendentals=0
        ),
        name="optimizer",
    )(*inputs, *before)


def own_rows(values, index, chunk):
    early = lax.dynamic_slice_in_dim(values, index * chunk, chunk, 0)
    late = lax.dynamic_slice_in_dim(values, (3 - index) * chunk, chunk, 0)
    return jnp.concatenate([early, late], axis=0)


def in_order(mine, other, index, chunk):
    inner = jnp.where(index == 0, other, mine)
    outer = jnp.where(index == 0, mine, other)
    return jnp.concatenate([outer[:chunk], inner, outer[chunk:]], axis=0)


def token_outputs(own_output, part_input, part_encoder, core, chunk):
    return (
        in_order(own_output, swapped(own_output), core, chunk),
        part_input.astype(F32) + swapped(part_input).astype(F32),
        part_encoder.astype(F32) + swapped(part_encoder).astype(F32),
    )


def key_bounds(key_ids, query_ids, chunk):
    rows = query_ids.reshape(-1, chunk)
    lowest = jnp.sum((key_ids[None] < rows[:, :1]).astype(jnp.int32), axis=1, keepdims=True)
    highest = jnp.sum((key_ids[None] <= rows[:, -1:]).astype(jnp.int32), axis=1, keepdims=True)
    return jnp.concatenate([lowest, highest + (chunk - 1)], axis=1) // chunk


def per_device(
    decoder_input,
    encoder_states,
    decoder_segments,
    encoder_segments,
    output_cotangent,
    block_slots,
    master,
    first_moment,
    second_moment,
    row_statistics,
    column_statistics,
    row_basis,
    column_basis,
    vectors,
    vector_first,
    vector_second,
):
    core = lax.axis_index("tensor")
    cores = lax.axis_size("tensor")
    ring, rings = lax.axis_index("dp"), lax.axis_size("dp")
    owned_count, block_height = master.shape[1], master.shape[2]
    vector_cols = vectors.shape[1]
    length, width = decoder_input.shape[1], decoder_input.shape[2]
    row_count = width // block_height
    block_total = block_slots.shape[0]
    column_count = block_total // row_count
    chunk = length // 4
    per_ring = owned_count * HD + VECTOR_ROWS
    group = block_height // vector_cols

    payload = low(master[0]).transpose(0, 2, 1).reshape(owned_count * HD, block_height)
    lane = jnp.arange(block_height) // vector_cols
    here = lane == ring % group
    small = jnp.where(here[None], jnp.tile(low(vectors), (1, group)), jnp.zeros((), BF16))
    small = jnp.pad(small, ((0, VECTOR_ROWS - vectors.shape[0]), (0, 0)))
    tokens, encoder_rows = decoder_input[0], encoder_states[0]
    ids, encoder_ids = decoder_segments[0], encoder_segments[0]
    own_tokens = own_rows(tokens, core, chunk)
    own_ids = own_rows(ids, core, chunk)
    own_cotangent = own_rows(output_cotangent[0], core, chunk)
    places = jnp.arange(length, dtype=jnp.int32)
    own_places = own_rows(places, core, chunk)
    self_allowed = (ids[:, None] == own_ids[None, :]) & (places[:, None] <= own_places[None, :])
    self_bias = jnp.where(self_allowed, 0.0, NEGATIVE).astype(F32)
    cross_bias = jnp.where(encoder_ids[:, None] == own_ids[None, :], 0.0, NEGATIVE).astype(F32)
    here_and_core = jnp.full((1,), core, jnp.int32)
    ends = jnp.stack([here_and_core + 1, 4 - here_and_core])
    self_edges = jnp.concatenate([key_bounds(ids, own_ids, chunk)[:, :1], ends], axis=1)
    self_scalars = jnp.concatenate([self_edges.reshape(-1), here_and_core])
    cross_edges = key_bounds(encoder_ids, own_ids, chunk)
    cross_scalars = jnp.concatenate([cross_edges.reshape(-1), here_and_core])

    payload = jnp.concatenate([payload, small], axis=0)
    owner, local = block_slots // owned_count, block_slots % owned_count
    chips = jnp.arange(rings, dtype=jnp.int32)
    grid_of_chips = rings == DEPTH * SIDE * SIDE
    if grid_of_chips:
        starts = apart(ring, owner, 1) * per_ring + local * HD
        slices = [(index ^ core) * rings * per_ring for index in range(cores)]
        ends = (apart(ring, chips, 1) + 1) * per_ring - VECTOR_ROWS
        early_count = owned_count // 2
        sizes = (early_count * HD, per_ring - early_count * HD)
        order = jnp.array(PLACES, jnp.int32)
        late = local // early_count
        sum_rows = local % early_count * HD + jnp.where(
            late == 1,
            rings * sizes[0] + order[apart(ring, owner, -1)] * sizes[1],
            order[apart(ring, owner, -1)] * sizes[0],
        )
        sum_ends = rings * sizes[0] + (order[apart(ring, chips, -1)] + 1) * sizes[1] - VECTOR_ROWS
    else:
        starts = owner * cores * per_ring + local * HD
        slices = [index * per_ring for index in range(cores)]
        ends = (chips * cores + 1) * per_ring - VECTOR_ROWS
        sum_rows = owner * per_ring + local * HD
        sum_ends = (chips + 1) * per_ring - VECTOR_ROWS
    starts = jnp.concatenate([starts + start for start in slices])
    beside = (starts, ends, own_tokens, own_cotangent, self_bias, cross_bias)
    beside += (self_scalars, cross_scalars, sum_rows, sum_ends)
    if grid_of_chips:
        pieces, beside = gather_chips(payload, beside)
        pieces += [swapped(piece) for piece in pieces]
    else:
        pieces = [lax.all_gather(payload, ("dp", "tensor"), axis=0, tiled=True)]
    starts, ends, own_tokens, own_cotangent, self_bias, cross_bias, *scalars = beside
    self_scalars, cross_scalars, sum_rows, sum_ends = scalars
    layer = call_layer(
        (self_scalars, cross_scalars, starts, ends),
        pieces,
        (tokens, own_tokens, self_bias, encoder_rows, cross_bias, own_cotangent),
        cores,
        group,
    )
    own_output, ff_mine, cross_mine, sent, part_encoder, grad_one, norms = layer[:7]
    w_self, q_self, k_self, lse_self, ctxt_self = layer[7:]
    self_mine, self_sent, part_input = call_self_backward(
        self_scalars,
        (grad_one, ctxt_self, w_self, q_self, tokens, own_tokens, k_self, lse_self, self_bias),
    )

    terms = (ff_mine, cross_mine, swapped(sent), self_mine, swapped(self_sent), norms)
    shift = ((block_height - ring % group * vector_cols) % block_height)[None]
    arrays = [one[0].transpose(0, 2, 1) for one in (master, first_moment, second_moment)]
    arrays += [
        one[0] for one in (row_statistics, column_statistics, row_basis, column_basis)
    ]
    vector_states = [vectors, vector_first, vector_second]
    if grid_of_chips:
        cuts = [size * places for size in sizes for places in (4, 4, 2, 2, 4)]
        parts = scatter(sum_rows, sum_ends, terms, cuts, cores, block_height, group)
        own_output, part_encoder, part_input, parts = lax.optimization_barrier(
            (own_output, part_encoder, part_input, parts)
        )
        tokens_out = token_outputs(own_output, part_input, part_encoder, core, chunk)
        column, tokens_out = reduce_plane(*parts[:5], tokens_out)
        block_output, input_gradient, encoder_gradient = tokens_out
        column, parts = lax.optimization_barrier((column, parts[5:]))
        column, early = reduce_plane(*parts, reduce_column(column))
        updated = optimize(shift, early, arrays, 0, early_count, [], [])
        updated = optimize(
            shift, reduce_column(column), arrays, 1, early_count, vector_states, updated
        )
    else:
        (whole,) = scatter(
            sum_rows,
            sum_ends,
            terms,
            [rings * per_ring],
            cores,
            block_height,
            group,
        )
        summed = lax.psum_scatter(whole, "dp", scatter_dimension=0, tiled=True)
        updated = optimize(shift, [summed], arrays, 0, owned_count, vector_states, [])
        tokens_out = token_outputs(own_output, part_input, part_encoder, core, chunk)
        block_output, input_gradient, encoder_gradient = tokens_out

    return (
        block_output[None],
        input_gradient[None],
        encoder_gradient[None],
        *[one.transpose(0, 2, 1)[None] for one in updated[:3]],
        *[one[None] for one in updated[3:7]],
        *updated[7:],
    )


def solution(mesh):
    blocks = P("tensor", "dp", None, None)
    rows = P("dp", None, None)
    return jax.shard_map(
        per_device,
        mesh=mesh,
        in_specs=(rows, rows, P("dp", None), P("dp", None), rows, P())
        + (blocks,) * 7
        + (P(None, "dp"),) * 3,
        out_specs=(rows,) * 3 + (blocks,) * 7 + (P(None, "dp"),) * 3,
        check_vma=False,
    )
```

```python
import functools

import jax
import jax.numpy as jnp
from jax import lax
from jax.experimental import pallas as pl
from jax.experimental.pallas import tpu as pltpu
from jax.sharding import PartitionSpec as P

HD = 64
FF = 2048
STEP = 10

NEGATIVE = -1e30
EPS_NORM = 1e-05
MOMENT_DECAY = 0.5
LEARN_RATE = 0.04
WEIGHT_DECAY = 0.01
VECTOR_RATE = 0.25
ADAM_EPS = 1e-08
NEWTON_TURNS = 8
EARLY_TURNS = 5
VECTOR_ROWS = 16
DEPTH, SIDE = 4, 2
MIB = 2**20
F32 = jnp.float32
BF16 = jnp.bfloat16
VMEM = pl.BlockSpec(memory_space=pltpu.VMEM)
SMEM = pl.BlockSpec(memory_space=pltpu.SMEM)
ANY = pl.BlockSpec(memory_space=pl.ANY)


def nn(left, right):
    return lax.dot_general(left, right, (((1,), (0,)), ((), ())), preferred_element_type=F32)


def nt(left, right):
    return lax.dot_general(left, right, (((1,), (1,)), ((), ())), preferred_element_type=F32)


def tn(left, right):
    return lax.dot_general(left, right, (((0,), (0,)), ((), ())), preferred_element_type=F32)


def low(values):
    return values.astype(BF16)


def span(number, size):
    return slice(number * size, (number + 1) * size)


def rows_at(number, size):
    return pl.ds(pl.multiple_of(number * size, size), size)


def shape(*dims, dtype=F32):
    return jax.ShapeDtypeStruct(dims, dtype)


def scratch(shapes):
    return [pltpu.VMEM(one.shape, one.dtype) for one in shapes]


def limit(mib):
    return pltpu.CompilerParams(vmem_limit_bytes=mib * MIB)


def block_places(columns, cores):
    hidden = FF // cores // HD
    heads = (columns - 2 * hidden) // 8
    places = []
    for column in range(columns):
        if column < 8 * heads:
            places.append((column // heads, column % heads * HD))
        else:
            column -= 8 * heads
            places.append((8 + column // hidden, column % hidden * HD))
    return places, heads * HD, hidden * HD


def start_copies(pairs, semaphores, first=0):
    copies = [
        pltpu.make_async_copy(source, target, semaphores.at[first + number])
        for number, (source, target) in enumerate(pairs)
    ]
    for copy in copies:
        copy.start()
    return copies


def wait_for(copies):
    for copy in copies:
        copy.wait()


def in_a_row(pieces, target_ref):
    pairs, start = [], 0
    for piece in pieces:
        pairs.append((piece, target_ref.at[pl.ds(start, piece.shape[0])]))
        start += piece.shape[0]
    return pairs


def assemble(rows_ref, ends_ref, gathered_ref, w_refs, vec_ref, cores, group):
    height = gathered_ref.shape[1]
    row_count = vec_ref.shape[1] // height
    total = rows_ref.shape[0] // cores
    columns = total // row_count
    places, head_rows, hidden_rows = block_places(columns, cores)
    for core in range(cores):
        for row in range(row_count):
            for column in range(columns):
                kind, inner = places[column]
                size = head_rows if kind < 8 else hidden_rows
                target = (kind % 4 * cores + core) * size + inner
                source = pl.multiple_of(rows_ref[core * total + row * columns + column], 16)
                block = gathered_ref[pl.ds(source, HD), :]
                w_refs[kind // 4][target : target + HD, span(row, height)] = block
    rings = ends_ref.shape[0]
    for part in range(row_count):
        values = jnp.zeros((VECTOR_ROWS, height), F32)
        for ring in range(part * group, min((part + 1) * group, rings)):
            start = pl.multiple_of(ends_ref[ring], 16)
            values = values + gathered_ref[pl.ds(start, VECTOR_ROWS), :].astype(F32)
        vec_ref[:, span(part, height)] = values


def scatter_kernel(rows_ref, ends_ref, *refs, cores, group, cuts):
    ff_mine, cross_mine, arrived, self_mine, self_in, vec_ref = refs[:6]
    outs, refs = refs[6 : 6 + cuts], refs[6 + cuts :]
    terms, (all_ref, in_sems, out_sems) = refs[:7], refs[7:]
    ff_in, cross_in, vec_in = in_a_row((terms[1], terms[3], terms[6]), arrived)
    pairs = [(ff_mine, terms[0]), ff_in[::-1], (cross_mine, terms[2]), cross_in[::-1]]
    pairs += [(self_mine, terms[4]), (self_in, terms[5]), vec_in[::-1]]
    copies = start_copies(pairs, in_sems)
    height = all_ref.shape[1]
    row_count = vec_ref.shape[1] // height
    columns = rows_ref.shape[0] // row_count
    places, head_rows, hidden_rows = block_places(columns, cores)
    for part, (first, last, size) in enumerate(
        ((8, 10, hidden_rows), (4, 8, head_rows), (0, 4, head_rows))
    ):
        one, two = terms[2 * part : 2 * part + 2]
        wait_for(copies[2 * part : 2 * part + 2])
        for column in range(columns):
            kind, inner = places[column]
            if first <= kind < last:
                start = (kind - first) * size + inner
                for row in range(row_count):
                    here = slice(start, start + HD), span(row, height)
                    target = pl.multiple_of(rows_ref[row * columns + column], 16)
                    total = one[here].astype(F32) + two[here].astype(F32)
                    all_ref[pl.ds(target, HD), :] = low(total)
    wait_for(copies[6:])
    total = low(vec_ref[...] + terms[6][...].astype(F32))
    for ring in range(ends_ref.shape[0]):
        start = pl.multiple_of(ends_ref[ring], 16)
        all_ref[pl.ds(start, VECTOR_ROWS), :] = total[:, span(ring // group, height)]
    pairs = [(part, out) for out, part in in_a_row(outs, all_ref)]
    wait_for(start_copies(pairs, out_sems))


def scatter(rows, ends, terms, cuts, cores, height, group):
    return pl.pallas_call(
        functools.partial(scatter_kernel, cores=cores, group=group, cuts=len(cuts)),
        out_shape=[shape(cut, height, dtype=BF16) for cut in cuts],
        in_specs=[SMEM, SMEM] + [ANY] * 5 + [VMEM],
        out_specs=[ANY] * len(cuts),
        scratch_shapes=scratch([*terms[:1] * 2, *terms[1:2] * 2, *terms[3:4] * 2])
        + [
            pltpu.VMEM(terms[5].shape, BF16),
            pltpu.VMEM((sum(cuts), height), BF16),
            pltpu.SemaphoreType.DMA((7,)),
            pltpu.SemaphoreType.DMA((len(cuts),)),
        ],
        compiler_params=limit(63),
        name="scatter",
    )(rows, ends, *terms)


def hop(values, *steps):
    sizes = (DEPTH, SIDE, SIDE)
    pairs = []
    for source in range(DEPTH * SIDE * SIDE):
        place = (source // (SIDE * SIDE), source // SIDE % SIDE, source % SIDE)
        z, y, x = ((one + step) % size for one, step, size in zip(place, steps, sizes))
        pairs.append((source, (z * SIDE + y) * SIDE + x))
    return lax.ppermute(values, "dp", pairs)


def swapped(values):
    return lax.ppermute(values, "tensor", [(0, 1), (1, 0)])


def apart(ring, other, sign):
    side = SIDE * SIDE
    deep = (sign * (ring // side - other // side)) % DEPTH
    across = (ring // SIDE % SIDE) ^ (other // SIDE % SIDE)
    return (across * SIDE + ((ring % SIDE) ^ (other % SIDE))) * DEPTH + deep


def gather_chips(own, beside):
    deep = [hop(own, step, 0, 0) for step in range(1, DEPTH)]
    near = [hop(own, 0, 0, 1), hop(own, 0, 1, 0), hop(own, 0, 1, 1)]
    deep, near, beside = lax.optimization_barrier((jnp.concatenate(deep, axis=0), near, beside))
    by_x, by_y = hop(deep, 0, 0, 1), hop(deep, 0, 1, 0)
    cut = deep.shape[0] // 32 * 16
    pieces = [own, deep, near[0], by_x, near[1], by_y, near[2]]
    return pieces + [hop(by_y[:cut], 0, 0, 1), hop(by_x[cut:], 0, 1, 0)], beside


PLACES = (12, 13, 14, 15, 2, 3, 10, 11, 8, 9, 6, 7, 0, 1, 4, 5)


def fold(*terms):
    return low(functools.reduce(lambda one, two: one + two, [term.astype(F32) for term in terms]))


def reduce_plane(along_x, along_y, late_y, late_x, here, beside):
    half = late_x.shape[0]
    from_x, from_y = hop(along_x, 0, 0, 1), hop(along_y, 0, 1, 0)
    from_x, from_y, beside = lax.optimization_barrier((from_x, from_y, beside))
    more_y = hop(fold(late_y, from_x[:half]), 0, 1, 0)
    more_x = hop(fold(late_x, from_y[:half]), 0, 0, 1)
    column = jnp.concatenate(
        [fold(here[:half], from_x[half:], more_y), fold(here[half:], from_y[half:], more_x)],
        axis=0,
    )
    return column, beside


def reduce_column(column):
    rows = column.shape[0] // DEPTH
    return [column[:rows]] + [
        hop(column[step * rows : (step + 1) * rows], step, 0, 0) for step in range(1, DEPTH)
    ]


def norm_forward(total_ref, vec_ref, first, hat_ref, inverse_ref, out_ref, step=64):
    gain, shift = vec_ref[first : first + 1], vec_ref[first + 1 : first + 2]

    def body(number, carry):
        rows = rows_at(number, step)
        values = total_ref[rows]
        center = values - jnp.mean(values, axis=1, keepdims=True)
        inverse = lax.rsqrt(jnp.mean(center * center, axis=1, keepdims=True) + EPS_NORM)
        hat = center * inverse
        hat_ref[rows] = hat
        inverse_ref[rows] = inverse
        out_ref[rows] = (hat * gain + shift).astype(out_ref.dtype)
        return carry

    lax.fori_loop(0, total_ref.shape[0] // step, body, 0, unroll=8)


def norm_backward(grad_ref, hat_ref, inverse_ref, gain, out_ref, step=64):
    width = grad_ref.shape[1]

    def body(number, carry):
        rows = rows_at(number, step)
        grad, hat = grad_ref[rows].astype(F32), hat_ref[rows]
        scaled = grad * gain
        middle = jnp.mean(scaled, axis=1, keepdims=True)
        slope = jnp.mean(scaled * hat, axis=1, keepdims=True)
        out_ref[rows] = (scaled - middle - hat * slope) * inverse_ref[rows]
        return (
            carry[0] + jnp.sum((grad * hat).reshape(step // 8, 8, width), axis=0),
            carry[1] + jnp.sum(grad.reshape(step // 8, 8, width), axis=0),
        )

    zeros = jnp.zeros((8, width), F32)
    sums = lax.fori_loop(0, grad_ref.shape[0] // step, body, (zeros, zeros), unroll=8)
    return [jnp.sum(one, axis=0, keepdims=True) for one in sums]


def split_heads(source_ref, masked_ref, factor):
    for head in range(masked_ref.shape[0]):
        pair = source_ref[:, span(head // 2, 2 * HD)]
        lane = lax.broadcasted_iota(jnp.int32, pair.shape, 1)
        here = (lane >= HD) if head % 2 else (lane < HD)
        masked_ref[head] = jnp.where(here, pair, jnp.zeros_like(pair)) * jnp.asarray(factor, BF16)


def staged(count, early, middle, late, ahead=2, lag=2):
    ready = [early(number) for number in range(min(ahead, count))]
    held = []
    for number in range(count):
        now = ready.pop(0)
        if number + ahead < count:
            ready.append(early(number + ahead))
        held.append((number, middle(number, now)))
        if len(held) > lag:
            late(*held.pop(0))
    while held:
        late(*held.pop(0))


def attend_forward(bounds_ref, bias_ref, masked_q, k_ref, vt_ref, m_ref, l_ref, acc_ref, lse_ref,
                   ctxt_ref):
    heads, chunk = m_ref.shape
    for part in range(lse_ref.shape[1] // chunk):
        cols = span(part, chunk)
        m_ref[...] = jnp.full(m_ref.shape, NEGATIVE, F32)
        l_ref[...] = jnp.zeros(l_ref.shape, F32)
        acc_ref[...] = jnp.zeros(acc_ref.shape, F32)

        def body(number, carry):
            keys = rows_at(number, chunk)
            bias = bias_ref[keys, cols]

            def early(head):
                return nt(k_ref[keys, span(head // 2, 2 * HD)], masked_q[head, cols]) + bias

            def middle(head, scores):
                row = slice(head, head + 1)
                before = m_ref[row]
                highest = jnp.maximum(before, jnp.max(scores, axis=0, keepdims=True))
                shrink = jnp.exp(before - highest)
                expons = jnp.exp(scores - highest)
                l_ref[row] = l_ref[row] * shrink + jnp.sum(expons, axis=0, keepdims=True)
                m_ref[row] = highest
                return shrink, low(expons)

            def late(head, pair):
                rows = span(head, HD)
                acc_ref[rows] = acc_ref[rows] * pair[0] + nn(vt_ref[rows, keys], pair[1])

            staged(heads, early, middle, late)
            return carry

        lax.fori_loop(bounds_ref[2 * part], bounds_ref[2 * part + 1], body, 0)
        for head in range(heads):
            rows = span(head, HD)
            ctxt_ref[rows, cols] = low(acc_ref[rows] / l_ref[head : head + 1])
        lse_ref[:, cols] = m_ref[...] + jnp.log(l_ref[...])


def branch_forward(bounds_ref, x_ref, own_ref, w_ref, bias_ref, vec_ref,
                   q_ref, k_ref, lse_ref, ctxt_ref, hat_ref, inverse_ref, y_ref, first):
    keys, width = k_ref.shape
    heads, queries = lse_ref.shape
    chunk = keys // 4

    def body(masked_q, vt_ref, m_ref, l_ref, acc_ref):
        q_ref[...] = low(nt(low(own_ref[...]), w_ref[span(0, width)]))
        split_heads(q_ref, masked_q, HD**-0.5)
        k_ref[...] = low(nt(x_ref[...], w_ref[span(1, width)]))
        vt_ref[...] = low(nt(w_ref[span(2, width)], x_ref[...]))
        attend_forward(
            bounds_ref, bias_ref, masked_q, k_ref, vt_ref, m_ref, l_ref, acc_ref, lse_ref, ctxt_ref
        )
        y_ref[...] = own_ref[...].astype(F32) + tn(ctxt_ref[...], w_ref[span(3, width)])
        norm_forward(y_ref, vec_ref, first, hat_ref, inverse_ref, y_ref)

    pl.run_scoped(
        body,
        pltpu.VMEM((heads, queries, 2 * HD), BF16),
        pltpu.VMEM((width, keys), BF16),
        pltpu.VMEM((heads, chunk), F32),
        pltpu.VMEM((heads, chunk), F32),
        pltpu.VMEM((width, chunk), F32),
    )


def branch_backward(scalars_ref, x_ref, own_ref, w_ref, bias_ref, grad_ref, q_ref, k_ref, lse_ref,
                    ctxt_ref, mine_ref, sent_ref, part_ref, norm, arrive):
    heads, queries = lse_ref.shape
    keys, width = k_ref.shape
    chunk = queries // 2

    def body(masked_q, masked_g, v_ref, kt_ref, delta_ref, dqt_ref, dk_ref, dv_ref, dq_ref, out_ref):
        core = scalars_ref[4]
        half = width // 2
        arrive(0)

        def keep(kind, gradient):
            out_ref[...] = low(gradient)
            mine_ref[span(kind, half)] = out_ref[rows_at(core, half)]
            sent_ref[span(kind, half)] = out_ref[rows_at(1 - core, half)]

        grad_low = low(grad_ref[...])
        w_out = w_ref[span(3, width)]
        keep(3, nn(ctxt_ref[...], grad_low))
        out_ref[...] = low(nt(grad_low, w_out))
        split_heads(out_ref, masked_g, 1.0)
        arrive(1)
        split_heads(q_ref, masked_q, HD**-0.5)
        grad_t = low(nt(w_out, grad_low)).astype(F32) * ctxt_ref[...].astype(F32)
        for head in range(heads):
            delta_ref[head : head + 1] = jnp.sum(grad_t[span(head, HD)], axis=0, keepdims=True)
        v_ref[...] = low(nt(x_ref[...], w_ref[span(2, width)]))
        kt_ref[...] = low(nt(w_ref[span(1, width)], x_ref[...]))
        dqt_ref[...] = jnp.zeros(dqt_ref.shape, F32)
        dk_ref[...] = jnp.zeros(dk_ref.shape, F32)
        dv_ref[...] = jnp.zeros(dv_ref.shape, F32)
        for part in range(2):
            cols = span(part, chunk)

            def pair(number, carry):
                keys = rows_at(number, chunk)
                bias = bias_ref[keys, cols]

                def early(head):
                    pair = span(head // 2, 2 * HD)
                    return (
                        nt(k_ref[keys, pair], masked_q[head, cols]) + bias,
                        nt(v_ref[keys, pair], masked_g[head, cols]),
                    )

                def middle(head, both):
                    row = slice(head, head + 1)
                    chances = jnp.exp(both[0] - lse_ref[row, cols])
                    return low(chances), low(chances * (both[1] - delta_ref[row, cols]))

                def late(head, both):
                    pair, rows = span(head // 2, 2 * HD), span(head, HD)
                    dv_ref[keys, pair] += nn(both[0], masked_g[head, cols])
                    dk_ref[keys, pair] += nn(both[1], masked_q[head, cols])
                    dqt_ref[rows, cols] += nn(kt_ref[rows, keys], both[1])

                staged(heads, early, middle, late)
                return carry

            lax.fori_loop(scalars_ref[2 * part], scalars_ref[2 * part + 1], pair, 0)
        dqt = low(dqt_ref[...] * HD**-0.5)
        keep(0, nn(dqt, low(own_ref[...])))
        dk, dv = low(dk_ref[...]), low(dv_ref[...])
        keep(1, tn(dk, x_ref[...]))
        keep(2, tn(dv, x_ref[...]))
        dq_ref[...] = grad_ref[...] + tn(dqt, w_ref[span(0, width)])
        if norm is not None:
            part_ref[...] = low(nn(dk, w_ref[span(1, width)]) + nn(dv, w_ref[span(2, width)]))
            hat_ref, inverse_ref, gain, next_ref, norms_ref, place = norm
            sums = norm_backward(dq_ref, hat_ref, inverse_ref, gain, next_ref)
            norms_ref[place : place + 1] = sums[0]
            norms_ref[place + 1 : place + 2] = sums[1]
        else:
            dk_ref[...] = nn(dk, w_ref[span(1, width)]) + nn(dv, w_ref[span(2, width)])
            for part, place in enumerate((core, 3 - core)):
                dk_ref[rows_at(place, chunk)] += dq_ref[span(part, chunk)]
            part_ref[...] = low(dk_ref[...])

    pl.run_scoped(
        body,
        pltpu.VMEM((heads, queries, 2 * HD), BF16),
        pltpu.VMEM((heads, queries, 2 * HD), BF16),
        pltpu.VMEM((keys, width), BF16),
        pltpu.VMEM((width, keys), BF16),
        pltpu.VMEM((heads, queries), F32),
        pltpu.VMEM((width, queries), F32),
        pltpu.VMEM((keys, width), F32),
        pltpu.VMEM((keys, width), F32),
        pltpu.VMEM((queries, width), F32),
        pltpu.VMEM((width, width), BF16),
    )


def gelu_both(values):
    scale = (2.0 / jnp.pi) ** 0.5
    square = values * values
    bend = jnp.tanh(values * (scale + scale * 0.044715 * square))
    half = 0.5 + 0.5 * bend
    slope = half + (0.5 * values) * (1.0 - bend * bend) * (scale + 3.0 * scale * 0.044715 * square)
    return values * half, slope


def feed_both(core, y_ref, w_ref, vec_ref, cot_ref, hat_two, inverse_two,
              block_ref, next_ref, mine_ref, sent_ref, norms_ref, arrive, step=256):
    queries, width = y_ref.shape
    hidden = w_ref.shape[0] // 2
    half = hidden // 2
    chunks = hidden // step

    def body(low_ref, hid_ref, slope_ref, total_ref, hat_ref, inverse_ref, grad_low):
        low_ref[...] = low(y_ref[...])
        total_ref[...] = y_ref[...]

        def early(number):
            return nt(w_ref[span(number, step)], low_ref[...])

        def middle(number, up):
            hid, slope = gelu_both(up)
            hid_ref[span(number, step)] = low(hid)
            slope_ref[span(number, step)] = slope

        def late(number, _):
            lower = w_ref[hidden + number * step : hidden + (number + 1) * step]
            total_ref[...] += tn(hid_ref[span(number, step)], lower)

        staged(chunks, early, middle, late, 1, 1)
        norm_forward(total_ref, vec_ref, 4, hat_ref, inverse_ref, block_ref)
        sums = norm_backward(cot_ref, hat_ref, inverse_ref, vec_ref[4:5], total_ref)
        norms_ref[4:5] = sums[0]
        norms_ref[5:6] = sums[1]
        grad_low[...] = low(total_ref[...])

        def place(number):
            inner = number % (chunks // 2)
            row = (core if number < chunks // 2 else 1 - core) * half + inner * step
            return inner, pl.multiple_of(row, step)

        def down(number):
            row = place(number)[1]
            return nt(w_ref[pl.ds(pl.multiple_of(hidden + row, step), step)], grad_low[...])

        def turn(number, grad_hidden):
            return low(slope_ref[pl.ds(place(number)[1], step)] * grad_hidden)

        def sums_of(number, grad_up):
            inner, row = place(number)
            rows = pl.ds(row, step)
            kept = mine_ref if number < chunks // 2 else sent_ref
            kept[span(inner, step)] = low(nn(grad_up, low_ref[...]))
            kept[half + inner * step : half + (inner + 1) * step] = low(nn(hid_ref[rows], grad_low[...]))
            total_ref[...] += tn(grad_up, w_ref[rows])

        staged(chunks, down, turn, sums_of, 1, 1)
        sums = norm_backward(total_ref, hat_two, inverse_two, vec_ref[2:3], next_ref)
        norms_ref[2:3] = sums[0]
        norms_ref[3:4] = sums[1]

    pl.run_scoped(
        body,
        pltpu.VMEM((queries, width), BF16),
        pltpu.VMEM((hidden, queries), BF16),
        pltpu.VMEM((hidden, queries), F32),
        pltpu.VMEM((queries, width), F32),
        pltpu.VMEM((queries, width), F32),
        pltpu.VMEM((queries, 1), F32),
        pltpu.VMEM((queries, width), BF16),
    )


def layer_kernel(self_ref, cross_ref, rows_ref, ends_ref, *refs, cores, group, pieces):
    gathered, refs = refs[:pieces], refs[pieces:]
    ins, refs = refs[:6], refs[6:]
    block_out, ff_mine_out, mine_out, sent_out, part_out, next_out = refs[:6]
    norms_ref, w_out, q_out, k_out, lse_out, ctxt_out = refs[6:12]
    refs = refs[12:]
    w_self, w_cross, w_feed, vec_ref, x_ref, own_ref, bias_ref, enc_ref, bias_cross, cot_ref = refs[:10]
    self_saved, cross_saved, refs = refs[10:14], refs[14:18], refs[18:]
    hat_one, inverse_one, y_one, hat_two, inverse_two, y_two, refs = *refs[:6], refs[6:]
    block_ref, ff_mine, ff_sent, mine_ref, sent_ref, part_ref, grad_ref, next_ref = refs[:8]
    norms_low, refs = refs[8], refs[1:]
    sent_parts = [part for _, part in in_a_row((ff_sent, sent_ref, norms_low), sent_out)]
    piece_sems, in_sems, out_sems = refs[8:]
    norms_ref[...] = jnp.zeros(norms_ref.shape, F32)

    targets = (x_ref, own_ref, bias_ref, enc_ref, bias_cross, cot_ref)

    def fetch(gathered_ref):
        arriving = start_copies(in_a_row(gathered, gathered_ref), piece_sems)
        start_copies(zip(ins, targets), in_sems)
        wait_for(arriving)
        assemble(
            rows_ref, ends_ref, gathered_ref, (w_self, w_cross, w_feed), vec_ref, cores, group
        )

    total = sum(piece.shape[0] for piece in gathered)
    pl.run_scoped(fetch, pltpu.VMEM((total, gathered[0].shape[1]), BF16))
    arriving = [
        pltpu.make_async_copy(source, target, in_sems.at[number])
        for number, (source, target) in enumerate(zip(ins, targets))
    ]
    wait_for(arriving[:3])
    leaving = start_copies([(w_self, w_out)], out_sems)
    branch_forward(
        self_ref, x_ref, own_ref, w_self, bias_ref, vec_ref, *self_saved, hat_one, inverse_one,
        y_one, 0,
    )
    leaving += start_copies(zip(self_saved, (q_out, k_out, lse_out, ctxt_out)), out_sems, 1)
    wait_for(arriving[3:5])
    branch_forward(
        cross_ref, enc_ref, y_one, w_cross, bias_cross, vec_ref, *cross_saved, hat_two, inverse_two,
        y_two, 2,
    )
    wait_for(arriving[5:])
    feed_both(
        self_ref[4], y_two, w_feed, vec_ref, cot_ref, hat_two, inverse_two, block_ref, grad_ref,
        ff_mine, ff_sent, norms_ref, None,
    )
    pairs = [(block_ref, block_out), (ff_mine, ff_mine_out), (ff_sent, sent_parts[0])]
    leaving += start_copies(pairs, out_sems, 5)
    branch_backward(
        cross_ref, enc_ref, y_one, w_cross, bias_cross, grad_ref, *cross_saved, mine_ref, sent_ref,
        part_ref, (hat_one, inverse_one, vec_ref[0:1], next_ref, norms_ref, 0), lambda number: None,
    )
    norms_low[...] = low(norms_ref[...])
    pairs = [(mine_ref, mine_out), (sent_ref, sent_parts[1]), (norms_low, sent_parts[2])]
    pairs += [(part_ref, part_out), (next_ref, next_out)]
    leaving += start_copies(pairs, out_sems, 8)
    wait_for(leaving)


def saved_shapes(keys, queries, width):
    heads = width // HD
    return [
        shape(queries, width, dtype=BF16),
        shape(keys, width, dtype=BF16),
        shape(heads, queries),
        shape(width, queries, dtype=BF16),
    ]


def call_layer(scalars, pieces, inputs, cores, group):
    keys, queries = inputs[2].shape
    width = inputs[0].shape[1]
    saved = saved_shapes(keys, queries, width)
    weights = shape(4 * width, width, dtype=BF16)
    tokens = shape(queries, width)
    norm = [tokens, shape(queries, 1), tokens]
    own, feed = shape(queries, width, dtype=BF16), shape(FF, width, dtype=BF16)
    branch, rows = shape(2 * width, width, dtype=BF16), shape(keys, width, dtype=BF16)
    sent = shape(FF + 2 * width + VECTOR_ROWS, width, dtype=BF16)
    kept = [weights, weights, shape(2 * FF, width, dtype=BF16), shape(VECTOR_ROWS, width)]
    kept += [*inputs, *saved, *saved, *norm, *norm]
    kept += [own, feed, feed, branch, branch, rows, tokens, tokens]
    kept += [shape(VECTOR_ROWS, width, dtype=BF16)]
    norms = shape(VECTOR_ROWS, width)
    return pl.pallas_call(
        functools.partial(layer_kernel, cores=cores, group=group, pieces=len(pieces)),
        out_shape=[own, feed, branch, sent, rows, tokens, norms, weights, *saved],
        in_specs=[SMEM] * 4 + [ANY] * (len(pieces) + len(inputs)),
        out_specs=[ANY] * 6 + [VMEM] + [ANY] * 5,
        scratch_shapes=scratch(kept)
        + [
            pltpu.SemaphoreType.DMA((len(pieces),)),
            pltpu.SemaphoreType.DMA((6,)),
            pltpu.SemaphoreType.DMA((13,)),
        ],
        compiler_params=limit(56),
        name="layer",
    )(*scalars, *pieces, *inputs)


def self_backward_kernel(scalars_ref, *refs):
    ins, (mine_out, sent_out, part_out), refs = refs[:9], refs[9:12], refs[12:]
    grad_ref, ctxt_ref, w_ref, q_ref, x_ref, own_ref, k_ref, lse_ref, bias_ref = refs[:9]
    mine_ref, sent_ref, part_ref, in_sems, out_sems = refs[9:]
    copies = start_copies(zip(ins, refs[:9]), in_sems)
    branch_backward(
        scalars_ref, x_ref, own_ref, w_ref, bias_ref, grad_ref, q_ref, k_ref, lse_ref, ctxt_ref,
        mine_ref, sent_ref, part_ref, None,
        lambda number: wait_for(copies[3:] if number else copies[:3]),
    )
    pairs = [(mine_ref, mine_out), (sent_ref, sent_out), (part_ref, part_out)]
    wait_for(start_copies(pairs, out_sems))


def call_self_backward(scalars, inputs):
    keys, width = inputs[4].shape
    outs = [
        shape(2 * width, width, dtype=BF16),
        shape(2 * width, width, dtype=BF16),
        shape(keys, width, dtype=BF16),
    ]
    return pl.pallas_call(
        self_backward_kernel,
        out_shape=outs,
        in_specs=[SMEM] + [ANY] * 9,
        out_specs=[ANY] * 3,
        scratch_shapes=scratch([*inputs, *outs])
        + [pltpu.SemaphoreType.DMA((9,)), pltpu.SemaphoreType.DMA((3,))],
        compiler_params=limit(63),
        cost_estimate=pl.CostEstimate(
            flops=12 * 10**9, bytes_accessed=12 * MIB, transcendentals=0
        ),
        name="self_backward",
    )(scalars, *inputs)


def halves(values):
    high = low(values)
    return high, low(values - high.astype(F32))


def fine(dot, left, right):
    left_high, left_low = halves(left)
    right_high, right_low = halves(right)
    return dot(left_high, right_high) + (dot(left_high, right_low) + dot(left_low, right_high))


def newton_turn(x_ref, s_ref, z_ref):
    count, size = x_ref.shape[0], x_ref.shape[1]
    for number in range(count):
        high, rest = halves(x_ref[number])
        z_ref[number] = jnp.concatenate([high, rest], axis=1)
        right = jnp.concatenate(
            [jnp.concatenate([high, high], axis=1), jnp.concatenate([rest, rest], axis=1)], axis=0
        )
        product = nt(z_ref[number], right)
        high, rest = halves(product[:, :size] + product[:, size:])
        s_ref[number] = jnp.concatenate([high, rest], axis=1)
    for number in range(count):
        terms = z_ref[number]
        product = nn(s_ref[number], jnp.concatenate([terms, terms], axis=0))
        x_ref[number] = 1.5 * x_ref[number] - 0.5 * (product[:, :size] + product[:, size:])


def early_turn(x_ref, s_ref, z_ref):
    count, size = x_ref.shape[0], x_ref.shape[1]
    for number in range(count):
        high = low(x_ref[number])
        z_ref[number, :, :size] = high
        s_ref[number, :, :size] = low(nt(high, high))
    for number in range(count):
        product = nn(s_ref[number, :, :size], z_ref[number, :, :size])
        x_ref[number] = 1.5 * x_ref[number] - 0.5 * product


def adam_terms(gradient, first, second):
    first_new = MOMENT_DECAY * first + (1.0 - MOMENT_DECAY) * gradient
    second_new = MOMENT_DECAY * second + (1.0 - MOMENT_DECAY) * gradient * gradient
    correction = 1.0 - MOMENT_DECAY**STEP
    direction = first_new / correction / (jnp.sqrt(second_new / correction) + ADAM_EPS)
    return first_new, second_new, direction


def optimizer_kernel(shift_ref, *refs, terms, vectors, held):
    grads, refs = refs[:terms], refs[terms:]
    master_ref, first_ref, second_ref, left_ref, right_ref, left_basis, right_basis = refs[:7]
    vec_in, refs = refs[7 : 7 + vectors], refs[7 + vectors + held :]
    new_master, new_first, new_second, new_left, new_right = refs[:5]
    new_left_basis, new_right_basis = refs[5:7]
    vec_out, (g_ref, x_ref, s_ref, z_ref, p_ref) = refs[7 : 7 + vectors], refs[7 + vectors :]
    count, side, height = master_ref.shape
    keep = MOMENT_DECAY

    def unit(matrix):
        total = jnp.sum(jnp.sum(matrix * matrix, axis=1, keepdims=True), axis=0, keepdims=True)
        return matrix * lax.rsqrt(total + 1e-06)

    g_ref[...] = fold(*[one[...] for one in grads])
    for pair in range((count + 1) // 2):
        x_ref[count + pair] = jnp.zeros((height, height), F32)
    for block in range(count):
        gradient = g_ref[span(block, side)]
        new_left[block] = keep * left_ref[block] + (1.0 - keep) * tn(gradient, gradient)
        new_right[block] = keep * right_ref[block] + (1.0 - keep) * nt(gradient, gradient)
    for block in range(count):
        x_ref[block] = unit(fine(nn, new_left[block], left_basis[block]))
        corner = span(block % 2, side)
        x_ref[count + block // 2, corner, corner] = unit(
            fine(nn, new_right[block], right_basis[block])
        )

    def rough(number, carry):
        early_turn(x_ref, s_ref, z_ref)
        return carry

    def turn(number, carry):
        newton_turn(x_ref, s_ref, z_ref)
        return carry

    lax.fori_loop(0, EARLY_TURNS, rough, 0, unroll=True)
    lax.fori_loop(EARLY_TURNS, NEWTON_TURNS, turn, 0, unroll=True)
    for block in range(count):
        corner = span(block % 2, side)
        new_left_basis[block] = x_ref[block]
        new_right_basis[block] = x_ref[count + block // 2, corner, corner]
    for block in range(count):
        high, rest = halves(new_left_basis[block])
        gradient = g_ref[span(block, side)]
        partway = nn(gradient, high) + nn(gradient, rest)
        turned = fine(tn, new_right_basis[block], partway)
        new_first[block], new_second[block], p_ref[block] = adam_terms(
            turned, first_ref[block], second_ref[block]
        )
    for block in range(count):
        partback = nn(low(new_right_basis[block]), low(p_ref[block]))
        step = nt(low(partback), low(new_left_basis[block]))
        new_master[block] = (
            master_ref[block] * (1.0 - LEARN_RATE * WEIGHT_DECAY) - LEARN_RATE * step
        )
    if vectors:
        vec_ref, vec_first, vec_second = vec_in
        rows, columns = vec_ref.shape
        tail = pltpu.roll(g_ref[count * side :].astype(F32), shift_ref[0], 1)
        vec_out[1][...], vec_out[2][...], direction = adam_terms(
            tail[:rows, :columns], vec_first[...], vec_second[...]
        )
        vec_out[0][...] = vec_ref[...] - VECTOR_RATE * direction


def optimize(shift, grads, arrays, number, count, vectors, before):
    def part(one):
        return pl.BlockSpec((count,) + one.shape[1:], lambda step: (number, 0, 0))

    side, height = arrays[0].shape[1:]
    matrices = count + (count + 1) // 2
    inputs = [shift, *grads, *arrays, *vectors]
    whole = [pl.BlockSpec(one.shape, lambda step: (0, 0)) for one in vectors]
    return pl.pallas_call(
        functools.partial(
            optimizer_kernel, terms=len(grads), vectors=len(vectors), held=len(before)
        ),
        grid=(1,),
        out_shape=[shape(*one.shape) for one in [*arrays, *vectors]],
        in_specs=[SMEM]
        + [pl.BlockSpec(one.shape, lambda step: (0, 0)) for one in grads]
        + [part(one) for one in arrays]
        + whole
        + [pl.BlockSpec(memory_space=pl.ANY)] * len(before),
        out_specs=[part(one) for one in arrays] + whole,
        input_output_aliases={len(inputs) + place: place for place in range(len(before))},
        scratch_shapes=[
            pltpu.VMEM(grads[0].shape, BF16),
            pltpu.VMEM((matrices, height, height), F32),
            pltpu.VMEM((matrices, height, 2 * height), BF16),
            pltpu.VMEM((matrices, height, 2 * height), BF16),
            pltpu.VMEM((count, side, height), F32),
        ],
        compiler_params=limit(24),
        cost_estimate=pl.CostEstimate(
            flops=matrices * NEWTON_TURNS * 8 * height**3, bytes_accessed=16 * MIB, transcendentals=0
        ),
        name="optimizer",
    )(*inputs, *before)


def own_rows(values, index, chunk):
    early = lax.dynamic_slice_in_dim(values, index * chunk, chunk, 0)
    late = lax.dynamic_slice_in_dim(values, (3 - index) * chunk, chunk, 0)
    return jnp.concatenate([early, late], axis=0)


def in_order(mine, other, index, chunk):
    inner = jnp.where(index == 0, other, mine)
    outer = jnp.where(index == 0, mine, other)
    return jnp.concatenate([outer[:chunk], inner, outer[chunk:]], axis=0)


def token_outputs(own_output, part_input, part_encoder, core, chunk):
    return (
        in_order(own_output, swapped(own_output), core, chunk),
        part_input.astype(F32) + swapped(part_input).astype(F32),
        part_encoder.astype(F32) + swapped(part_encoder).astype(F32),
    )


def key_bounds(key_ids, query_ids, chunk):
    rows = query_ids.reshape(-1, chunk)
    lowest = jnp.sum((key_ids[None] < rows[:, :1]).astype(jnp.int32), axis=1, keepdims=True)
    highest = jnp.sum((key_ids[None] <= rows[:, -1:]).astype(jnp.int32), axis=1, keepdims=True)
    return jnp.concatenate([lowest, highest + (chunk - 1)], axis=1) // chunk


def per_device(
    decoder_input,
    encoder_states,
    decoder_segments,
    encoder_segments,
    output_cotangent,
    block_slots,
    master,
    first_moment,
    second_moment,
    row_statistics,
    column_statistics,
    row_basis,
    column_basis,
    vectors,
    vector_first,
    vector_second,
):
    core = lax.axis_index("tensor")
    cores = lax.axis_size("tensor")
    ring, rings = lax.axis_index("dp"), lax.axis_size("dp")
    owned_count, block_height = master.shape[1], master.shape[2]
    vector_cols = vectors.shape[1]
    length, width = decoder_input.shape[1], decoder_input.shape[2]
    row_count = width // block_height
    block_total = block_slots.shape[0]
    column_count = block_total // row_count
    chunk = length // 4
    per_ring = owned_count * HD + VECTOR_ROWS
    group = block_height // vector_cols

    payload = low(master[0]).transpose(0, 2, 1).reshape(owned_count * HD, block_height)
    lane = jnp.arange(block_height) // vector_cols
    here = lane == ring % group
    small = jnp.where(here[None], jnp.tile(low(vectors), (1, group)), jnp.zeros((), BF16))
    small = jnp.pad(small, ((0, VECTOR_ROWS - vectors.shape[0]), (0, 0)))
    tokens, encoder_rows = decoder_input[0], encoder_states[0]
    ids, encoder_ids = decoder_segments[0], encoder_segments[0]
    own_tokens = own_rows(tokens, core, chunk)
    own_ids = own_rows(ids, core, chunk)
    own_cotangent = own_rows(output_cotangent[0], core, chunk)
    places = jnp.arange(length, dtype=jnp.int32)
    own_places = own_rows(places, core, chunk)
    self_allowed = (ids[:, None] == own_ids[None, :]) & (places[:, None] <= own_places[None, :])
    self_bias = jnp.where(self_allowed, 0.0, NEGATIVE).astype(F32)
    cross_bias = jnp.where(encoder_ids[:, None] == own_ids[None, :], 0.0, NEGATIVE).astype(F32)
    here_and_core = jnp.full((1,), core, jnp.int32)
    ends = jnp.stack([here_and_core + 1, 4 - here_and_core])
    self_edges = jnp.concatenate([key_bounds(ids, own_ids, chunk)[:, :1], ends], axis=1)
    self_scalars = jnp.concatenate([self_edges.reshape(-1), here_and_core])
    cross_edges = key_bounds(encoder_ids, own_ids, chunk)
    cross_scalars = jnp.concatenate([cross_edges.reshape(-1), here_and_core])

    payload = jnp.concatenate([payload, small], axis=0)
    owner, local = block_slots // owned_count, block_slots % owned_count
    chips = jnp.arange(rings, dtype=jnp.int32)
    grid_of_chips = rings == DEPTH * SIDE * SIDE
    if grid_of_chips:
        starts = apart(ring, owner, 1) * per_ring + local * HD
        slices = [(index ^ core) * rings * per_ring for index in range(cores)]
        ends = (apart(ring, chips, 1) + 1) * per_ring - VECTOR_ROWS
        early_count = owned_count // 2
        sizes = (early_count * HD, per_ring - early_count * HD)
        order = jnp.array(PLACES, jnp.int32)
        late = local // early_count
        sum_rows = local % early_count * HD + jnp.where(
            late == 1,
            rings * sizes[0] + order[apart(ring, owner, -1)] * sizes[1],
            order[apart(ring, owner, -1)] * sizes[0],
        )
        sum_ends = rings * sizes[0] + (order[apart(ring, chips, -1)] + 1) * sizes[1] - VECTOR_ROWS
    else:
        starts = owner * cores * per_ring + local * HD
        slices = [index * per_ring for index in range(cores)]
        ends = (chips * cores + 1) * per_ring - VECTOR_ROWS
        sum_rows = owner * per_ring + local * HD
        sum_ends = (chips + 1) * per_ring - VECTOR_ROWS
    starts = jnp.concatenate([starts + start for start in slices])
    beside = (starts, ends, own_tokens, own_cotangent, self_bias, cross_bias)
    beside += (self_scalars, cross_scalars, sum_rows, sum_ends)
    if grid_of_chips:
        pieces, beside = gather_chips(payload, beside)
        pieces += [swapped(piece) for piece in pieces]
    else:
        pieces = [lax.all_gather(payload, ("dp", "tensor"), axis=0, tiled=True)]
    starts, ends, own_tokens, own_cotangent, self_bias, cross_bias, *scalars = beside
    self_scalars, cross_scalars, sum_rows, sum_ends = scalars
    layer = call_layer(
        (self_scalars, cross_scalars, starts, ends),
        pieces,
        (tokens, own_tokens, self_bias, encoder_rows, cross_bias, own_cotangent),
        cores,
        group,
    )
    own_output, ff_mine, cross_mine, sent, part_encoder, grad_one, norms = layer[:7]
    w_self, q_self, k_self, lse_self, ctxt_self = layer[7:]
    self_mine, self_sent, part_input = call_self_backward(
        self_scalars,
        (grad_one, ctxt_self, w_self, q_self, tokens, own_tokens, k_self, lse_self, self_bias),
    )

    terms = (ff_mine, cross_mine, swapped(sent), self_mine, swapped(self_sent), norms)
    shift = ((block_height - ring % group * vector_cols) % block_height)[None]
    arrays = [one[0].transpose(0, 2, 1) for one in (master, first_moment, second_moment)]
    arrays += [
        one[0] for one in (row_statistics, column_statistics, row_basis, column_basis)
    ]
    vector_states = [vectors, vector_first, vector_second]
    if grid_of_chips:
        cuts = [size * places for size in sizes for places in (4, 4, 2, 2, 4)]
        parts = scatter(sum_rows, sum_ends, terms, cuts, cores, block_height, group)
        own_output, part_encoder, part_input, parts = lax.optimization_barrier(
            (own_output, part_encoder, part_input, parts)
        )
        tokens_out = token_outputs(own_output, part_input, part_encoder, core, chunk)
        column, tokens_out = reduce_plane(*parts[:5], tokens_out)
        block_output, input_gradient, encoder_gradient = tokens_out
        column, parts = lax.optimization_barrier((column, parts[5:]))
        column, early = reduce_plane(*parts, reduce_column(column))
        updated = optimize(shift, early, arrays, 0, early_count, [], [])
        updated = optimize(
            shift, reduce_column(column), arrays, 1, early_count, vector_states, updated
        )
    else:
        (whole,) = scatter(
            sum_rows,
            sum_ends,
            terms,
            [rings * per_ring],
            cores,
            block_height,
            group,
        )
        summed = lax.psum_scatter(whole, "dp", scatter_dimension=0, tiled=True)
        updated = optimize(shift, [summed], arrays, 0, owned_count, vector_states, [])
        tokens_out = token_outputs(own_output, part_input, part_encoder, core, chunk)
        block_output, input_gradient, encoder_gradient = tokens_out

    return (
        block_output[None],
        input_gradient[None],
        encoder_gradient[None],
        *[one.transpose(0, 2, 1)[None] for one in updated[:3]],
        *[one[None] for one in updated[3:7]],
        *updated[7:],
    )


def solution(mesh):
    blocks = P("tensor", "dp", None, None)
    rows = P("dp", None, None)
    return jax.shard_map(
        per_device,
        mesh=mesh,
        in_specs=(rows, rows, P("dp", None), P("dp", None), rows, P())
        + (blocks,) * 7
        + (P(None, "dp"),) * 3,
        out_specs=(rows,) * 3 + (blocks,) * 7 + (P(None, "dp"),) * 3,
        check_vma=False,
    )
```
